32 devices in a mesh: dp: 8 (over z, y), expert: 2 (over core), col: 2 (over x).
Axes of the slice: x: 2, y: 2, z: 4, core: 2. Of those that a mesh axis runs over, the one named last changes fastest.
Arguments:
- tokens: bfloat16 [8192, 1536], P(('dp', 'expert'), 'col'), may hold values from -6 to 6
- gain_attn: float32 [1536], P('col'), may hold values from 0.5 to 1.5
- w_query: bfloat16 [1536, 1536], P('col', 'expert'), may hold values from -0.625 to 0.625
- key_matrix: bfloat16 [1536, 512], P('col', 'expert'), may hold values from -0.625 to 0.625
- value_matrix: bfloat16 [1536, 512], P('col', 'expert'), may hold values from -0.15625 to 0.15625
- w_out: bfloat16 [1536, 1536], P('expert', 'col'), may hold values from -2.5 to 2.5
- gain_moe: float32 [1536], P('col'), may hold values from 0.5 to 1.5
- w_router: bfloat16 [1536, 40], P('col'), may hold values from -0.078125 to 0.078125
- w_gate: bfloat16 [40, 1536, 512], P('expert', 'col'), may hold values from -0.15625 to 0.15625
- w_up: bfloat16 [40, 1536, 512], P('expert', 'col'), may hold values from -0.15625 to 0.15625
- w_down: bfloat16 [40, 512, 1536], P('expert', None, 'col'), may hold values from -4 to 4
- segments: int32 [16, 512], P('dp'), may hold values from 0 to 3, never falling along the last dimension, each value on 1 to 256 neighbouring positions
- routes: int32 [8192, 8], P(('dp', 'expert')), may hold values from 0 to 39, all different within a row; in each aligned block of 512 rows (0 to 511, 512 to 1023, ...) at most 192 rows name the same one
- cotangent: bfloat16 [8192, 1536], P(('dp', 'expert'), 'col'), may hold values from -6 to 6
Outputs:
- output: float32 [8192, 1536], P(('dp', 'expert'), 'col')
- grad_tokens: float32 [8192, 1536], P(('dp', 'expert'), 'col')
- grad_gain_attn: float32 [1536], P('col')
- grad_query: float32 [1536, 1536], P('col', 'expert')
- grad_key: float32 [1536, 512], P('col', 'expert')
- grad_value: float32 [1536, 512], P('col', 'expert')
- grad_out: float32 [1536, 1536], P('expert', 'col')
- grad_gain_moe: float32 [1536], P('col')
- grad_router: float32 [1536, 40], P('col')
- grad_gate: float32 [40, 1536, 512], P('expert', 'col', 'dp')
- grad_up: float32 [40, 1536, 512], P('expert', 'col', 'dp')
- grad_down: float32 [40, 512, 1536], P('expert', 'dp', 'col')
The draws below stay inside these ranges and needn't reach their ends.
Inputs may be any that keep to these rules, and one draw needn't show every extreme that they name: `routes`: in each aligned block of 512 rows (one sequence) no expert is named by more than 192 rows, and one expert is named by exactly 192 rows in some blocks. `segments`: never falls along a sequence; a document has 1 to 256 tokens, one of them exactly that many.
All inputs are finite; a program needn't handle non-finite values.
Results may differ from the reference program's by a relative error of at most 0.017.
Values may be sent and summed in bfloat16 or wider, within the bound.
A program may use at most 384 MiB of HBM per device.

```python
import math
import jax
import jax.numpy as jnp
import numpy as np
from jax import lax

MODEL_WIDTH = 1536
QUERY_HEADS = 24
KEY_VALUE_HEADS = 8
HEAD_WIDTH = 64
EXPERTS = 40
FFE = 512
TOPK = 8
TOK_DEV = 512
DOCS = 4
CAP = 192
SEQS = 16
TOKENS = 8192


def block_scale(own_key, shape, cuts, least, high):
    level = 1.0
    for position, shards_of in cuts:
        draws = jax.random.uniform(jax.random.fold_in(jax.random.fold_in(own_key, 6), position), (shards_of,), jnp.float32, least / len(cuts), high / len(cuts))
        level = level * jnp.repeat(jnp.exp(draws), shape[position] // shards_of).reshape((-1,) + (1,) * (len(shape) - 1 - position))
    return level


def length_profile(count, total, most, slope):
    portions = [(1 << 20) // math.isqrt(standing ** slope) + 1 for standing in range(2, count + 1)]
    spare, counts = total - most - (count - 1), [1] * (count - 1)
    while spare > 0:
        free = [i for i in range(count - 1) if counts[i] < most]
        mass, left = sum([portions[i] for i in free]), spare
        for i in free:
            more = min(most - counts[i], max(1, left * portions[i] // mass), spare)
            counts[i] = counts[i] + more
            spare = spare - more
    return np.array([most] + counts)


def ragged(own_key, amount, total, bound, slope):
    if amount == 2:
        one = jax.random.randint(own_key, (), max(1, total - bound), min(bound, total - 1) + 1)
        return jnp.stack([one, total - one])
    lengths = jnp.asarray(length_profile(amount, total, bound, slope), jnp.int32)
    pairs = (amount - 1) // 2
    giver, receiver = lengths[1:1 + 2 * pairs:2], lengths[2:2 + 2 * pairs:2]
    margin = jnp.minimum(giver - 1, bound - receiver)
    moved = jax.random.randint(jax.random.fold_in(own_key, 1), (pairs,), 0, 1 << 20) % (margin + 1)
    lengths = lengths.at[1:1 + 2 * pairs:2].set(giver - moved).at[2:2 + 2 * pairs:2].set(receiver + moved)
    return lengths[jax.random.permutation(jax.random.fold_in(own_key, 2), amount)]


def assign_block(key, own, number, rows, count, top, reach, slope):
    sequence = jax.random.permutation(key, count)
    heavy_load, ordinary = portions_of(count, rows * top, reach, slope, True), portions_of(count, rows * top, reach, slope, False)
    places = jnp.arange(count)

    def named(tallies, turn):
        used = int((tallies > 0).sum())
        fixed = max(1, used // 4)
        moved = fixed + (places - fixed + turn * (used - fixed)) % max(1, count - fixed)
        return jnp.zeros((count,), jnp.int32).at[sequence[jnp.where(places < fixed, places, moved)]].set(jnp.asarray(tallies, jnp.int32))

    tallies = jnp.where(number % 4 == 0, named(heavy_load, number // 4), named(ordinary, number - number // 4 - 1))
    mixed = jax.random.permutation(jax.random.fold_in(own, 3), count)
    source_of, receiver = mixed[0:count // 2 * 2:2], mixed[1:count // 2 * 2:2]
    room = jnp.minimum(tallies[source_of] - 1, reach - tallies[receiver]) // 2
    room = jnp.where((source_of == sequence[0]) | (receiver == sequence[0]) | (tallies[receiver] == 0), 0, jnp.maximum(room, 0))
    moved = jax.random.randint(jax.random.fold_in(own, 4), (count // 2,), 0, 1 << 20) % (room + 1)
    tallies = tallies.at[source_of].add(-moved).at[receiver].add(moved)
    members = jnp.searchsorted(jnp.cumsum(tallies), jnp.arange(rows * top), side="right").astype(jnp.int32)
    table = members.reshape(top, rows).T
    table = table[jax.random.permutation(jax.random.fold_in(own, 1), rows)]
    turn = jax.random.randint(jax.random.fold_in(own, 2), (rows, 1), 0, top)
    return jnp.take_along_axis(table, (jnp.arange(top)[None, :] + turn) % top, axis=1)


def portions_of(count, total, bound, skew, full):
    weights = [(1 << 20) // math.isqrt(rank ** skew) + 1 for rank in range(1, count + 1)]
    largest = bound if full else min(bound, max(-(-total // count), total * weights[0] // sum(weights)))
    least = 1 if total - largest >= count - 1 else 0
    counts, surplus = [largest] + [least] * (count - 1), total - largest - least * (count - 1)
    while surplus > 0:
        free = [i for i in range(1, count) if counts[i] < largest] or [i for i in range(1, count) if counts[i] < bound]
        whole, left = sum([weights[i] for i in free]), surplus
        for i in free:
            addition = min(bound - counts[i], max(1, left * weights[i] // whole), surplus)
            counts[i] = counts[i] + addition
            surplus = surplus - addition
    return np.array(counts)


def centred(key, dims, width, bound, shards=(), kind=jnp.bfloat16):
    result = jax.random.normal(key, dims, jnp.float32) * width
    if len(shards) > 0:
        result = block_scale(key, dims, shards, -0.22, 0.18) * result
    return jnp.clip(result, min=-bound, max=bound).astype(kind)


def setup_inputs(seed: int = 0) -> dict:
    arg_keys = jax.random.split(jax.random.key(seed), 15)
    tokens = centred(arg_keys[0], (TOKENS, MODEL_WIDTH), 1.0, 6.0, ((0, 16), (1, 2)))
    gain_attn = jnp.clip(1.0 + 0.1 * jax.random.normal(arg_keys[1], (MODEL_WIDTH,), jnp.float32), 0.5, 1.5)
    w_query = centred(arg_keys[2], (MODEL_WIDTH, QUERY_HEADS * HEAD_WIDTH), (MODEL_WIDTH // 16) ** -0.5, 0.625, ((0, 2), (1, 2)))
    key_matrix = centred(arg_keys[3], (MODEL_WIDTH, KEY_VALUE_HEADS * HEAD_WIDTH), (MODEL_WIDTH // 16) ** -0.5, 0.625, ((0, 2), (1, 2)))
    value_matrix = centred(arg_keys[4], (MODEL_WIDTH, KEY_VALUE_HEADS * HEAD_WIDTH), MODEL_WIDTH ** -0.5, 0.15625, ((0, 2), (1, 2)))
    w_out = centred(arg_keys[5], (QUERY_HEADS * HEAD_WIDTH, MODEL_WIDTH), (QUERY_HEADS * HEAD_WIDTH // 256) ** -0.5, 2.5, ((0, 2), (1, 2)))
    gain_moe = jnp.clip(1.0 + 0.1 * jax.random.normal(arg_keys[6], (MODEL_WIDTH,), jnp.float32), 0.5, 1.5)
    w_router = centred(arg_keys[7], (MODEL_WIDTH, EXPERTS), (4 * MODEL_WIDTH) ** -0.5, 0.078125, ((0, 2),))
    w_gate = centred(arg_keys[8], (EXPERTS, MODEL_WIDTH, FFE), MODEL_WIDTH ** -0.5, 0.15625, ((0, 2), (1, 2)))
    w_up = centred(arg_keys[9], (EXPERTS, MODEL_WIDTH, FFE), MODEL_WIDTH ** -0.5, 0.15625, ((0, 2), (1, 2)))
    w_down = centred(arg_keys[10], (EXPERTS, FFE, MODEL_WIDTH), 2 ** -0.5, 4.0, ((0, 2), (2, 2)))
    segments = jax.vmap(lambda own: jnp.searchsorted(jnp.cumsum(ragged(own, DOCS, TOK_DEV, TOK_DEV // 2, 1)), jnp.arange(TOK_DEV), side="right"))(jax.random.split(arg_keys[11], SEQS)).reshape((SEQS, TOK_DEV)).astype(jnp.int32)
    routes_keys = jax.random.split(jax.random.fold_in(arg_keys[12], 1), TOKENS // TOK_DEV)
    routes_turns = jax.random.permutation(jax.random.fold_in(arg_keys[12], 3), TOKENS // TOK_DEV)
    routes = jax.vmap(lambda own, number: assign_block(jax.random.fold_in(arg_keys[12], 2), own, number, TOK_DEV, EXPERTS, TOPK, CAP, 1))(routes_keys, routes_turns).reshape((TOKENS, TOPK))
    cotangent = centred(arg_keys[13], (TOKENS, MODEL_WIDTH), 1.0, 6.0, ((0, 16), (1, 2)))
    return dict(tokens=tokens, gain_attn=gain_attn, w_query=w_query, key_matrix=key_matrix, value_matrix=value_matrix, w_out=w_out, gain_moe=gain_moe, w_router=w_router, w_gate=w_gate, w_up=w_up, w_down=w_down, segments=segments, routes=routes, cotangent=cotangent)


EPS = 1e-06
RESIDUAL = 0.22
SCORE_SCALE = 0.015625
THETA = 10000.0
NEG = -1000000000.0
HIGHEST = lax.Precision.HIGHEST

@jax.custom_vjp
def lower_half(v):
    return lax.optimization_barrier(v.astype(jnp.bfloat16)).astype(jnp.float32)

@jax.custom_vjp
def lower_half_backward(v):
    return v

def low_keep(v):
    return (lower_half(v), None)

def low_pass(kept, grad):
    return (grad,)

def back_keep(v):
    return (v, None)

def back_low(kept, grad):
    return (lower_half(grad),)
lower_half.defvjp(low_keep, low_pass)
lower_half_backward.defvjp(back_keep, back_low)

def highest_product(left, right):
    return jnp.dot(left, right, precision=HIGHEST, preferred_element_type=jnp.float32)

def doc_positions(seg_row):
    length_total = seg_row.shape[0]
    index = jnp.arange(length_total, dtype=jnp.int32)
    before = jnp.concatenate([jnp.full((1,), -1, jnp.int32), seg_row[:-1].astype(jnp.int32)])
    starts = jnp.where(seg_row != before, index, 0)
    return index - lax.cummax(starts, axis=0)

def rope_tables(positions, head_size):
    half = head_size // 2
    freq = jnp.exp(jnp.arange(half, dtype=jnp.float32) * (-2.0 * math.log(THETA) / head_size))
    angle = positions.astype(jnp.float32)[:, None] * freq[None, :]
    return (jnp.cos(angle)[:, None, :], jnp.sin(angle)[:, None, :])

def apply_rotation(heads, cosine_table, sine_table):
    half = heads.shape[-1] // 2
    first = heads[..., :half]
    second = heads[..., half:]
    return jnp.concatenate([first * cosine_table - second * sine_table, second * cosine_table + first * sine_table], -1)

def rms_norm(value_rows, gain):
    return value_rows * lax.rsqrt(lax.optimization_barrier(jnp.mean(value_rows * value_rows, -1, keepdims=True)) + EPS) * gain

def slot_targets(route_rows, capacity, count):
    flat = route_rows.reshape(-1).astype(jnp.int32)
    onehot = (flat[:, None] == jnp.arange(count, dtype=jnp.int32)[None, :]).astype(jnp.int32)
    before = jnp.cumsum(onehot, 0) - onehot
    slot = lax.optimization_barrier(jnp.sum(before * onehot, 1))
    return flat * capacity + slot

def block_forward(params, inputs, seg_row, route_rows):
    gain_attn, w_query, key_matrix, value_matrix, w_out, gain_moe, w_router, w_gate, w_up, w_down = params
    length_total = inputs.shape[0]
    normalized_input = lower_half(rms_norm(inputs, gain_attn))
    query_rows = lower_half_backward(highest_product(normalized_input, w_query)).reshape(length_total, QUERY_HEADS, HEAD_WIDTH)
    key_rows = lower_half_backward(highest_product(normalized_input, key_matrix)).reshape(length_total, KEY_VALUE_HEADS, HEAD_WIDTH)
    value_rows = lower_half(lower_half_backward(highest_product(normalized_input, value_matrix))).reshape(length_total, KEY_VALUE_HEADS, HEAD_WIDTH)
    cosine_table, sine_table = rope_tables(doc_positions(seg_row), HEAD_WIDTH)
    query_rows = lower_half(apply_rotation(query_rows, cosine_table, sine_table)).reshape(length_total, KEY_VALUE_HEADS, QUERY_HEADS // KEY_VALUE_HEADS, HEAD_WIDTH)
    key_rows = lower_half(apply_rotation(key_rows, cosine_table, sine_table))
    scores = lower_half_backward(jnp.einsum('qkgd,skd->kgqs', query_rows, key_rows, precision=HIGHEST) * SCORE_SCALE)
    index = jnp.arange(length_total)
    allowed = (seg_row[:, None] == seg_row[None, :]) & (index[None, :] <= index[:, None])
    scores = jnp.where(allowed, scores, NEG)
    probs = lower_half(jax.nn.softmax(scores, axis=-1))
    mixed = jnp.einsum('kgqs,skd->qkgd', probs, value_rows, precision=HIGHEST).reshape(length_total, QUERY_HEADS * HEAD_WIDTH)
    mixed = lower_half_backward(lower_half(mixed))
    attn = lower_half_backward(highest_product(mixed, w_out))
    middle = inputs + RESIDUAL * attn
    normed_moe = lower_half(rms_norm(middle, gain_moe))
    logits = highest_product(normed_moe, w_router)
    gates = jax.nn.softmax(jnp.take_along_axis(logits, route_rows, 1), axis=-1)
    targets = slot_targets(route_rows, CAP, EXPERTS)
    buffer = jnp.zeros((EXPERTS * CAP, MODEL_WIDTH), jnp.float32).at[targets].set(jnp.repeat(normed_moe, TOPK, 0))
    buffer = lower_half_backward(buffer.reshape(EXPERTS, CAP, MODEL_WIDTH))
    gate_val = lower_half_backward(jnp.einsum('ecd,edf->ecf', buffer, w_gate, precision=HIGHEST))
    up_val = lower_half_backward(jnp.einsum('ecd,edf->ecf', buffer, w_up, precision=HIGHEST))
    hidden = lower_half(jax.nn.silu(gate_val) * up_val)
    expert_out = lower_half_backward(lower_half(jnp.einsum('ecf,efd->ecd', hidden, w_down, precision=HIGHEST)))
    returned = expert_out.reshape(EXPERTS * CAP, MODEL_WIDTH)[targets].reshape(length_total, TOPK, MODEL_WIDTH)
    moe = jnp.einsum('tk,tkd->td', gates, returned, precision=HIGHEST)
    return middle + RESIDUAL * moe

def reference(tokens, gain_attn, w_query, key_matrix, value_matrix, w_out, gain_moe, w_router, w_gate, w_up, w_down, segments, routes, cotangent):
    params = tuple((item.astype(jnp.float32) for item in (gain_attn, w_query, key_matrix, value_matrix, w_out, gain_moe, w_router, w_gate, w_up, w_down)))
    inputs = tokens.astype(jnp.float32).reshape(SEQS, TOK_DEV, MODEL_WIDTH)
    route_blocks = routes.reshape(SEQS, TOK_DEV, TOPK)
    stepper = jax.checkpoint(block_forward)

    def forward(weights, inputs_all):

        def scan_body(carry, blocks):
            return (carry, stepper(weights, blocks[0], blocks[1], blocks[2]))
        return lax.scan(scan_body, None, (inputs_all, segments, route_blocks))[1]
    outputs, pullback = jax.vjp(forward, params, inputs)
    grads, grad_in = pullback(cotangent.astype(jnp.float32).reshape(SEQS, TOK_DEV, MODEL_WIDTH))
    return (outputs.reshape(TOKENS, MODEL_WIDTH), grad_in.reshape(TOKENS, MODEL_WIDTH), grads[0], grads[1], grads[2], grads[3], grads[4], grads[5], grads[6], grads[7], grads[8], grads[9])
```

```python
import math

import jax
import jax.numpy as jnp
from jax import lax
from jax.experimental import pallas as pl
from jax.experimental.pallas import tpu as pltpu
from jax.sharding import PartitionSpec as P

HEAD_WIDTH = 64
ZPARTS = 4
LANES = 128
TILE = 512

EPS = 1e-06
RESIDUAL = 0.22
SCORE_SCALE = 0.015625
THETA = 10000.0
NEG = -1000000000.0


def doc_positions(seg_row):
    length_total = seg_row.shape[0]
    index = jnp.arange(length_total, dtype=jnp.int32)
    before = jnp.concatenate([jnp.full((1,), -1, jnp.int32), seg_row[:-1]])
    starts = jnp.where(seg_row != before, index, 0)
    return index - lax.cummax(starts, axis=0)


def rope_tables(positions, head_size):
    half = head_size // 2
    freq = jnp.exp(jnp.arange(half, dtype=jnp.float32) * (-2.0 * math.log(THETA) / head_size))
    angle = positions.astype(jnp.float32)[:, None] * freq[None, :]
    return (jnp.cos(angle)[:, None, :], jnp.sin(angle)[:, None, :])


def apply_rotation(heads, cosine_table, sine_table):
    half = heads.shape[-1] // 2
    first = heads[..., :half]
    second = heads[..., half:]
    return jnp.concatenate(
        [first * cosine_table - second * sine_table, second * cosine_table + first * sine_table], -1
    )


def unrotate(grads, cosine_table, sine_table):
    half = grads.shape[-1] // 2
    first = grads[..., :half]
    second = grads[..., half:]
    return jnp.concatenate(
        [first * cosine_table + second * sine_table, second * cosine_table - first * sine_table], -1
    )


def allowed_mask(seg_rows):
    index = jnp.arange(seg_rows.shape[1])
    same = seg_rows[:, :, None] == seg_rows[:, None, :]
    return same & (index[None, None, :] <= index[None, :, None])


def block_scores(query_rows, key_rows, allowed):
    scores = (
        jnp.einsum("bqkgd,bskd->bkgqs", query_rows, key_rows, preferred_element_type=jnp.float32)
        * SCORE_SCALE
    )
    return jnp.where(allowed[:, None, None], scores, NEG)


def attend_forward(query_rows, key_rows, value_rows, allowed):
    scores = block_scores(query_rows, key_rows, allowed)
    peak = jnp.max(scores, -1, keepdims=True)
    expo = jnp.exp(scores - peak)
    total = jnp.sum(expo, -1, keepdims=True)
    probs = (expo / total).astype(jnp.bfloat16)
    outputs = jnp.einsum("bkgqs,bskd->bqkgd", probs, value_rows, preferred_element_type=jnp.float32)
    totals = peak + jnp.log(total)
    return (outputs, totals)


def attend_backward(query_rows, key_rows, value_rows, allowed, totals, grad_mixed):
    scores = block_scores(query_rows, key_rows, allowed)
    probs = jnp.exp(scores - totals)
    slope = jnp.einsum(
        "bqkgd,bskd->bkgqs", grad_mixed, value_rows, preferred_element_type=jnp.float32
    )
    delta = jnp.sum(probs * slope, -1, keepdims=True)
    dscore = (probs * (slope - delta)).astype(jnp.bfloat16)
    grad_queries = (
        jnp.einsum("bkgqs,bskd->bqkgd", dscore, key_rows, preferred_element_type=jnp.float32)
        * SCORE_SCALE
    )
    grad_keys = (
        jnp.einsum("bkgqs,bqkgd->bskd", dscore, query_rows, preferred_element_type=jnp.float32)
        * SCORE_SCALE
    )
    grad_values = jnp.einsum(
        "bkgqs,bqkgd->bskd",
        probs.astype(jnp.bfloat16),
        grad_mixed,
        preferred_element_type=jnp.float32,
    )
    return (grad_queries, grad_keys, grad_values)


def flip(value, axis, mask=1):
    size = lax.axis_size(axis)
    return lax.ppermute(value, axis, [(i, i ^ mask) for i in range(size)])


def across(value):
    return flip(value, "col")


def sibling(value):
    return flip(value, "expert")


def dot_nn(a, b):
    return jnp.dot(a, b, preferred_element_type=jnp.float32)


def dot_nt(a, b):
    return lax.dot_general(a, b, (((1,), (1,)), ((), ())), preferred_element_type=jnp.float32)


def dot_tn(a, b):
    return lax.dot_general(a, b, (((0,), (0,)), ((), ())), preferred_element_type=jnp.float32)


def moe_kernel(
    base_ref,
    routes_ref,
    h_own,
    h_far,
    c_own,
    c_far,
    pair_own,
    pair_far,
    down_own,
    down_far,
    router_own,
    router_far,
    moe_own,
    moe_far,
    back_own,
    back_far,
    hidden_ref,
    slopes_ref,
    dlog_ref,
):
    experts = down_own.shape[0] // LANES
    rows = h_own.shape[0]
    lane = lax.broadcasted_iota(jnp.int32, (rows, LANES), 1)
    chosen = lane == routes_ref[:, 0:1]
    for k in range(1, routes_ref.shape[1]):
        chosen = chosen | (lane == routes_ref[:, k : k + 1])
    logits = dot_nn(h_own[...], router_own[...]) + dot_nn(h_far[...], router_far[...])
    peak = jnp.max(jnp.where(chosen, logits, -jnp.inf), axis=1, keepdims=True)
    expo = jnp.where(chosen, jnp.exp(logits - peak), 0.0)
    gates = expo / jnp.sum(expo, axis=1, keepdims=True)
    grad_gates = jnp.zeros((rows, LANES), jnp.float32)
    for e in range(experts):
        here = lane == base_ref[0] + e
        gate = jnp.sum(jnp.where(here, gates, 0.0), axis=1, keepdims=True)
        pair_rows = pl.ds(2 * LANES * e, 2 * LANES)
        down_rows = pl.ds(LANES * e, LANES)
        pair = dot_nt(h_own[...], pair_own[pair_rows, :]) + dot_nt(
            h_far[...], pair_far[pair_rows, :]
        )
        slope = dot_nt(c_own[...], down_own[down_rows, :]) + dot_nt(
            c_far[...], down_far[down_rows, :]
        )
        slope = RESIDUAL * slope
        gate_val = pair[:, :LANES]
        up_val = pair[:, LANES:]
        sigma = jax.nn.sigmoid(gate_val)
        silu = gate_val * sigma
        hidden = silu * up_val
        dgate = jnp.sum(hidden * slope, axis=1, keepdims=True)
        grad_gates = jnp.where(here, dgate, grad_gates)
        dz = gate * slope
        hidden_ref[:, LANES * e : LANES * (e + 1)] = (gate * hidden).astype(jnp.bfloat16)
        slopes_ref[:, 2 * LANES * e : 2 * LANES * e + LANES] = (
            dz * up_val * (sigma + silu * (1.0 - sigma))
        ).astype(jnp.bfloat16)
        slopes_ref[:, 2 * LANES * e + LANES : 2 * LANES * (e + 1)] = (dz * silu).astype(
            jnp.bfloat16
        )
    dlog = gates * (grad_gates - jnp.sum(gates * grad_gates, axis=1, keepdims=True))
    dlog_high = dlog.astype(jnp.bfloat16)
    dlog_low = (dlog - dlog_high.astype(jnp.float32)).astype(jnp.bfloat16)
    dlog_ref[:, :LANES] = dlog_high
    dlog_ref[:, LANES:] = dlog_low
    moe_own[...] = dot_nn(hidden_ref[...], down_own[...]).astype(jnp.bfloat16)
    moe_far[...] = dot_nn(hidden_ref[...], down_far[...]).astype(jnp.bfloat16)
    for out, pair, router in ((back_own, pair_own, router_own), (back_far, pair_far, router_far)):
        total = dot_nt(dlog_high, router[...]) + dot_nt(dlog_low, router[...])
        out[...] = (total + dot_nn(slopes_ref[...], pair[...])).astype(jnp.bfloat16)


def moe_chunk(base, routes, h_own, h_far, c_own, c_far, weights):
    rows, part = h_own.shape
    experts = weights[2].shape[0] // LANES
    by_row = lambda width: pl.BlockSpec((TILE, width), lambda i, *_: (i, 0))
    whole = lambda a: pl.BlockSpec(
        a.shape, lambda i, *_: (0,) * a.ndim, pipeline_mode=pl.Buffered(1)
    )
    outs = [part, part, part, part, experts * LANES, 2 * experts * LANES, 2 * LANES]
    flops = 2 * rows * 2 * part * experts * LANES * 6
    return pl.pallas_call(
        moe_kernel,
        out_shape=[jax.ShapeDtypeStruct((rows, w), jnp.bfloat16) for w in outs],
        grid_spec=pltpu.PrefetchScalarGridSpec(
            num_scalar_prefetch=1,
            grid=(rows // TILE,),
            in_specs=[by_row(routes.shape[1])]
            + [by_row(part)] * 4
            + [whole(w) for w in weights],
            out_specs=[by_row(w) for w in outs],
        ),
        compiler_params=pltpu.CompilerParams(vmem_limit_bytes=56 * 1024 * 1024),
        cost_estimate=pl.CostEstimate(
            flops=flops, bytes_accessed=40_000_000, transcendentals=rows * experts * LANES
        ),
        name="moe_rows",
    )(base, routes, h_own, h_far, c_own, c_far, *weights)


def weight_kernel(side_ref, *refs):
    chunks = (len(refs) - 4) // 6
    hidden = refs[:chunks]
    slopes = refs[chunks : 2 * chunks]
    h_own, h_far, c_own, c_far = (
        refs[(2 + i) * chunks : (3 + i) * chunks] for i in range(4)
    )
    outs = refs[6 * chunks :]
    half = LANES // 2
    first = side_ref[0] == 0
    for keep, send, rows_h, rows_c in (
        (outs[0], outs[2], h_own, c_own),
        (outs[1], outs[3], h_far, c_far),
    ):
        pair = sum(dot_tn(s[...], h[...]) for s, h in zip(slopes, rows_h))
        down = sum(dot_tn(s[...], c[...]) for s, c in zip(hidden, rows_c)) * RESIDUAL
        for i, block in enumerate((pair[:LANES], pair[LANES:], down)):
            low, high = block[:half], block[half:]
            keep[0, half * i : half * (i + 1), :] = jnp.where(first, low, high)
            send[0, half * i : half * (i + 1), :] = jnp.where(first, high, low).astype(
                jnp.bfloat16
            )


def weight_grads(side, start, count, hidden, slopes, h_own, h_far, c_own, c_far):
    rows, part = h_own[0].shape
    whole = pl.BlockSpec((rows, part), lambda e, *_: (0, 0), pipeline_mode=pl.Buffered(1))
    out = pl.BlockSpec((1, 3 * LANES // 2, part), lambda e, *_: (e, 0, 0))
    n = len(hidden)
    shape = (count, 3 * LANES // 2, part)
    return pl.pallas_call(
        weight_kernel,
        out_shape=[jax.ShapeDtypeStruct(shape, jnp.float32)] * 2
        + [jax.ShapeDtypeStruct(shape, jnp.bfloat16)] * 2,
        grid_spec=pltpu.PrefetchScalarGridSpec(
            num_scalar_prefetch=1,
            grid=(count,),
            in_specs=[pl.BlockSpec((rows, LANES), lambda e, *_: (0, e + start))] * n
            + [pl.BlockSpec((rows, 2 * LANES), lambda e, *_: (0, e + start))] * n
            + [whole] * (4 * n),
            out_specs=[out] * 4,
        ),
        compiler_params=pltpu.CompilerParams(vmem_limit_bytes=60 * 1024 * 1024),
        cost_estimate=pl.CostEstimate(
            flops=2 * n * rows * 2 * part * count * LANES * 3,
            bytes_accessed=40_000_000,
            transcendentals=0,
        ),
        name="expert_weight_grads",
    )(side, *hidden, *slopes, *h_own, *h_far, *c_own, *c_far)


def gather_tokens(value, step, relay):
    far = across(value)
    chunks = [(value, far), (flip(value, "dp", step), flip(far, "dp", step))]
    for k in range(2, ZPARTS):
        got = flip(value, "dp", k * step)
        chunks.append((got, across(got) if relay else flip(far, "dp", k * step)))
    return [
        tuple(jnp.concatenate([piece, sibling(piece)], 0) for piece in pair) for pair in chunks
    ]


def add_wide(*parts):
    return sum(p.astype(jnp.float32) for p in parts)


def scatter_tokens(chunks, step):
    own, far, later = 0.0, 0.0, []
    for k, (p_own, p_far) in enumerate(chunks):
        rows = p_own.shape[0] // 2
        s_own = add_wide(p_own[:rows], sibling(p_own[rows:]))
        s_far = add_wide(p_far[:rows], sibling(p_far[rows:]))
        if k == 0:
            own, far = s_own, s_far
        elif k == 1:
            own = own + flip(s_own.astype(jnp.bfloat16), "dp", step).astype(jnp.float32)
            far = far + flip(s_far.astype(jnp.bfloat16), "dp", step).astype(jnp.float32)
        else:
            piece = s_own + across(s_far.astype(jnp.bfloat16)).astype(jnp.float32)
            later.append(flip(piece.astype(jnp.bfloat16), "dp", k * step))
    return add_wide(own, across(far.astype(jnp.bfloat16)), *later)


def halve(value, index, mask, axis):
    low, high = jnp.split(value, 2, axis)
    upper = (index & mask) != 0
    send = jnp.where(upper, low, high).astype(jnp.bfloat16)
    return jnp.where(upper, high, low) + flip(send, "dp", mask).astype(jnp.float32)


def sum_over_dp(value, index):
    size = lax.axis_size("dp")
    masks = []
    while 1 << len(masks) < size:
        masks.append(1 << len(masks))
    for mask in masks:
        value = halve(value, index, mask, 0)
    value = value.astype(jnp.bfloat16)
    for mask in masks[::-1]:
        got = flip(value, "dp", mask)
        upper = (index & mask) != 0
        value = jnp.concatenate([jnp.where(upper, got, value), jnp.where(upper, value, got)], 0)
    return value.astype(jnp.float32)


def sum_small(value):
    value = value + sibling(value)
    mask = 1
    while mask < lax.axis_size("dp"):
        value = value + flip(value, "dp", mask)
        mask *= 2
    return value


def on_device(
    tokens,
    gain_attn,
    w_query,
    key_matrix,
    value_matrix,
    w_out,
    gain_moe,
    w_router,
    w_gate,
    w_up,
    w_down,
    segments,
    routes,
    cotangent,
):
    col = lax.axis_index("col")
    core = lax.axis_index("expert")
    group = lax.axis_index("dp")
    step = lax.axis_size("dp") // ZPARTS
    zed, member = group // step, group % step

    local, part, ffn = w_gate.shape
    width = part * lax.axis_size("col")
    mine = local // 2
    units = ffn // ZPARTS
    experts = local * lax.axis_size("expert")

    def cut_pair(which):
        def cut(w):
            piece = lax.dynamic_slice(w, (which * mine, 0, zed * units), (mine, part, units))
            return jnp.swapaxes(piece, 1, 2)

        return jnp.concatenate([cut(w_gate), cut(w_up)], 1)

    def cut_down(which):
        return lax.dynamic_slice(w_down, (which * mine, zed * units, 0), (mine, units, part))

    side = member & 1
    split = mine // 2

    def fetch(cut):
        whole = cut(1 - col)
        half = lax.dynamic_slice_in_dim(whole, side * split, split, 0)
        got = across(half)
        other = flip(got, "dp", 1)
        first = jnp.where(side == 0, got, other)
        second = jnp.where(side == 0, other, got)
        return jnp.concatenate([first, second], 0).reshape(-1, part)

    pair_far = fetch(cut_pair)
    down_far = fetch(cut_down)
    pair_own = cut_pair(col).reshape(-1, part)
    down_own = cut_down(col).reshape(-1, part)
    router_own = jnp.pad(w_router, ((0, 0), (0, LANES - experts)))
    router_far = across(router_own)
    weights = [pair_own, pair_far, down_own, down_far, router_own, router_far]

    route_rows = routes.T
    route_rows = jnp.concatenate([route_rows, sibling(route_rows)], 1)
    route_chunks = [route_rows] + [flip(route_rows, "dp", k * step) for k in range(1, ZPARTS)]
    route_chunks = [r.T for r in route_chunks]
    c_chunks = gather_tokens(cotangent, step, False)

    def both(own):
        return jnp.concatenate([own, sibling(own)], 0)

    length_total = tokens.shape[0]
    rows_own, rows_far = both(tokens), both(across(tokens))
    gain_far = across(gain_attn)
    wide_own, wide_far = rows_own.astype(jnp.float32), rows_far.astype(jnp.float32)
    square = jnp.sum(wide_own * wide_own, 1) + jnp.sum(wide_far * wide_far, 1)
    inv_rows = lax.rsqrt(square / width + EPS)
    normed_own = (wide_own * inv_rows[:, None] * gain_attn).astype(jnp.bfloat16)
    normed_far = (wide_far * inv_rows[:, None] * gain_far).astype(jnp.bfloat16)
    inputs, inv_first = wide_own[:length_total], inv_rows[:length_total]

    q_width = w_query.shape[1] // 2
    kv_width = key_matrix.shape[1] // 2
    qkv_width = q_width + 2 * kv_width
    kv_heads = kv_width // HEAD_WIDTH
    group_size = q_width // kv_width

    def qkv_columns(which):
        def cut(w):
            return lax.dynamic_slice_in_dim(w, which * (w.shape[1] // 2), w.shape[1] // 2, 1)

        return jnp.concatenate([cut(w_query), cut(key_matrix), cut(value_matrix)], 1)

    def out_rows(which):
        return lax.dynamic_slice_in_dim(w_out, which * q_width, q_width, 0)

    qkv_here, qkv_there = qkv_columns(col), qkv_columns(1 - col)
    qkv_far = across(qkv_there)
    out_here, out_there = out_rows(col), out_rows(1 - col)
    out_far = across(out_there)

    qkv = dot_nn(normed_own, qkv_here) + dot_nn(normed_far, qkv_far)
    seg_rows = jnp.where(core == 0, segments, segments[::-1])
    allowed = allowed_mask(seg_rows)
    positions = jax.vmap(doc_positions)(seg_rows).reshape(-1)
    cosine_table, sine_table = rope_tables(positions, HEAD_WIDTH)

    def heads(value, *count):
        return value.reshape(2, length_total, *count, HEAD_WIDTH)

    query_rows = apply_rotation(
        qkv[:, :q_width].reshape(2 * length_total, -1, HEAD_WIDTH), cosine_table, sine_table
    )
    query_rows = heads(query_rows.astype(jnp.bfloat16), kv_heads, group_size)
    key_rows = apply_rotation(
        qkv[:, q_width : q_width + kv_width].reshape(2 * length_total, -1, HEAD_WIDTH),
        cosine_table,
        sine_table,
    )
    key_rows = heads(key_rows.astype(jnp.bfloat16), kv_heads)
    value_rows = heads(qkv[:, q_width + kv_width :].astype(jnp.bfloat16), kv_heads)
    mixed, totals = attend_forward(query_rows, key_rows, value_rows, allowed)
    mixed = mixed.reshape(2 * length_total, q_width).astype(jnp.bfloat16)
    mixed_far = across(mixed)
    attn = dot_nn(mixed, out_here) + dot_nn(mixed_far, out_there)
    attn = attn[:length_total] + sibling(attn[length_total:])
    middle = inputs + RESIDUAL * attn
    square = jnp.sum(middle * middle, 1)
    inv_second = lax.rsqrt((square + across(square)) / width + EPS)
    normed_moe = (middle * inv_second[:, None] * gain_moe).astype(jnp.bfloat16)

    h_chunks = gather_tokens(normed_moe, step, True)
    base = (core * local + col * mine).astype(jnp.int32).reshape(1)
    results = [
        moe_chunk(base, r, h[0], h[1], c[0], c[1], weights)
        for r, h, c in zip(route_chunks, h_chunks, c_chunks)
    ]
    moe = scatter_tokens([(r[0], r[1]) for r in results], step)
    output = middle + RESIDUAL * moe
    grad_normed_moe = scatter_tokens([(r[2], r[3]) for r in results], step)
    hidden = [r[4] for r in results]
    slopes = [r[5] for r in results]
    h_own, h_far = [h[0] for h in h_chunks], [h[1] for h in h_chunks]
    c_own, c_far = [c[0] for c in c_chunks], [c[1] for c in c_chunks]

    half_mask = step // 2
    upper = ((member & half_mask) != 0).astype(jnp.int32).reshape(1)
    own_parts, far_parts = [], []
    for start in range(0, mine, split):
        keep_own, keep_far, send_own, send_far = weight_grads(
            upper, start, split, hidden, slopes, h_own, h_far, c_own, c_far
        )
        keep_own = keep_own + flip(send_own, "dp", half_mask).astype(jnp.float32)
        keep_far = keep_far + flip(send_far, "dp", half_mask).astype(jnp.float32)
        shape = (split, 3, units // 2, part)
        keep_own, keep_far = keep_own.reshape(shape), keep_far.reshape(shape)
        mask = half_mask // 2
        while mask:
            keep_own = halve(keep_own, member, mask, 2)
            keep_far = halve(keep_far, member, mask, 2)
            mask //= 2
        own_parts.append(keep_own)
        far_parts.append(across(keep_far.astype(jnp.bfloat16)).astype(jnp.float32))
    own_part, far_part = jnp.concatenate(own_parts, 0), jnp.concatenate(far_parts, 0)
    expert_grads = jnp.concatenate(
        [jnp.where(col == 0, own_part, far_part), jnp.where(col == 0, far_part, own_part)], 0
    )
    grad_gate = jnp.swapaxes(expert_grads[:, 0], 1, 2)
    grad_up = jnp.swapaxes(expert_grads[:, 1], 1, 2)
    grad_down = expert_grads[:, 2]

    def router_term(rows):
        both = sum(dot_tn(h, r[6]) for h, r in zip(rows, results))
        return both[:, :experts] + both[:, LANES : LANES + experts]

    grad_router = router_term(h_own) + across(router_term(h_far))

    scaled_moe = grad_normed_moe * gain_moe
    grad_gain_moe = jnp.sum(grad_normed_moe * middle * inv_second[:, None], 0)
    inner_moe = jnp.sum(middle * scaled_moe, 1)
    inner_moe = inner_moe + across(inner_moe)
    grad_final = cotangent.astype(jnp.float32)
    grad_middle = (
        grad_final
        + inv_second[:, None] * scaled_moe
        - middle * (inv_second**3 * inner_moe / width)[:, None]
    )
    grad_attn = (RESIDUAL * grad_middle).astype(jnp.bfloat16)
    da_own, da_far = both(grad_attn), both(across(grad_attn))
    grad_mixed = dot_nt(da_own, out_here) + dot_nt(da_far, out_far)
    grad_out_here = dot_tn(mixed, da_own)
    grad_out_there = dot_tn(mixed_far, da_own)
    grad_mixed = heads(grad_mixed.astype(jnp.bfloat16), kv_heads, group_size)
    grad_queries, grad_keys, grad_values = attend_backward(
        query_rows, key_rows, value_rows, allowed, totals, grad_mixed
    )
    grad_queries = unrotate(
        grad_queries.reshape(2 * length_total, -1, HEAD_WIDTH), cosine_table, sine_table
    )
    grad_keys = unrotate(
        grad_keys.reshape(2 * length_total, -1, HEAD_WIDTH), cosine_table, sine_table
    )
    grad_qkv = jnp.concatenate(
        [g.reshape(2 * length_total, -1) for g in (grad_queries, grad_keys, grad_values)], 1
    ).astype(jnp.bfloat16)
    grad_qkv_far = across(grad_qkv)
    grad_normed = dot_nt(grad_qkv, qkv_here) + dot_nt(grad_qkv_far, qkv_there)
    grad_normed = grad_normed[:length_total] + sibling(grad_normed[length_total:])
    grad_qkv_w = jnp.concatenate(
        [dot_tn(normed_own, grad_qkv), dot_tn(normed_own, grad_qkv_far)], 1
    )
    scaled_attn = grad_normed * gain_attn
    grad_gain_attn = jnp.sum(grad_normed * inputs * inv_first[:, None], 0)
    inner_attn = jnp.sum(inputs * scaled_attn, 1)
    inner_attn = inner_attn + across(inner_attn)
    grad_tokens = (
        grad_middle
        + inv_first[:, None] * scaled_attn
        - inputs * (inv_first**3 * inner_attn / width)[:, None]
    )
    grad_router = sum_small(grad_router.T).T
    grad_gain_moe = sum_small(grad_gain_moe)
    grad_gain_attn = sum_small(grad_gain_attn)
    grad_out_w = sum_over_dp(jnp.concatenate([grad_out_here, grad_out_there], 0), group)
    grad_out_w = jnp.where(
        col == 0, grad_out_w, jnp.concatenate([grad_out_w[q_width:], grad_out_w[:q_width]], 0)
    )
    grad_qkv_w = sum_over_dp(grad_qkv_w, group)
    grad_here, grad_there = grad_qkv_w[:, :qkv_width], grad_qkv_w[:, qkv_width:]

    def columns(start, stop):
        here, there = grad_here[:, start:stop], grad_there[:, start:stop]
        return jnp.where(
            col == 0,
            jnp.concatenate([here, there], 1),
            jnp.concatenate([there, here], 1),
        )

    return (
        output,
        grad_tokens,
        grad_gain_attn,
        columns(0, q_width),
        columns(q_width, q_width + kv_width),
        columns(q_width + kv_width, qkv_width),
        grad_out_w,
        grad_gain_moe,
        grad_router,
        grad_gate,
        grad_up,
        grad_down,
    )


def solution(mesh):
    in_specs = (
        P(("dp", "expert"), "col"),
        P("col"),
        P("col", "expert"),
        P("col", "expert"),
        P("col", "expert"),
        P("expert", "col"),
        P("col"),
        P("col", None),
        P("expert", "col", None),
        P("expert", "col", None),
        P("expert", None, "col"),
        P("dp", None),
        P(("dp", "expert"), None),
        P(("dp", "expert"), "col"),
    )
    out_specs = (
        P(("dp", "expert"), "col"),
        P(("dp", "expert"), "col"),
        P("col"),
        P("col", "expert"),
        P("col", "expert"),
        P("col", "expert"),
        P("expert", "col"),
        P("col"),
        P("col", None),
        P("expert", "col", "dp"),
        P("expert", "col", "dp"),
        P("expert", "dp", "col"),
    )
    return jax.shard_map(
        on_device, mesh=mesh, in_specs=in_specs, out_specs=out_specs, check_vma=False
    )
```

```python
import functools
import math

import jax
import jax.numpy as jnp
from jax import lax
from jax.experimental import pallas as pl
from jax.experimental.pallas import tpu as pltpu
from jax.sharding import PartitionSpec as P

HEAD_WIDTH = 64
(
    COT,
    TOK,
    DOWN,
    QKV,
    GATE,
    UP,
    ROUTER,
    GAIN,
    ROUTES,
    MIXED,
    ATTN,
    SQUARE,
    H,
    BACK,
    DA,
    DQKV,
    INNER,
    GRADS,
    MOE,
    SMALL,
    SUM,
) = range(21)
X, C, Y, Z, FAR_X, FAR_C, FAR_Z = range(7)
ZPARTS = 4
LANES = 128


EPS = 1e-06
RESIDUAL = 0.22
SCORE_SCALE = 0.015625
THETA = 10000.0
NEG = -1000000000.0


def doc_positions(seg_row):
    length_total = seg_row.shape[0]
    index = jnp.arange(length_total, dtype=jnp.int32)
    before = jnp.concatenate([jnp.full((1,), -1, jnp.int32), seg_row[:-1]])
    starts = jnp.where(seg_row != before, index, 0)
    return index - lax.cummax(starts, axis=0)


def flip(value, axis, mask=1):
    size = lax.axis_size(axis)
    return lax.ppermute(value, axis, [(i, i ^ mask) for i in range(size)])


def dot_nn(a, b):
    return jnp.dot(a, b, preferred_element_type=jnp.float32)


def dot_nt(a, b):
    return lax.dot_general(a, b, (((1,), (1,)), ((), ())), preferred_element_type=jnp.float32)


def dot_tn(a, b):
    return lax.dot_general(a, b, (((0,), (0,)), ((), ())), preferred_element_type=jnp.float32)


def add_wide(*parts):
    return sum(p.astype(jnp.float32) for p in parts)


def low(value):
    return value.astype(jnp.bfloat16)


class Place:
    def __init__(self):
        self.col = lax.axis_index("col")
        self.core = lax.axis_index("expert")
        group = lax.axis_index("dp")
        self.step = lax.axis_size("dp") // ZPARTS
        self.zed, self.member = group // self.step, group % self.step
        self.half = self.step // 2
        self.side = (self.member // self.half) % 2

    def x(self):
        return {"col": 1 - self.col}

    def c(self):
        return {"expert": 1 - self.core}

    def y(self):
        return {"dp": self.zed * self.step + self.member + self.half * (1 - 2 * self.side)}

    def z(self, k):
        zed = self.zed
        other = (zed + 1 - 2 * (zed % 2), (zed + 2) % ZPARTS, ZPARTS - 1 - zed)[k - 1]
        return {"dp": other * self.step + self.member}

    def bits(self):
        levels = []
        mask = self.half
        while mask:
            bit = (self.member // mask) % 2
            partner = self.zed * self.step + self.member + mask * (1 - 2 * bit)
            levels.append(({"dp": partner}, bit))
            mask //= 2
        return levels, [(self.z(1), self.zed % 2), (self.z(2), self.zed // 2)]


def greet(partners):
    barrier = pltpu.get_barrier_semaphore()
    for partner in partners:
        pl.semaphore_signal(
            barrier, inc=1, device_id=partner, device_id_type=pl.DeviceIdType.MESH
        )
    pl.semaphore_wait(barrier, len(partners))


class Transfers:
    def __init__(self, sems):
        self.sems, self.table, self.waited = sems, {}, set()

    def add(self, key, src, dst, partner):
        self.table[key] = (len(self.table), src, dst, partner)

    def copy(self, key):
        i, src, dst, partner = self.table[key]
        return pltpu.make_async_remote_copy(
            src_ref=src,
            dst_ref=dst,
            send_sem=self.sems.at[0, i],
            recv_sem=self.sems.at[1, i],
            device_id=partner,
            device_id_type=pl.DeviceIdType.MESH,
        )

    def start(self, *keys):
        for key in keys:
            self.copy(key).start()

    def arrived(self, *keys):
        for key in keys:
            self.waited.add(key)
            self.copy(key).wait_recv()

    def sent(self, *keys):
        for key in keys:
            self.copy(key).wait_send()

    def finish(self, *sent):
        for key in self.table:
            if key not in sent:
                self.copy(key).wait_send()
        for key in self.table:
            if key not in self.waited:
                self.copy(key).wait_recv()


def moves(sems, *pairs):
    copies = [pltpu.make_async_copy(src, dst, sems.at[i]) for i, (src, dst) in enumerate(pairs)]
    for copy in copies:
        copy.start()
    for copy in copies:
        copy.wait()


ANY = pl.BlockSpec(memory_space=pl.ANY)


def whole_block(a):
    return pl.BlockSpec(a.shape, lambda *_: (0,) * a.ndim, pipeline_mode=pl.Buffered(1))


def turn(block, cosine, sine):
    lane = lax.broadcasted_iota(jnp.int32, block.shape, 1) % HEAD_WIDTH
    ahead = pltpu.roll(block, LANES - HEAD_WIDTH // 2, 1)
    behind = pltpu.roll(block, HEAD_WIDTH // 2, 1)
    return block * cosine + jnp.where(lane < HEAD_WIDTH // 2, ahead, behind) * sine


def score_tiles(rows):
    half = rows // 2
    return ((0, half, half), (half, rows, rows))


def allowed_tile(seg_row, seg_col, across_keys):
    shape = (seg_col.shape[0], seg_row.shape[1])
    down, along = (lax.broadcasted_iota(jnp.int32, shape, axis) for axis in (0, 1))
    order = down <= along if across_keys else along <= down
    return jnp.where((seg_row == seg_col) & order, 1.0, 0.0)


def swap_heads(value):
    return pltpu.roll(value.astype(jnp.float32), HEAD_WIDTH, 1).astype(value.dtype)


def attend_rows(q_ref, keys_ref, values_ref, allowed_ref, out_ref, base, blocks):
    rows = allowed_ref.shape[0]
    group = blocks

    def body(j, carry):
        cols = pl.ds(pl.multiple_of(j * LANES, LANES), LANES)
        for start, stop, keys in score_tiles(rows):
            lane = lax.broadcasted_iota(jnp.int32, (stop - start, LANES), 1)
            query = q_ref[base + start : base + stop, cols]
            allowed = allowed_ref[start:stop, :keys] > 0
            outs = []
            for side, part in enumerate((lane < HEAD_WIDTH, lane >= HEAD_WIDTH)):
                other = (2 * j + side) // group
                other = other + side - 2 * other * side
                key_rows = keys_ref[other, base : base + keys, :]
                scores = dot_nt(jnp.where(part, query, jnp.zeros_like(query)), key_rows)
                scores = jnp.where(allowed, scores * SCORE_SCALE, NEG)
                expo = jnp.exp(scores - jnp.max(scores, axis=1, keepdims=True))
                probs = expo * (1.0 / jnp.sum(expo, axis=1, keepdims=True))
                outs.append(dot_nn(low(probs), values_ref[other, base : base + keys, :]))
            mixed = jnp.where(lane < HEAD_WIDTH, outs[0], outs[1])
            out_ref[base + start : base + stop, cols] = low(mixed)
        return carry

    lax.fori_loop(0, blocks, body, 0)


def weight_slice(ref, which, half, split, zed, wide):
    first = (2 * which + half) * split
    units = pl.ds(pl.multiple_of(zed * LANES, LANES), LANES)
    if wide:
        return ref.at[pl.ds(first, split), units, :]
    return ref.at[pl.ds(first, split), :, units]


def qkv_slices(refs, which):
    widths = [ref.shape[1] // 2 for ref in refs]
    return [
        ref.at[:, pl.ds(pl.multiple_of(which * w, LANES), w)] for ref, w in zip(refs, widths)
    ]


def qkv_targets(target, refs):
    widths = [ref.shape[1] // 2 for ref in refs]
    starts = [sum(widths[:i]) for i in range(len(widths))]
    return [target.at[:, pl.ds(start, w)] for start, w in zip(starts, widths)]


def front_kernel(*refs):
    tokens, cot, w_down, w_gate, w_up, router, routes = refs[:7]
    qkv = refs[7:10]
    gain, gain_moe, w_out, cosine, sine, seg_row, seg_col = refs[10:17]
    (
        down_got,
        down_other,
        gate_got,
        gate_other,
        up_got,
        up_other,
        router_far,
        c_own,
        c_far,
        route_all,
        grad_hidden,
        q_ref,
        keys,
        values,
        mixed,
        mixed_far,
        normed,
        inv_first,
        middle_ref,
        inv_second,
        h2_ref,
    ) = refs[17:38]
    tok, qkv_here, qkv_far, gain_far, normed_far, give, got, square, square_far = refs[38:47]
    own_buf, far_buf, down_own, down_buf, grad_buf, allowed, sems, local = refs[47:]
    place = Place()
    t = Transfers(sems)
    x, c, y = place.x(), place.c(), place.y()
    z = [None] + [place.z(k) for k in range(1, ZPARTS)]
    rows, part = tokens.shape
    ks = range(1, ZPARTS)
    t.add((TOK, X), tokens, tok.at[0], x)
    t.add((TOK, C), tokens, tok.at[1], c)
    t.add((TOK, FAR_C), tok.at[0], tok.at[2], c)
    there = qkv_slices(qkv, 1 - place.col)
    for i, target in enumerate(qkv_targets(qkv_far, qkv)):
        t.add((QKV, X, i), there[i], target, x)
    t.add((GAIN, X), gain, gain_far, x)
    t.add((ROUTER, X), router, router_far, x)
    t.add((COT, X), cot, c_far.at[0, 0], x)
    t.add((COT, C, 0), cot, c_own.at[0, 1], c)
    t.add((COT, FAR_C, 0), c_far.at[0, 0], c_far.at[0, 1], c)
    t.add((ROUTES, C, 0), routes, route_all.at[0, 1], c)
    for k in ks:
        t.add((COT, Z, k), cot, c_own.at[k, 0], z[k])
        t.add((COT, FAR_Z, k), c_far.at[0, 0], c_far.at[k, 0], z[k])
        t.add((COT, C, k), c_own.at[k, 0], c_own.at[k, 1], c)
        t.add((COT, FAR_C, k), c_far.at[k, 0], c_far.at[k, 1], c)
        t.add((ROUTES, Z, k), routes, route_all.at[k, 0], z[k])
        t.add((ROUTES, C, k), route_all.at[k, 0], route_all.at[k, 1], c)
    split = down_got.shape[0]
    for key, ref, land, other in (
        (DOWN, w_down, down_got, down_other),
        (GATE, w_gate, gate_got, gate_other),
        (UP, w_up, up_got, up_other),
    ):
        src = weight_slice(ref, 1 - place.col, place.side, split, place.zed, key == DOWN)
        t.add((key, X), src, land, x)
        t.add((key, Y), land, other, y)
    for i in range(2):
        cut = pl.ds(rows * i, rows)
        t.add((MIXED, X, i), mixed.at[cut], mixed_far.at[cut], x)
    t.add((ATTN, C), give, got, c)
    t.add((SQUARE, X), square, square_far, x)

    greet([x, c, y, *z[1:]])
    t.start((COT, X), (TOK, X), (GAIN, X), *[(QKV, X, i) for i in range(3)], (ROUTER, X))
    t.start((TOK, C), (COT, C, 0), (ROUTES, C, 0), *[(ROUTES, Z, k) for k in ks])
    t.start((COT, Z, 1), (COT, Z, 2), (COT, Z, 3))
    own_cut = functools.partial(weight_slice, w_down, place.col, split=split, zed=place.zed)
    moves(
        local,
        (cot, c_own.at[0, 0]),
        (routes, route_all.at[0, 0]),
        (own_cut(half=place.side, wide=True), down_own.at[pl.ds(0, split)]),
        (own_cut(half=1 - place.side, wide=True), down_own.at[pl.ds(split, split)]),
        *zip(qkv_slices(qkv, place.col), qkv_targets(qkv_here, qkv)),
    )

    def norm(own, far, base):
        own, far = own.astype(jnp.float32), far.astype(jnp.float32)
        total = jnp.sum(own * own, 1, keepdims=True) + jnp.sum(far * far, 1, keepdims=True)
        inv = lax.rsqrt(total / (2 * part) + EPS)
        normed[base : base + rows, :] = (own * inv * gain[...]).astype(jnp.bfloat16)
        normed_far[base : base + rows, :] = (far * inv * gain_far[...]).astype(jnp.bfloat16)
        return inv

    def masks(b):
        allowed[...] = allowed_tile(seg_row[b : b + 1, :], seg_col[:, b : b + 1], False)

    masks(1)
    t.arrived((COT, X))
    t.start((COT, FAR_C, 0), *[(COT, FAR_Z, k) for k in ks])
    t.arrived((TOK, X), (GAIN, X))
    t.start((TOK, FAR_C))
    inv = norm(tokens[...], tok[0], 0)
    inv_first[...] = jnp.broadcast_to(inv, inv_first.shape)
    t.arrived((TOK, C), (TOK, FAR_C))
    norm(tok[1], tok[2], rows)
    for k in ks:
        t.arrived((ROUTES, Z, k))
        t.start((ROUTES, C, k))
    t.arrived((COT, Z, 1))
    t.start((COT, C, 1))
    t.arrived(*[(QKV, X, i) for i in range(3)])
    t.start((DOWN, X))

    width = q_ref.shape[1]
    for base in (rows, 0):
        cut = slice(base, base + rows)
        qkv_rows = dot_nn(normed[cut, :], qkv_here[...])
        qkv_rows = qkv_rows + dot_nn(normed_far[cut, :], qkv_far[...])
        for i in range(width // LANES + 1):
            block = qkv_rows[:, LANES * i : LANES * (i + 1)]
            block = turn(block, cosine[cut, :], sine[cut, :])
            if i < width // LANES:
                q_ref[cut, LANES * i : LANES * (i + 1)] = low(block)
            else:
                keys[0, cut, :] = low(block)
                keys[1, cut, :] = swap_heads(low(block))
        block = low(qkv_rows[:, width + LANES :])
        values[0, cut, :] = block
        values[1, cut, :] = swap_heads(block)
    attend_rows(q_ref, keys, values, allowed, mixed, rows, width // LANES)
    t.start((MIXED, X, 1))
    t.arrived((COT, Z, 2))
    t.start((COT, C, 2))
    masks(0)
    attend_rows(q_ref, keys, values, allowed, mixed, 0, width // LANES)
    t.start((MIXED, X, 0))
    t.arrived((DOWN, X))
    t.start((DOWN, Y), (GATE, X))

    def project(base):
        cut = slice(base, base + rows)
        first = pl.ds(pl.multiple_of(place.col * width, LANES), width)
        second = pl.ds(pl.multiple_of((1 - place.col) * width, LANES), width)
        return dot_nn(mixed[cut, :], w_out[first, :]) + dot_nn(mixed_far[cut, :], w_out[second, :])

    def stored(i):
        out = grad_hidden.at[pl.ds(rows * i, rows)]
        return pltpu.make_async_copy(grad_buf.at[i % 2], out, local.at[8 + i % 2])

    def hidden_grads(i):
        k, p = i // 2, i % 2
        if p == 1:
            t.arrived((COT, C, k), (COT, FAR_C, k))
        moves(local, (c_own.at[k, p], own_buf), (c_far.at[k, p], far_buf))
        if i > 1:
            stored(i - 2).wait()
        size = split * LANES
        for n in range(2):
            own_rows = down_own[split * n : split * (n + 1)].reshape(size, part)
            far_rows = down_buf[n].reshape(size, part)
            total = dot_nt(own_buf[...], own_rows) + dot_nt(far_buf[...], far_rows)
            grad_buf[i % 2, :, size * n : size * (n + 1)] = RESIDUAL * total
        stored(i).start()

    t.arrived((MIXED, X, 1))
    give[...] = project(rows)
    t.start((ATTN, C))
    t.arrived((MIXED, X, 0))
    attn = project(0)
    t.arrived((ATTN, C))
    middle = tokens[...].astype(jnp.float32) + RESIDUAL * (attn + got[...])
    middle_ref[...] = middle
    total = jnp.sum(middle * middle, 1, keepdims=True)
    square[...] = jnp.broadcast_to(total, (rows, LANES)).T[:8, :]
    t.start((SQUARE, X))
    t.arrived((DOWN, Y))
    moves(local, (down_got, down_buf.at[0]), (down_other, down_buf.at[1]))
    t.arrived((SQUARE, X))
    t.start((UP, X))
    total = total + jnp.broadcast_to(square_far[:1, :], (LANES, rows)).T[:, :1]
    inv = lax.rsqrt(total / (2 * part) + EPS)
    inv_second[...] = jnp.broadcast_to(inv, inv_second.shape)
    h2_ref[...] = low(middle_ref[...] * inv * gain_moe[...])

    hidden_grads(0)
    hidden_grads(1)
    t.arrived((COT, FAR_Z, 1))
    t.start((COT, FAR_C, 1))
    hidden_grads(2)
    t.arrived((GATE, X))
    t.start((GATE, Y))
    hidden_grads(3)
    t.arrived((COT, FAR_Z, 2))
    t.start((COT, FAR_C, 2))
    t.arrived((COT, Z, 3))
    t.start((COT, C, 3))
    hidden_grads(4)
    hidden_grads(5)
    t.arrived((COT, FAR_Z, 3))
    t.start((COT, FAR_C, 3))
    hidden_grads(6)
    t.arrived((UP, X))
    t.start((UP, Y))
    hidden_grads(7)
    stored(6).wait()
    stored(7).wait()
    t.finish()


def front(tokens, cot, w_down, w_gate, w_up, router, routes, qkv, *others):
    rows, part = tokens.shape
    gain, w_out = others[0], others[2]
    vmem = pl.BlockSpec(memory_space=pltpu.VMEM)
    shape = lambda dims, dtype=jnp.bfloat16: jax.ShapeDtypeStruct(dims, dtype)
    like = lambda a: shape(a.shape, a.dtype)
    stack = lambda a: shape((ZPARTS, 2, *a.shape), a.dtype)
    mine = w_down.shape[0] // 2
    width, kv = qkv[0].shape[1] // 2, qkv[1].shape[1] // 2
    down, pair = shape((mine // 2, LANES, part)), shape((mine // 2, part, LANES))
    hbm_outs = [down, down, pair, pair, pair, pair, like(router)]
    hbm_outs += [stack(cot), stack(cot), stack(routes)]
    hbm_outs += [shape((2 * ZPARTS * rows, mine * LANES), jnp.float32)]
    vmem_outs = [
        shape((2 * rows, width)),
        shape((2, 2 * rows, kv)),
        shape((2, 2 * rows, kv)),
        shape((2 * rows, width)),
        shape((2 * rows, width)),
        shape((2 * rows, part)),
        shape((rows, LANES), jnp.float32),
        shape((rows, part), jnp.float32),
        shape((rows, LANES), jnp.float32),
        shape((rows, part)),
    ]
    buffer = pltpu.VMEM((rows, part), jnp.bfloat16)
    wide = pltpu.VMEM((rows, part), jnp.float32)
    small = pltpu.VMEM((8, rows), jnp.float32)
    weights = pltpu.VMEM((part, width + 2 * kv), jnp.bfloat16)
    count = 12 + 6 * (ZPARTS - 1) + 6 + 2 + 2
    return pl.pallas_call(
        front_kernel,
        out_shape=hbm_outs + vmem_outs,
        in_specs=[vmem] + [ANY] * 9 + [vmem] * len(others),
        out_specs=[ANY] * len(hbm_outs) + [vmem] * len(vmem_outs),
        scratch_shapes=[
            pltpu.VMEM((3, rows, part), jnp.bfloat16),
            weights,
            weights,
            pltpu.VMEM(gain.shape, jnp.float32),
            pltpu.VMEM((2 * rows, part), jnp.bfloat16),
            wide,
            wide,
            small,
            small,
            buffer,
            buffer,
            pltpu.VMEM((mine, LANES, part), jnp.bfloat16),
            pltpu.VMEM((2, mine // 2, LANES, part), jnp.bfloat16),
            pltpu.VMEM((2, rows, mine * LANES), jnp.float32),
            pltpu.VMEM((rows, rows), jnp.float32),
            pltpu.SemaphoreType.DMA((2, count)),
            pltpu.SemaphoreType.DMA((10,)),
        ],
        compiler_params=pltpu.CompilerParams(
            collective_id=0, has_side_effects=True, vmem_limit_bytes=58 * 1024 * 1024
        ),
        name="front",
    )(tokens, cot, w_down, w_gate, w_up, router, routes, *qkv, *others)


def moe_kernel(*refs):
    routes_ref, grad_ref, router_own, router_far, h2 = refs[:5]
    w_gate, w_up, w_down, gate_got, gate_other, up_got, up_other, down_got, down_other = refs[5:14]
    (
        h_own_all,
        h_far_all,
        moe_own,
        moe_far,
        hidden_ref,
        slopes_ref,
        dlog_ref,
        s0_own,
        s0_far,
        z1_own,
        z1_far,
        piece2,
        s3_own,
        s3_far,
    ) = refs[14:28]
    h_own, h_far, keep_own, keep_far, give_own, give_far, got_own, got_far, got_x = refs[28:37]
    pair_own, pair_far, down_own, down_far, sems, local, fill = refs[37:]
    experts = down_own.shape[0]
    split = experts // 2
    rows = h_own.shape[0]
    place = Place()
    step = pl.program_id(0)
    t = Transfers(sems)
    x, c = place.x(), place.c()
    z = [None] + [place.z(k) for k in range(1, ZPARTS)]
    t.add((H, X), h2, h_far_all.at[0, 0], x)
    t.add((H, C, 0), h2, h_own_all.at[0, 1], c)
    t.add((H, FAR_C, 0), h_far_all.at[0, 0], h_far_all.at[0, 1], c)
    for k in range(1, ZPARTS):
        t.add((H, Z, k), h2, h_own_all.at[k, 0], z[k])
        if k == 1:
            t.add((H, FAR_X, 1), h_far_all.at[0, 0], h_far_all.at[1, 0], z[1])
        else:
            t.add((H, FAR_X, k), h_own_all.at[k, 0], h_far_all.at[k, 0], x)
        t.add((H, C, k), h_own_all.at[k, 0], h_own_all.at[k, 1], c)
        t.add((H, FAR_C, k), h_far_all.at[k, 0], h_far_all.at[k, 1], c)
    for k in range(ZPARTS):
        t.add((BACK, C, k), give_own, got_own.at[k], c)
        t.add((BACK, FAR_C, k), give_far, got_far.at[k], c)
    t.add((BACK, Z), got_own.at[1], z1_own, z[1])
    t.add((BACK, FAR_Z), got_far.at[1], z1_far, z[1])
    t.add((BACK, FAR_X), got_far.at[2], got_x, x)

    def join(k):
        for name in ((BACK, C, k), (BACK, FAR_C, k)):
            t.copy(name).wait_send()
        t.arrived((BACK, C, k), (BACK, FAR_C, k))
        for got, keep in ((got_own, keep_own), (got_far, keep_far)):
            total = got[k].astype(jnp.float32) + keep[...].astype(jnp.float32)
            got[k] = total.astype(jnp.bfloat16)

    @pl.when(step == 0)
    def _():
        greet([x, c, *z[1:]])
        t.start((H, X), (H, C, 0), (H, Z, 1), (H, Z, 2))
        cut = functools.partial(weight_slice, which=place.col, split=split, zed=place.zed)
        fills = []
        for i, half in enumerate((place.side, 1 - place.side)):
            gates = (cut(w_gate, half=half, wide=False), (gate_got, gate_other)[i])
            ups = (cut(w_up, half=half, wide=False), (up_got, up_other)[i])
            downs = (cut(w_down, half=half, wide=True), (down_got, down_other)[i])
            for n, (pair, down) in enumerate(((pair_own, down_own), (pair_far, down_far))):
                for e in range(split):
                    for m, src in enumerate((gates[n], ups[n])):
                        cols = pl.ds(LANES * (2 * e + m), LANES)
                        fills.append((src.at[e], pair.at[i, :, cols]))
                fills.append((downs[n], down.at[pl.ds(split * i, split)]))
        moves(fill, (h2, h_own_all.at[0, 0]), *fills)
        t.arrived((H, X))
        t.start((H, FAR_C, 0), (H, FAR_X, 1))

    @pl.when(step == 1)
    def _():
        t.arrived((H, C, 0), (H, FAR_C, 0), (H, Z, 1))
        t.start((H, C, 1))

    @pl.when(step == 2)
    def _():
        t.start((H, Z, 3))
        t.arrived((H, FAR_X, 1))
        t.start((H, FAR_C, 1))
        join(0)
        t.arrived((H, Z, 2))
        t.start((H, FAR_X, 2), (H, C, 2))

    @pl.when(step == 3)
    def _():
        t.arrived((H, C, 1), (H, FAR_C, 1))

    @pl.when(step == 4)
    def _():
        join(1)
        t.start((BACK, Z), (BACK, FAR_Z))
        t.arrived((H, FAR_X, 2))
        t.start((H, FAR_C, 2))
        t.arrived((H, Z, 3))
        t.start((H, FAR_X, 3), (H, C, 3))

    @pl.when(step == 5)
    def _():
        t.arrived((H, C, 2), (H, FAR_C, 2))

    @pl.when(step == 6)
    def _():
        join(2)
        t.start((BACK, FAR_X))
        t.arrived((H, FAR_X, 3))
        t.start((H, FAR_C, 3))

    @pl.when(step == 7)
    def _():
        t.arrived((H, C, 3), (H, FAR_C, 3))
        t.arrived((BACK, FAR_X))
        total = got_own[2].astype(jnp.float32) + got_x[...].astype(jnp.float32)
        got_own[2] = total.astype(jnp.bfloat16)

    for k in range(ZPARTS):
        for p in range(2):

            @pl.when(step == 2 * k + p)
            def _():
                moves(local, (h_own_all.at[k, p], h_own), (h_far_all.at[k, p], h_far))

    first = (place.core * 2 + place.col) * experts
    lane = lax.broadcasted_iota(jnp.int32, (rows, LANES), 1)
    chosen = lane == routes_ref[:, 0:1]
    for k in range(1, routes_ref.shape[1]):
        chosen = chosen | (lane == routes_ref[:, k : k + 1])
    logits = dot_nn(h_own[...], router_own[...]) + dot_nn(h_far[...], router_far[...])
    peak = jnp.max(jnp.where(chosen, logits, -jnp.inf), axis=1, keepdims=True)
    expo = jnp.where(chosen, jnp.exp(logits - peak), 0.0)
    gates = expo / jnp.sum(expo, axis=1, keepdims=True)
    grad_gates = jnp.zeros((rows, LANES), jnp.float32)
    for e in range(experts):
        here = lane == first + (e + place.side * split) % experts
        gate = jnp.sum(jnp.where(here, gates, 0.0), axis=1, keepdims=True)
        cols = slice(2 * LANES * (e % split), 2 * LANES * (e % split + 1))
        pair = dot_nn(h_own[...], pair_own[e // split, :, cols]) + dot_nn(
            h_far[...], pair_far[e // split, :, cols]
        )
        slope = grad_ref[:, LANES * e : LANES * (e + 1)]
        gate_val = pair[:, :LANES]
        up_val = pair[:, LANES:]
        sigma = jax.nn.sigmoid(gate_val)
        silu = gate_val * sigma
        hidden = silu * up_val
        dgate = jnp.sum(hidden * slope, axis=1, keepdims=True)
        grad_gates = jnp.where(here, dgate, grad_gates)
        dz = gate * slope
        hidden_ref[:, LANES * e : LANES * (e + 1)] = (gate * hidden).astype(jnp.bfloat16)
        slopes_ref[:, 2 * LANES * e : 2 * LANES * e + LANES] = (
            dz * up_val * (sigma + silu * (1.0 - sigma))
        ).astype(jnp.bfloat16)
        slopes_ref[:, 2 * LANES * e + LANES : 2 * LANES * (e + 1)] = (dz * silu).astype(
            jnp.bfloat16
        )
    dlog = gates * (grad_gates - jnp.sum(gates * grad_gates, axis=1, keepdims=True))
    dlog_high = dlog.astype(jnp.bfloat16)
    dlog_low = (dlog - dlog_high.astype(jnp.float32)).astype(jnp.bfloat16)
    dlog_ref[:, :LANES] = dlog_high
    dlog_ref[:, LANES:] = dlog_low

    def back(pairs, router):
        total = dot_nt(dlog_high, router[...]) + dot_nt(dlog_low, router[...])
        for i in range(2):
            cols = slice(2 * LANES * split * i, 2 * LANES * split * (i + 1))
            total = total + dot_nt(slopes_ref[:, cols], pairs[i])
        return total.astype(jnp.bfloat16)

    back_own, back_far = back(pair_own, router_own), back(pair_far, router_far)
    last = pl.num_programs(0) - 1

    @pl.when(step % 2 == 0)
    def _():
        keep_own[...] = back_own
        keep_far[...] = back_far

    @pl.when(step % 2 == 1)
    def _():
        give_own[...] = back_own
        give_far[...] = back_far

    for k in range(ZPARTS):

        @pl.when(step == 2 * k + 1)
        def _():
            t.start((BACK, C, k), (BACK, FAR_C, k))

    part = h_own.shape[1]
    moe_own[...] = low(dot_nn(hidden_ref[...], down_own[...].reshape(-1, part)))
    moe_far[...] = low(dot_nn(hidden_ref[...], down_far[...].reshape(-1, part)))

    @pl.when(step == last)
    def _():
        join(ZPARTS - 1)
        moves(
            local,
            (got_own.at[0], s0_own),
            (got_far.at[0], s0_far),
            (got_own.at[2], piece2),
            (got_own.at[3], s3_own),
            (got_far.at[3], s3_far),
        )
        t.finish(*[(BACK, hop, k) for hop in (C, FAR_C) for k in range(ZPARTS)])


def moe_layer(routes, grad_hidden, routers, h2, weights):
    tile, part = h2.shape
    rows = grad_hidden.shape[0]
    experts = grad_hidden.shape[1] // LANES
    by_row = lambda width: pl.BlockSpec((tile, width), lambda i: (i, 0))
    stack = jax.ShapeDtypeStruct((ZPARTS, 2, tile, part), jnp.bfloat16)
    one = jax.ShapeDtypeStruct((tile, part), jnp.bfloat16)
    widths = [part, part, experts * LANES, 2 * experts * LANES, 2 * LANES]
    buffer = pltpu.VMEM((tile, part), jnp.bfloat16)
    stacked = pltpu.VMEM((ZPARTS, tile, part), jnp.bfloat16)
    pair = pltpu.VMEM((2, part, experts * LANES), jnp.bfloat16)
    down = pltpu.VMEM((experts, LANES, part), jnp.bfloat16)
    count = 3 + 4 * (ZPARTS - 1) + 2 * ZPARTS + 3
    return pl.pallas_call(
        moe_kernel,
        out_shape=[stack, stack]
        + [jax.ShapeDtypeStruct((rows, w), jnp.bfloat16) for w in widths]
        + [one] * 7,
        grid=(rows // tile,),
        in_specs=[by_row(routes.shape[1]), by_row(experts * LANES)]
        + [whole_block(r) for r in routers]
        + [ANY] * (1 + len(weights)),
        out_specs=[ANY, ANY] + [by_row(w) for w in widths] + [ANY] * 7,
        scratch_shapes=[buffer] * 6
        + [stacked] * 2
        + [buffer, pair, pair, down, down]
        + [
            pltpu.SemaphoreType.DMA((2, count)),
            pltpu.SemaphoreType.DMA((5,)),
            pltpu.SemaphoreType.DMA((5 + 4 * experts,)),
        ],
        compiler_params=pltpu.CompilerParams(
            collective_id=1, has_side_effects=True, vmem_limit_bytes=60 * 1024 * 1024
        ),
        name="moe_layer",
    )(routes, grad_hidden, *routers, h2, *weights)


def weight_kernel(cargo, n_cargo, *refs):
    h_own, h_far, c_own, c_far, hidden, slopes = refs[:6]
    sources = refs[6 : 6 + n_cargo]
    outs = refs[6 + n_cargo : 10 + n_cargo]
    landed = refs[10 + n_cargo : 10 + 2 * n_cargo]
    sems = refs[-1]
    place = Place()
    step = pl.program_id(0)
    t = Transfers(sems)
    partners = {X: place.x(), Y: place.y(), C: place.c()}
    partners.update({(Z, k): place.z(k) for k in range(1, ZPARTS)})
    to = {name: partners[name] for name in cargo}
    for i, name in enumerate(cargo):
        t.add(i, sources[i], landed[i], to[name])

    @pl.when(step == 0)
    def _():
        greet(list(to.values()))
        t.start(*t.table)

    half = LANES // 2
    tile = h_own.shape[2]
    first = place.side == 0
    for keep, give, rows_h, rows_c in (
        (outs[0], outs[2], h_own, c_own),
        (outs[1], outs[3], h_far, c_far),
    ):
        pair, down = 0.0, 0.0
        for i in range(2 * ZPARTS):
            rows = slice(tile * i, tile * (i + 1))
            pair = pair + dot_tn(slopes[rows, :], rows_h[i // 2, i % 2])
            down = down + dot_tn(hidden[rows, :], rows_c[i // 2, i % 2])
        for i, block in enumerate((pair[:LANES], pair[LANES:], RESIDUAL * down)):
            low, high = block[:half], block[half:]
            keep[0, half * i : half * (i + 1), :] = jnp.where(first, low, high)
            give[0, half * i : half * (i + 1), :] = jnp.where(first, high, low).astype(
                jnp.bfloat16
            )

    @pl.when(step == pl.num_programs(0) - 1)
    def _():
        t.finish()


def weight_grads(number, start, count, resident, hidden, slopes, cargo):
    part = resident[0].shape[-1]
    rows = hidden.shape[0]
    out = pl.BlockSpec((1, 3 * LANES // 2, part), lambda e: (e, 0, 0))
    shape = (count, 3 * LANES // 2, part)
    names = tuple(name for name, _ in cargo)
    arrays = [array for _, array in cargo]
    return pl.pallas_call(
        functools.partial(weight_kernel, names, len(names)),
        out_shape=[jax.ShapeDtypeStruct(shape, jnp.float32)] * 2
        + [jax.ShapeDtypeStruct(shape, jnp.bfloat16)] * 2
        + [jax.ShapeDtypeStruct(a.shape, a.dtype) for a in arrays],
        grid=(count,),
        in_specs=[whole_block(a) for a in resident]
        + [
            pl.BlockSpec((rows, LANES), lambda e: (0, e + start)),
            pl.BlockSpec((rows, 2 * LANES), lambda e: (0, e + start)),
        ]
        + [ANY] * len(arrays),
        out_specs=[out] * 4 + [ANY] * len(arrays),
        scratch_shapes=[pltpu.SemaphoreType.DMA((2, len(names)))],
        compiler_params=pltpu.CompilerParams(
            collective_id=2 + number, has_side_effects=True, vmem_limit_bytes=60 * 1024 * 1024
        ),
        name="expert_weight_grads",
    )(*resident, hidden, slopes, *arrays)


def unturn(block, cosine, sine):
    return block * cosine + turn(block, jnp.zeros_like(cosine), -sine)


def attend_back_rows(
    q_ref, keys_ref, values_ref, grad_ref, allowed_ref, out_ref, dk, dv, cosine, sine, base, blocks
):
    rows = allowed_ref.shape[0]
    dk[...] = jnp.zeros_like(dk)
    dv[...] = jnp.zeros_like(dv)

    def body(j, carry):
        cols = pl.ds(pl.multiple_of(j * LANES, LANES), LANES)
        for start, stop, keys in score_tiles(rows):
            cut = slice(base + start, base + stop)
            lane = lax.broadcasted_iota(jnp.int32, (stop - start, LANES), 1)
            query, grad = q_ref[cut, cols], grad_ref[cut, cols]
            allowed = allowed_ref[:keys, start:stop] > 0
            dqs = []
            for side, part in enumerate((lane < HEAD_WIDTH, lane >= HEAD_WIDTH)):
                other = (2 * j + side) // blocks
                other = other + side - 2 * other * side
                key_rows = keys_ref[other, base : base + keys, :]
                value_rows = values_ref[other, base : base + keys, :]
                one_query = jnp.where(part, query, jnp.zeros_like(query))
                one_grad = jnp.where(part, grad, jnp.zeros_like(grad))
                scores = jnp.where(allowed, dot_nt(key_rows, one_query) * SCORE_SCALE, NEG)
                expo = jnp.exp(scores - jnp.max(scores, axis=0, keepdims=True))
                probs = expo * (1.0 / jnp.sum(expo, axis=0, keepdims=True))
                slope = dot_nt(value_rows, one_grad)
                delta = jnp.sum(probs * slope, axis=0, keepdims=True)
                dscore = low(probs * (slope - delta))
                dv[other, :keys, :] = dv[other, :keys, :] + dot_nn(low(probs), one_grad)
                dk[other, :keys, :] = dk[other, :keys, :] + dot_nn(dscore, one_query)
                dqs.append(dot_tn(dscore, key_rows))
            dq = jnp.where(lane < HEAD_WIDTH, dqs[0], dqs[1]) * SCORE_SCALE
            out_ref[cut, cols] = low(unturn(dq, cosine[cut, :], sine[cut, :]))
        return carry

    lax.fori_loop(0, blocks, body, 0)
    cut = slice(base, base + rows)
    width = blocks * LANES
    total = (dk[0] + pltpu.roll(dk[1], HEAD_WIDTH, 1)) * SCORE_SCALE
    out_ref[cut, width : width + LANES] = low(unturn(total, cosine[cut, :], sine[cut, :]))
    out_ref[cut, width + LANES :] = low(dv[0] + pltpu.roll(dv[1], HEAD_WIDTH, 1))


class WholeSum:
    def __init__(self, t, name, ref, levels, stages, lands):
        self.t, self.name, self.ref = t, name, ref
        self.stages, self.lands, self.count = stages, lands, len(levels)
        offset, rows = 0, ref.shape[0]
        self.kept, self.other = [], []
        for i, (partner, bit) in enumerate(levels):
            rows = rows // 2
            self.other.append((offset + (1 - bit) * rows, rows))
            offset = offset + bit * rows
            self.kept.append((offset, rows))
            t.add((SUM, name, i), stages[i], lands[i], partner)
            t.add((SUM, name, 2 * self.count - 1 - i), stages[i], lands[self.count + i], partner)

    def rows(self, place):
        return pl.ds(pl.multiple_of(place[0], 8), place[1])

    def send(self, i):
        j = min(i, 2 * self.count - 1 - i)
        if i >= self.count:
            self.t.sent((SUM, self.name, j))
        place = (self.other if i < self.count else self.kept)[j]
        self.stages[j][...] = low(self.ref[self.rows(place), :])
        self.t.start((SUM, self.name, i))

    def land(self, i):
        self.t.arrived((SUM, self.name, i))
        if i < self.count:
            cut = self.rows(self.kept[i])
            total = self.ref[cut, :] + self.lands[i][...].astype(jnp.float32)
            self.ref[cut, :] = low(total).astype(jnp.float32) if i == self.count - 1 else total
        else:
            j = 2 * self.count - 1 - i
            cut = self.rows(self.other[j])
            self.ref[cut, :] = self.lands[self.count + j][...].astype(jnp.float32)

    def next(self, i):
        self.land(i)
        if i + 1 < 2 * self.count:
            self.send(i + 1)

    def keys(self):
        return [(SUM, self.name, i) for i in range(self.count)]


class SmallSum:
    def __init__(self, t, name, ref, partners, lands):
        self.t, self.name, self.ref, self.lands = t, name, ref, lands
        for i, partner in enumerate(partners):
            t.add((SMALL, name, i), ref, lands.at[i], partner)

    def send(self, i):
        self.t.start((SMALL, self.name, i))

    def land(self, i):
        self.t.sent((SMALL, self.name, i))
        self.t.arrived((SMALL, self.name, i))
        self.ref[...] = self.ref[...] + self.lands[i]

    def next(self, i):
        self.land(i)
        if i + 1 < self.lands.shape[0]:
            self.send(i + 1)

    def keys(self):
        return [(SMALL, self.name, i) for i in range(self.lands.shape[0])]


SUMMED = 40


def back_kernel(count, with_grads, *refs):
    refs = list(refs)
    take = lambda n: [refs.pop(0) for _ in range(n)]
    qkv = take(3)
    moe_srcs = take(4)
    tokens, cot, middle, inv_first, inv_second, gain, gain_moe = take(7)
    parts = take(5)
    q_ref, keys, values, mixed, mixed_far, normed, cosine, sine, seg_row, seg_col = take(10)
    w_out, out_far, small_own, small_there = take(4)
    if with_grads:
        grad_srcs, keep_first = take(4), take(1)[0]
    moe_lands = take(4)
    if with_grads:
        grad_lands = take(4)
    grad_tokens, grad_q, grad_k, grad_v, grad_out, small, small_last = take(7)
    qkv_here, qkv_there, da_own, da_far, grad_mixed, dqkv, dqkv_far, give, got = take(9)
    grad_middle, grad_here, grad_there, allowed, dk, dv, square, square_far = take(8)
    small_land, small_lands, last_lands = take(3)
    stages, lands = [], []
    for _ in range(3):
        stages.append(take(count))
        lands.append(take(2 * count))
    if with_grads:
        first_land, first_sum = take(2)
    sems, local = take(2)
    place = Place()
    t = Transfers(sems)
    x, c, y = place.x(), place.c(), place.y()
    rows, part = tokens.shape
    width = q_ref.shape[1]
    low_levels, high_levels = place.bits()
    partners = [partner for partner, _ in low_levels + high_levels]
    t.add((INNER, 0), square.at[0], square_far.at[0], x)
    t.add((INNER, 1), square.at[1], square_far.at[1], x)
    t.add((SMALL, X), small_there, small_land, x)
    first, second = pl.ds(0, rows), pl.ds(rows, rows)
    t.add((DA, X), da_own.at[first], da_far.at[first], x)
    t.add((DA, C), da_own.at[first], da_own.at[second], c)
    t.add((DA, FAR_C), da_far.at[first], da_far.at[second], c)
    for i, cut in enumerate((first, second)):
        t.add((DQKV, i), dqkv.at[cut], dqkv_far.at[cut], x)
    t.add((ATTN, C), give, got, c)
    for i, partner in enumerate((place.z(1), place.z(2), place.z(3), x)):
        t.add((MOE, i), moe_srcs[i], moe_lands[i], partner)
    if with_grads:
        t.add((GRADS, Y, 0), grad_srcs[0], first_land, y)
        t.add((GRADS, Y, 1), grad_srcs[1], grad_lands[0], y)
        t.add((GRADS, Y, 2), grad_srcs[2], grad_lands[1], y)
        t.add((GRADS, X, 0), grad_srcs[3], grad_lands[2], x)
        t.add((GRADS, X, 1), first_sum, grad_lands[3], x)
    sum_out = WholeSum(t, 0, grad_out, high_levels + low_levels, stages[0], lands[0])
    sum_here = WholeSum(t, 1, grad_here, low_levels + high_levels, stages[1], lands[1])
    sum_there = WholeSum(t, 2, grad_there, high_levels + low_levels, stages[2], lands[2])
    small_sum = SmallSum(t, 0, small, [c] + partners, small_lands)
    last_sum = SmallSum(t, 1, small_last, [c] + partners, last_lands)

    greet([x, c, place.z(3)] + partners)
    t.start((SMALL, X), (MOE, 1), (MOE, 2))
    if with_grads:
        t.start((GRADS, Y, 0))
    here, there = qkv_slices(qkv, place.col), qkv_slices(qkv, 1 - place.col)
    targets = [*qkv_targets(qkv_here, qkv), *qkv_targets(qkv_there, qkv)]
    moves(local, *zip([*here, *there], targets))

    def masks(b):
        allowed[...] = allowed_tile(seg_row[b : b + 1, :], seg_col[:, b : b + 1], True)

    def exchange_sum(i, total):
        square[i] = jnp.broadcast_to(total, (rows, LANES)).T[:8, :]
        t.start((INNER, i))

    def exchanged(i, total):
        t.arrived((INNER, i))
        return total + jnp.broadcast_to(square_far[i, :1, :], (LANES, rows)).T[:, :1]

    def norm_back(grad, value, inv, gain_row, inner):
        return inv * (grad * gain_row) - value * (inv * inv * inv * inner / (2 * part))

    grad = add_wide(*[p[...] for p in parts])
    inv = inv_second[:, :1]
    inner = jnp.sum(middle[...] * grad * gain_moe[...], 1, keepdims=True)
    exchange_sum(0, inner)
    small[...] = small_own[...]
    small[SUMMED : SUMMED + 1, :] = jnp.sum(grad * middle[...] * inv, 0, keepdims=True)
    inner = exchanged(0, inner)
    total = cot[...].astype(jnp.float32)
    total = total + norm_back(grad, middle[...], inv, gain_moe[...], inner)
    grad_middle[...] = total
    da_own[:rows, :] = low(RESIDUAL * total)
    t.start((DA, X), (DA, C))
    masks(1)
    t.arrived((SMALL, X))
    small[...] = small[...] + small_land[...]
    small_sum.send(0)
    t.arrived((DA, C))
    at_here = pl.ds(pl.multiple_of(place.col * width, LANES), width)
    at_there = pl.ds(pl.multiple_of((1 - place.col) * width, LANES), width)
    grad_out[at_here, :] = dot_tn(mixed[...], da_own[...])
    grad_out[at_there, :] = dot_tn(mixed_far[...], da_own[...])
    sum_out.send(0)
    small_sum.next(0)
    t.arrived((DA, X))
    t.start((DA, FAR_C))
    if with_grads:
        t.start((GRADS, X, 0))

    def mixed_back(cut):
        total = dot_nt(da_own[cut, :], w_out[at_here, :]) + dot_nt(da_far[cut, :], out_far[...])
        grad_mixed[cut, :] = low(total)

    mixed_back(slice(0, rows))
    t.arrived((DA, FAR_C))
    mixed_back(slice(rows, 2 * rows))
    attend = functools.partial(
        attend_back_rows, q_ref, keys, values, grad_mixed, allowed, dqkv, dk, dv, cosine, sine
    )
    attend(rows, width // LANES)
    t.start((DQKV, 1))
    sum_out.next(0)
    small_sum.next(1)
    if with_grads:
        t.arrived((GRADS, Y, 0))
        t.start((GRADS, Y, 1))
        first_sum[...] = low(keep_first[...] + first_land[...].astype(jnp.float32))
    t.start((MOE, 0))
    masks(0)
    attend(0, width // LANES)
    t.start((DQKV, 0))
    sum_out.next(1)
    grad_here[...] = dot_tn(normed[...], dqkv[...])
    sum_here.send(0)
    t.arrived((DQKV, 1))

    def tokens_back(cut):
        return dot_nt(dqkv[cut, :], qkv_here[...]) + dot_nt(dqkv_far[cut, :], qkv_there[...])

    give[...] = tokens_back(slice(rows, 2 * rows))
    t.start((ATTN, C))
    if with_grads:
        t.start((GRADS, Y, 2))
    sum_out.next(2)
    small_sum.next(2)
    t.arrived((DQKV, 0))
    t.start((MOE, 3))
    if with_grads:
        t.start((GRADS, X, 1))
    grad_there[...] = dot_tn(normed[...], dqkv_far[...])
    sum_there.send(0)
    grad = tokens_back(slice(0, rows))
    t.arrived((ATTN, C))
    grad = grad + got[...]
    got[...] = grad
    value = tokens[...].astype(jnp.float32)
    inv = inv_first[:, :1]
    inner = jnp.sum(value * grad * gain[...], 1, keepdims=True)
    exchange_sum(1, inner)
    small_last[...] = jnp.zeros_like(small_last)
    small_last[0:1, :] = jnp.sum(grad * value * inv, 0, keepdims=True)
    last_sum.send(0)
    sum_here.next(0)
    sum_out.next(3)
    inner = exchanged(1, inner)
    grad = norm_back(got[...], tokens[...].astype(jnp.float32), inv, gain[...], inner)
    grad_tokens[...] = grad_middle[...] + grad
    last_sum.next(0)
    for i in range(2 * count):
        if i + 4 < 2 * count:
            sum_out.next(i + 4)
        if i + 1 < 2 * count:
            sum_here.next(i + 1)
        sum_there.next(i)
        if i + 3 < small_lands.shape[0]:
            small_sum.next(i + 3)
        if i + 1 < last_lands.shape[0]:
            last_sum.next(i + 1)
    start = 0
    for out in (grad_q, grad_k, grad_v):
        size = out.shape[1] // 2
        cut = slice(start, start + size)
        out[:, pl.ds(pl.multiple_of(place.col * size, LANES), size)] = grad_here[:, cut]
        out[:, pl.ds(pl.multiple_of((1 - place.col) * size, LANES), size)] = grad_there[:, cut]
        start += size
    done = [key for each in (sum_out, sum_here, sum_there, small_sum, last_sum) for key in each.keys()]
    t.finish(*done)


def back(levels, qkv, moe_srcs, vmem_ins, grads):
    tokens, middle, q = vmem_ins[0], vmem_ins[2], vmem_ins[12]
    w_out, small_own = vmem_ins[22], vmem_ins[24]
    rows, part = tokens.shape
    width, kv = q.shape[1], qkv[1].shape[1] // 2
    both = width + 2 * kv
    vmem = pl.BlockSpec(memory_space=pltpu.VMEM)
    bf16, f32 = jnp.bfloat16, jnp.float32
    shape = jax.ShapeDtypeStruct
    like = lambda a: shape(a.shape, a.dtype)
    hbm_outs = [like(a) for a in moe_srcs]
    extra_ins, extra_specs, extra_scratch = [], [], []
    if grads:
        extra_ins = list(grads)
        extra_specs = [ANY] * 4 + [vmem]
        hbm_outs += [like(a) for a in grads[:4]]
        extra_scratch = [pltpu.VMEM(grads[0].shape, bf16)] * 2
    small_last = shape((8, part), f32)
    vmem_outs = [shape((rows, part), f32)]
    vmem_outs += [shape((part, w.shape[1]), f32) for w in qkv]
    vmem_outs += [shape(w_out.shape, f32), like(small_own), small_last]
    twice = lambda w, dtype=bf16: pltpu.VMEM((2 * rows, w), dtype)
    wide = pltpu.VMEM((rows, part), f32)
    pair = pltpu.VMEM((2, rows, LANES), f32)
    flat = pltpu.VMEM((2, 8, rows), f32)
    scratch = [pltpu.VMEM((part, both), bf16)] * 2
    scratch += [twice(part), twice(part), twice(width), twice(both), twice(both), wide, wide]
    scratch += [wide, pltpu.VMEM((part, both), f32), pltpu.VMEM((part, both), f32)]
    scratch += [pltpu.VMEM((rows, rows), f32), pair, pair, flat, flat]
    scratch += [pltpu.VMEM(small_own.shape, f32)]
    scratch += [pltpu.VMEM((levels + 1, *small_own.shape), f32)]
    scratch += [pltpu.VMEM((levels + 1, 8, part), f32)]
    for high, wide_cols in ((w_out.shape[0], part), (part, both), (part, both)):
        sizes = [pltpu.VMEM((high >> (i + 1), wide_cols), bf16) for i in range(levels)]
        scratch += sizes * 3
    scratch += extra_scratch
    count = 9 + 4 + 5 + 3 * 2 * levels + 2 * (levels + 1)
    scratch += [pltpu.SemaphoreType.DMA((2, count)), pltpu.SemaphoreType.DMA((6,))]
    return pl.pallas_call(
        functools.partial(back_kernel, levels, bool(grads)),
        out_shape=hbm_outs + vmem_outs,
        in_specs=[ANY] * (len(qkv) + len(moe_srcs)) + [vmem] * len(vmem_ins) + extra_specs,
        out_specs=[ANY] * len(hbm_outs) + [vmem] * len(vmem_outs),
        scratch_shapes=scratch,
        compiler_params=pltpu.CompilerParams(
            collective_id=4, has_side_effects=True, vmem_limit_bytes=62 * 1024 * 1024
        ),
        name="back",
    )(*qkv, *moe_srcs, *vmem_ins, *extra_ins)


def halve(value, index, mask, axis):
    first, last = jnp.split(value, 2, axis)
    upper = (index & mask) != 0
    send = low(jnp.where(upper, first, last))
    return jnp.where(upper, last, first) + flip(send, "dp", mask).astype(jnp.float32)


def on_device(
    tokens,
    gain_attn,
    w_query,
    key_matrix,
    value_matrix,
    w_out,
    gain_moe,
    w_router,
    w_gate,
    w_up,
    w_down,
    segments,
    routes,
    cotangent,
):
    col = lax.axis_index("col")
    core = lax.axis_index("expert")
    group = lax.axis_index("dp")
    dp_size = lax.axis_size("dp")
    step = dp_size // ZPARTS
    member = group % step
    levels = dp_size.bit_length() - 1
    half_mask = step // 2
    side = (member // half_mask) % 2

    local, part, ffn = w_gate.shape
    split = local // 4
    units = ffn // ZPARTS
    experts = local * lax.axis_size("expert")
    rows = tokens.shape[0]
    width = w_query.shape[1] // 2

    router_own = jnp.pad(w_router, ((0, 0), (0, LANES - experts)))
    seg_rows = jnp.where(core == 0, segments, segments[::-1])
    positions = jax.vmap(doc_positions)(seg_rows).reshape(-1, 1).astype(jnp.float32)
    half = HEAD_WIDTH // 2
    slot = jnp.arange(LANES, dtype=jnp.int32)
    freq = jnp.exp((slot % half).astype(jnp.float32) * (-2.0 * math.log(THETA) / HEAD_WIDTH))
    sign = jnp.where(slot % HEAD_WIDTH < half, -1.0, 1.0)
    cosine, sine = jnp.cos(positions * freq), jnp.sin(positions * freq) * sign
    qkv = [w_query, key_matrix, value_matrix]
    gain, gain_second = gain_attn[None], gain_moe[None]
    (
        down_got,
        down_other,
        gate_got,
        gate_other,
        up_got,
        up_other,
        router_far,
        c_own,
        c_far,
        route_all,
        grad_hidden,
        q,
        keys,
        values,
        mixed,
        mixed_far,
        normed,
        inv_first,
        middle,
        inv_second,
        h2,
    ) = front(
        tokens,
        cotangent,
        w_down,
        w_gate,
        w_up,
        router_own,
        routes.T,
        qkv,
        gain,
        gain_second,
        w_out,
        cosine,
        sine,
        seg_rows,
        seg_rows.T,
    )
    route_rows = jnp.swapaxes(route_all, 2, 3).reshape(2 * ZPARTS * rows, -1)
    (
        h_own,
        h_far,
        moe_own,
        moe_far,
        hidden,
        slopes,
        dlog,
        s0_own,
        s0_far,
        z1_own,
        z1_far,
        piece2,
        s3_own,
        s3_far,
    ) = moe_layer(
        route_rows,
        grad_hidden,
        [router_own, router_far],
        h2,
        [w_gate, w_up, w_down, gate_got, gate_other, up_got, up_other, down_got, down_other],
    )
    resident = [h_own, h_far, c_own, c_far]
    out_there = lax.dynamic_slice_in_dim(w_out, (1 - col) * width, width, 0)
    moe_own, moe_far = (a.reshape(ZPARTS, 2, rows, part) for a in (moe_own, moe_far))
    cargo = [
        ((Z, 2), piece2),
        (X, s3_far),
        (X, low(add_wide(s0_far, z1_far))),
        (X, out_there),
        (C, moe_own[:, 1]),
        (C, moe_far[:, 1]),
    ]
    *first_part, z2_piece, x3_far, x0_far, out_far, sib_own, sib_far = weight_grads(
        0, 0, split, resident, hidden, slopes, cargo
    )
    moe_own = low(add_wide(moe_own[:, 0], sib_own))
    moe_far = low(add_wide(moe_far[:, 0], sib_far))
    cargo = [
        ((Z, 3), low(add_wide(s3_own, x3_far))),
        (Y, first_part[3]),
        (X, moe_far[2:]),
        ((Z, 1), moe_far[1]),
    ]
    *second_part, z3_piece, y_far, moe_x, moe_z1_far = weight_grads(
        1, split, split, resident, hidden, slopes, cargo
    )
    moe_srcs = [
        moe_own[1],
        low(add_wide(moe_own[2], moe_x[0])),
        low(add_wide(moe_own[3], moe_x[1])),
        low(add_wide(moe_far[0], moe_z1_far)),
    ]

    def router_term(h_rows):
        total = dot_tn(dlog, h_rows.reshape(-1, part))
        total = total[:experts] + total[LANES : LANES + experts]
        return jnp.pad(total, ((0, 8), (0, 0)))

    vmem_ins = [
        tokens,
        cotangent,
        middle,
        inv_first,
        inv_second,
        gain,
        gain_second,
        s0_own,
        z1_own,
        z2_piece,
        x0_far,
        z3_piece,
        q,
        keys,
        values,
        mixed,
        mixed_far,
        normed,
        cosine,
        sine,
        seg_rows,
        seg_rows.T,
        w_out,
        out_far,
        router_term(h_own),
        router_term(h_far),
    ]
    swap = lambda a: flip(a, "dp", half_mask)
    plain = half_mask == 1
    grads = []
    if plain:
        second_far = low(add_wide(second_part[1], y_far))
        grads = [second_part[3], first_part[2], second_part[2], second_far, first_part[1]]
    outs = back(levels, qkv, moe_srcs, vmem_ins, grads)
    moe_parts, outs = outs[:4], outs[4:]
    if plain:
        (got_second, got_first, far_second, far_first), outs = outs[:4], outs[4:]
        own_first, own_second = add_wide(first_part[0], got_first), add_wide(
            second_part[0], got_second
        )
    else:

        def finish_grads(kept, got_own, got_far):
            shape = (split, 3, units // 2, part)
            keep_own = add_wide(kept[0], got_own).reshape(shape)
            keep_far = add_wide(kept[1], got_far).reshape(shape)
            mask = half_mask // 2
            while mask:
                keep_own = halve(keep_own, member, mask, 2)
                keep_far = halve(keep_far, member, mask, 2)
                mask //= 2
            return keep_own, flip(low(keep_far), "col")

        own_second, far_second = finish_grads(second_part, swap(first_part[2]), y_far)
        own_first, far_first = finish_grads(
            first_part, swap(second_part[2]), swap(second_part[3])
        )
    grad_tokens, grad_query, grad_key, grad_value, grad_out, small, small_last = outs

    def in_order(a, b, index):
        a, b = a.astype(jnp.float32), b.astype(jnp.float32)
        return jnp.concatenate([jnp.where(index == 0, a, b), jnp.where(index == 0, b, a)], 0)

    expert_grads = in_order(
        in_order(own_first, own_second, side), in_order(far_first, far_second, side), col
    )
    expert_grads = expert_grads.reshape(local, 3, -1, part)
    output = middle + RESIDUAL * add_wide(moe_own[0], *moe_parts)
    return (
        output,
        grad_tokens,
        small_last[0],
        grad_query,
        grad_key,
        grad_value,
        grad_out,
        small[SUMMED],
        small[:experts].T,
        jnp.swapaxes(expert_grads[:, 0], 1, 2),
        jnp.swapaxes(expert_grads[:, 1], 1, 2),
        expert_grads[:, 2],
    )


def solution(mesh):
    in_specs = (
        P(("dp", "expert"), "col"),
        P("col"),
        P("col", "expert"),
        P("col", "expert"),
        P("col", "expert"),
        P("expert", "col"),
        P("col"),
        P("col", None),
        P("expert", "col", None),
        P("expert", "col", None),
        P("expert", None, "col"),
        P("dp", None),
        P(("dp", "expert"), None),
        P(("dp", "expert"), "col"),
    )
    out_specs = (
        P(("dp", "expert"), "col"),
        P(("dp", "expert"), "col"),
        P("col"),
        P("col", "expert"),
        P("col", "expert"),
        P("col", "expert"),
        P("expert", "col"),
        P("col"),
        P("col", None),
        P("expert", "col", "dp"),
        P("expert", "col", "dp"),
        P("expert", "dp", "col"),
    )
    return jax.shard_map(
        on_device, mesh=mesh, in_specs=in_specs, out_specs=out_specs, check_vma=False
    )
```

```python
import functools
import math

import jax
import jax.numpy as jnp
from jax import lax
from jax.experimental import pallas as pl
from jax.experimental.pallas import tpu as pltpu
from jax.sharding import PartitionSpec as P

HEAD_WIDTH = 64
(
    COT,
    TOK,
    DOWN,
    QKV,
    GATE,
    UP,
    ROUTER,
    GAIN,
    ROUTES,
    MIXED,
    ATTN,
    SQUARE,
    H,
    BACK,
    DA,
    DQKV,
    INNER,
    GRADS,
    MOE,
    SMALL,
    SUM,
    OUT,
) = range(22)
X, C, Y, Z, FAR_X, FAR_C, FAR_Z = range(7)
ZPARTS = 4
LANES = 128


EPS = 1e-06
RESIDUAL = 0.22
SCORE_SCALE = 0.015625
THETA = 10000.0
NEG = -1000000000.0


def doc_positions(seg_row):
    length_total = seg_row.shape[0]
    index = jnp.arange(length_total, dtype=jnp.int32)
    before = jnp.concatenate([jnp.full((1,), -1, jnp.int32), seg_row[:-1]])
    starts = jnp.where(seg_row != before, index, 0)
    return index - lax.cummax(starts, axis=0)


def flip(value, axis, mask=1):
    size = lax.axis_size(axis)
    return lax.ppermute(value, axis, [(i, i ^ mask) for i in range(size)])


def dot_nn(a, b):
    return jnp.dot(a, b, preferred_element_type=jnp.float32)


def dot_nt(a, b):
    return lax.dot_general(a, b, (((1,), (1,)), ((), ())), preferred_element_type=jnp.float32)


def dot_tn(a, b):
    return lax.dot_general(a, b, (((0,), (0,)), ((), ())), preferred_element_type=jnp.float32)


def add_wide(*parts):
    return sum(p.astype(jnp.float32) for p in parts)


def low(value):
    return value.astype(jnp.bfloat16)


class Place:
    def __init__(self):
        self.col = lax.axis_index("col")
        self.core = lax.axis_index("expert")
        group = lax.axis_index("dp")
        self.step = lax.axis_size("dp") // ZPARTS
        self.zed, self.member = group // self.step, group % self.step
        self.half = self.step // 2
        self.side = (self.member // self.half) % 2

    def x(self):
        return {"col": 1 - self.col}

    def c(self):
        return {"expert": 1 - self.core}

    def y(self):
        return {"dp": self.zed * self.step + self.member + self.half * (1 - 2 * self.side)}

    def z(self, k):
        zed = self.zed
        other = (zed + 1 - 2 * (zed % 2), (zed + 2) % ZPARTS, ZPARTS - 1 - zed)[k - 1]
        return {"dp": other * self.step + self.member}

    def bits(self):
        levels = []
        mask = self.half
        while mask:
            bit = (self.member // mask) % 2
            partner = self.zed * self.step + self.member + mask * (1 - 2 * bit)
            levels.append(({"dp": partner}, bit))
            mask //= 2
        return levels, [(self.z(1), self.zed % 2), (self.z(2), self.zed // 2)]


def greet(partners):
    barrier = pltpu.get_barrier_semaphore()
    for partner in partners:
        pl.semaphore_signal(
            barrier, inc=1, device_id=partner, device_id_type=pl.DeviceIdType.MESH
        )
    pl.semaphore_wait(barrier, len(partners))


class Transfers:
    def __init__(self, sems):
        self.sems, self.table, self.waited = sems, {}, set()

    def add(self, key, src, dst, partner):
        self.table[key] = (len(self.table), src, dst, partner)

    def copy(self, key):
        i, src, dst, partner = self.table[key]
        return pltpu.make_async_remote_copy(
            src_ref=src,
            dst_ref=dst,
            send_sem=self.sems.at[0, i],
            recv_sem=self.sems.at[1, i],
            device_id=partner,
            device_id_type=pl.DeviceIdType.MESH,
        )

    def start(self, *keys):
        for key in keys:
            self.copy(key).start()

    def arrived(self, *keys):
        for key in keys:
            self.waited.add(key)
            self.copy(key).wait_recv()

    def sent(self, *keys):
        for key in keys:
            self.copy(key).wait_send()

    def finish(self, *sent):
        for key in self.table:
            if key not in sent:
                self.copy(key).wait_send()
        for key in self.table:
            if key not in self.waited:
                self.copy(key).wait_recv()


def moves(sems, *pairs):
    copies = [pltpu.make_async_copy(src, dst, sems.at[i]) for i, (src, dst) in enumerate(pairs)]
    for copy in copies:
        copy.start()
    for copy in copies:
        copy.wait()


ANY = pl.BlockSpec(memory_space=pl.ANY)


def like_of(a):
    return jax.ShapeDtypeStruct(a.shape, a.dtype)


def whole_block(a):
    return pl.BlockSpec(a.shape, lambda *_: (0,) * a.ndim, pipeline_mode=pl.Buffered(1))


def turn(block, cosine, sine):
    lane = lax.broadcasted_iota(jnp.int32, block.shape, 1) % HEAD_WIDTH
    ahead = pltpu.roll(block, LANES - HEAD_WIDTH // 2, 1)
    behind = pltpu.roll(block, HEAD_WIDTH // 2, 1)
    return block * cosine + jnp.where(lane < HEAD_WIDTH // 2, ahead, behind) * sine


def score_tiles(rows):
    half = rows // 2
    return ((0, half, half), (half, rows, rows))


def allowed_tile(seg_row, seg_col, across_keys):
    shape = (seg_col.shape[0], seg_row.shape[1])
    down, along = (lax.broadcasted_iota(jnp.int32, shape, axis) for axis in (0, 1))
    order = down <= along if across_keys else along <= down
    return jnp.where((seg_row == seg_col) & order, 1.0, 0.0)


def swap_heads(value):
    return pltpu.roll(value.astype(jnp.float32), HEAD_WIDTH, 1).astype(value.dtype)


def attend_rows(q_ref, keys_ref, values_ref, allowed_ref, out_ref, base, blocks):
    rows = allowed_ref.shape[0]
    group = blocks

    def body(j, carry):
        cols = pl.ds(pl.multiple_of(j * LANES, LANES), LANES)
        for start, stop, keys in score_tiles(rows):
            lane = lax.broadcasted_iota(jnp.int32, (stop - start, LANES), 1)
            query = q_ref[base + start : base + stop, cols]
            allowed = allowed_ref[start:stop, :keys] > 0
            outs = []
            for side, part in enumerate((lane < HEAD_WIDTH, lane >= HEAD_WIDTH)):
                other = (2 * j + side) // group
                other = other + side - 2 * other * side
                key_rows = keys_ref[other, base : base + keys, :]
                scores = dot_nt(jnp.where(part, query, jnp.zeros_like(query)), key_rows)
                scores = jnp.where(allowed, scores * SCORE_SCALE, NEG)
                expo = jnp.exp(scores - jnp.max(scores, axis=1, keepdims=True))
                probs = expo * (1.0 / jnp.sum(expo, axis=1, keepdims=True))
                outs.append(dot_nn(low(probs), values_ref[other, base : base + keys, :]))
            mixed = jnp.where(lane < HEAD_WIDTH, outs[0], outs[1])
            out_ref[base + start : base + stop, cols] = low(mixed)
        return carry

    lax.fori_loop(0, blocks, body, 0)


def weight_slice(ref, which, half, split, zed, wide):
    first = (2 * which + half) * split
    units = pl.ds(pl.multiple_of(zed * LANES, LANES), LANES)
    if wide:
        return ref.at[pl.ds(first, split), units, :]
    return ref.at[pl.ds(first, split), :, units]


def qkv_slices(refs, which):
    widths = [ref.shape[1] // 2 for ref in refs]
    return [
        ref.at[:, pl.ds(pl.multiple_of(which * w, LANES), w)] for ref, w in zip(refs, widths)
    ]


def qkv_targets(target, refs):
    widths = [ref.shape[1] // 2 for ref in refs]
    starts = [sum(widths[:i]) for i in range(len(widths))]
    return [target.at[:, pl.ds(start, w)] for start, w in zip(starts, widths)]


def front_kernel(*refs):
    tokens, cot, w_down, w_gate, w_up, router, routes = refs[:7]
    qkv = refs[7:10]
    gain, gain_moe, w_out, cosine, sine, seg_row, seg_col = refs[10:17]
    (
        down_got,
        down_other,
        gate_got,
        gate_other,
        up_got,
        router_far,
        c_own,
        c_far,
        route_all,
        grad_hidden,
        q_ref,
        keys,
        values,
        mixed,
        mixed_far,
        normed,
        normed_far,
        inv_first,
        middle_ref,
        inv_second,
        h2_ref,
    ) = refs[17:38]
    tok, qkv_here, qkv_far, gain_far, give, got, square, square_far = refs[38:46]
    own_buf, far_buf, down_own, down_buf, grad_buf, allowed, sems, local = refs[46:]
    place = Place()
    t = Transfers(sems)
    x, c, y = place.x(), place.c(), place.y()
    z = [None] + [place.z(k) for k in range(1, ZPARTS)]
    rows, part = tokens.shape
    ks = range(1, ZPARTS)
    t.add((TOK, X), tokens, tok.at[0], x)
    t.add((TOK, C), tokens, tok.at[1], c)
    t.add((TOK, FAR_C), tok.at[0], tok.at[2], c)
    there = qkv_slices(qkv, 1 - place.col)
    mine = pl.ds(pl.multiple_of(place.side * (part // 2), part // 2), part // 2)
    for i, target in enumerate(qkv_targets(qkv_far, qkv)):
        t.add((QKV, X, i), there[i].at[mine], target.at[mine], x)
        t.add((QKV, Y, i), target.at[mine], target.at[mine], y)
    t.add((GAIN, X), gain, gain_far, x)
    t.add((ROUTER, X), router, router_far, x)
    t.add((COT, X), cot, c_far.at[0, 0], x)
    t.add((COT, C, 0), cot, c_own.at[0, 1], c)
    t.add((COT, FAR_C, 0), c_far.at[0, 0], c_far.at[0, 1], c)
    t.add((ROUTES, C, 0), routes, route_all.at[0, 1], c)
    for k in ks:
        t.add((COT, Z, k), cot, c_own.at[k, 0], z[k])
        t.add((COT, FAR_Z, k), c_far.at[0, 0], c_far.at[k, 0], z[k])
        t.add((COT, C, k), c_own.at[k, 0], c_own.at[k, 1], c)
        t.add((COT, FAR_C, k), c_far.at[k, 0], c_far.at[k, 1], c)
        t.add((ROUTES, Z, k), routes, route_all.at[k, 0], z[k])
        t.add((ROUTES, C, k), route_all.at[k, 0], route_all.at[k, 1], c)
    split = down_got.shape[0]
    for key, ref, land, other in (
        (DOWN, w_down, down_got, down_other),
        (GATE, w_gate, gate_got, gate_other),
        (UP, w_up, up_got, None),
    ):
        src = weight_slice(ref, 1 - place.col, place.side, split, place.zed, key == DOWN)
        t.add((key, X), src, land, x)
        if key != UP:
            t.add((key, Y), land, other, y)
    for i in range(2):
        cut = pl.ds(rows * i, rows)
        t.add((MIXED, X, i), mixed.at[cut], mixed_far.at[cut], x)
    t.add((ATTN, C), give, got, c)
    t.add((SQUARE, X), square, square_far, x)

    greet([x, c, y, *z[1:]])
    t.start((TOK, X), (GAIN, X), *[(QKV, X, i) for i in range(3)])
    t.start((TOK, C), (COT, C, 0), (ROUTES, C, 0), *[(ROUTES, Z, k) for k in ks])
    t.start((COT, Z, 1), (COT, Z, 2), (COT, Z, 3))
    own_cut = functools.partial(weight_slice, w_down, place.col, split=split, zed=place.zed)
    moves(
        local,
        (cot, c_own.at[0, 0]),
        (routes, route_all.at[0, 0]),
        (own_cut(half=place.side, wide=True), down_own.at[pl.ds(0, split)]),
        (own_cut(half=1 - place.side, wide=True), down_own.at[pl.ds(split, split)]),
        *zip(qkv_slices(qkv, place.col), qkv_targets(qkv_here, qkv)),
    )

    def norm(own, far, base):
        own, far = own.astype(jnp.float32), far.astype(jnp.float32)
        total = jnp.sum(own * own, 1, keepdims=True) + jnp.sum(far * far, 1, keepdims=True)
        inv = lax.rsqrt(total / (2 * part) + EPS)
        normed[base : base + rows, :] = (own * inv * gain[...]).astype(jnp.bfloat16)
        normed_far[base : base + rows, :] = (far * inv * gain_far[...]).astype(jnp.bfloat16)
        return inv

    def masks(b):
        allowed[...] = allowed_tile(seg_row[b : b + 1, :], seg_col[:, b : b + 1], False)

    masks(1)
    t.arrived(*[(QKV, X, i) for i in range(3)])
    t.start(*[(QKV, Y, i) for i in range(3)])
    t.arrived((TOK, X), (GAIN, X))
    t.start((TOK, FAR_C), (COT, X), (ROUTER, X))
    inv = norm(tokens[...], tok[0], 0)
    inv_first[...] = jnp.broadcast_to(inv, inv_first.shape)
    t.arrived((TOK, C), (TOK, FAR_C))
    norm(tok[1], tok[2], rows)
    for k in ks:
        t.arrived((ROUTES, Z, k))
        t.start((ROUTES, C, k))
    t.arrived((COT, Z, 1))
    t.start((COT, C, 1))
    t.arrived(*[(QKV, Y, i) for i in range(3)])
    t.start((DOWN, X))

    width = q_ref.shape[1]
    for base in (rows, 0):
        cut = slice(base, base + rows)
        qkv_rows = dot_nn(normed[cut, :], qkv_here[...])
        qkv_rows = qkv_rows + dot_nn(normed_far[cut, :], qkv_far[...])
        for i in range(width // LANES + 1):
            block = qkv_rows[:, LANES * i : LANES * (i + 1)]
            block = turn(block, cosine[cut, :], sine[cut, :])
            if i < width // LANES:
                q_ref[cut, LANES * i : LANES * (i + 1)] = low(block)
            else:
                keys[0, cut, :] = low(block)
                keys[1, cut, :] = swap_heads(low(block))
        block = low(qkv_rows[:, width + LANES :])
        values[0, cut, :] = block
        values[1, cut, :] = swap_heads(block)
    attend_rows(q_ref, keys, values, allowed, mixed, rows, width // LANES)
    t.start((MIXED, X, 1))
    t.arrived((COT, X))
    t.start((COT, FAR_C, 0), (COT, FAR_Z, 1), (COT, FAR_Z, 2))
    masks(0)
    attend_rows(q_ref, keys, values, allowed, mixed, 0, width // LANES)
    t.start((MIXED, X, 0))
    t.start((GATE, X), (COT, FAR_Z, 3))
    t.arrived((COT, Z, 2))
    t.start((COT, C, 2))
    t.arrived((DOWN, X))
    t.start((DOWN, Y), (UP, X))

    def project(base):
        cut = slice(base, base + rows)
        first = pl.ds(pl.multiple_of(place.col * width, LANES), width)
        second = pl.ds(pl.multiple_of((1 - place.col) * width, LANES), width)
        return dot_nn(mixed[cut, :], w_out[first, :]) + dot_nn(mixed_far[cut, :], w_out[second, :])

    def stored(i):
        out = grad_hidden.at[pl.ds(rows * i, rows)]
        return pltpu.make_async_copy(grad_buf.at[i % 2], out, local.at[8 + i % 2])

    def hidden_grads(i):
        k, p = i // 2, i % 2
        if p == 1:
            t.arrived((COT, C, k), (COT, FAR_C, k))
        moves(local, (c_own.at[k, p], own_buf), (c_far.at[k, p], far_buf))
        if i > 1:
            stored(i - 2).wait()
        size = split * LANES
        for n in range(2):
            own_rows = down_own[split * n : split * (n + 1)].reshape(size, part)
            far_rows = down_buf[n].reshape(size, part)
            total = dot_nt(own_buf[...], own_rows) + dot_nt(far_buf[...], far_rows)
            grad_buf[i % 2, :, size * n : size * (n + 1)] = low(RESIDUAL * total)
        stored(i).start()

    t.arrived((MIXED, X, 1))
    give[...] = project(rows)
    t.start((ATTN, C))
    t.arrived((MIXED, X, 0))
    attn = project(0)
    t.arrived((ATTN, C))
    middle = tokens[...].astype(jnp.float32) + RESIDUAL * (attn + got[...])
    middle_ref[...] = middle
    total = jnp.sum(middle * middle, 1, keepdims=True)
    square[...] = jnp.broadcast_to(total, (rows, LANES)).T[:8, :]
    t.start((SQUARE, X))
    t.arrived((DOWN, Y))
    moves(local, (down_got, down_buf.at[0]), (down_other, down_buf.at[1]))
    t.arrived((SQUARE, X))
    total = total + jnp.broadcast_to(square_far[:1, :], (LANES, rows)).T[:, :1]
    inv = lax.rsqrt(total / (2 * part) + EPS)
    inv_second[...] = jnp.broadcast_to(inv, inv_second.shape)
    h2_ref[...] = low(middle_ref[...] * inv * gain_moe[...])

    hidden_grads(0)
    hidden_grads(1)
    t.arrived((COT, FAR_Z, 1))
    t.start((COT, FAR_C, 1))
    hidden_grads(2)
    t.arrived((GATE, X))
    t.start((GATE, Y))
    hidden_grads(3)
    t.arrived((COT, FAR_Z, 2))
    t.start((COT, FAR_C, 2))
    t.arrived((COT, Z, 3))
    t.start((COT, C, 3))
    hidden_grads(4)
    hidden_grads(5)
    t.arrived((COT, FAR_Z, 3))
    t.start((COT, FAR_C, 3))
    hidden_grads(6)
    hidden_grads(7)
    stored(6).wait()
    stored(7).wait()
    t.finish()


def front(tokens, cot, w_down, w_gate, w_up, router, routes, qkv, *others):
    rows, part = tokens.shape
    gain, w_out = others[0], others[2]
    vmem = pl.BlockSpec(memory_space=pltpu.VMEM)
    shape = lambda dims, dtype=jnp.bfloat16: jax.ShapeDtypeStruct(dims, dtype)
    like = lambda a: shape(a.shape, a.dtype)
    stack = lambda a: shape((ZPARTS, 2, *a.shape), a.dtype)
    mine = w_down.shape[0] // 2
    width, kv = qkv[0].shape[1] // 2, qkv[1].shape[1] // 2
    down, pair = shape((mine // 2, LANES, part)), shape((mine // 2, part, LANES))
    hbm_outs = [down, down, pair, pair, pair, like(router)]
    hbm_outs += [stack(cot), stack(cot), stack(routes)]
    hbm_outs += [shape((2 * ZPARTS * rows, mine * LANES))]
    vmem_outs = [
        shape((2 * rows, width)),
        shape((2, 2 * rows, kv)),
        shape((2, 2 * rows, kv)),
        shape((2 * rows, width)),
        shape((2 * rows, width)),
        shape((2 * rows, part)),
        shape((2 * rows, part)),
        shape((rows, LANES), jnp.float32),
        shape((rows, part), jnp.float32),
        shape((rows, LANES), jnp.float32),
        shape((rows, part)),
    ]
    buffer = pltpu.VMEM((rows, part), jnp.bfloat16)
    wide = pltpu.VMEM((rows, part), jnp.float32)
    small = pltpu.VMEM((8, rows), jnp.float32)
    weights = pltpu.VMEM((part, width + 2 * kv), jnp.bfloat16)
    count = 15 + 6 * (ZPARTS - 1) + 5 + 2 + 2
    return pl.pallas_call(
        front_kernel,
        out_shape=hbm_outs + vmem_outs,
        in_specs=[vmem] + [ANY] * 9 + [vmem] * len(others),
        out_specs=[ANY] * len(hbm_outs) + [vmem] * len(vmem_outs),
        scratch_shapes=[
            pltpu.VMEM((3, rows, part), jnp.bfloat16),
            weights,
            weights,
            pltpu.VMEM(gain.shape, jnp.float32),
            wide,
            wide,
            small,
            small,
            buffer,
            buffer,
            pltpu.VMEM((mine, LANES, part), jnp.bfloat16),
            pltpu.VMEM((2, mine // 2, LANES, part), jnp.bfloat16),
            pltpu.VMEM((2, rows, mine * LANES), jnp.bfloat16),
            pltpu.VMEM((rows, rows), jnp.float32),
            pltpu.SemaphoreType.DMA((2, count)),
            pltpu.SemaphoreType.DMA((10,)),
        ],
        compiler_params=pltpu.CompilerParams(
            collective_id=0, has_side_effects=True, vmem_limit_bytes=58 * 1024 * 1024
        ),
        name="front",
    )(tokens, cot, w_down, w_gate, w_up, router, routes, *qkv, *others)


def moe_kernel(*refs):
    routes_ref, grad_ref, router_own, router_far, h2 = refs[:5]
    w_gate, w_up, w_down, w_out, gate_got, gate_other, up_got, down_got, down_other = refs[5:14]
    (
        h_own_out,
        h_far_out,
        moe_own,
        moe_far,
        hidden_out,
        slopes_out,
        dlog_ref,
        up_other,
        out_far,
        s0_own,
        z1_own,
        x0_far,
        piece2,
        s3_own,
        s3_far,
    ) = refs[14:29]
    h_own_all, h_far_all, keep_own, keep_far, give_own, give_far, got_own, got_far = refs[29:37]
    got_x, z1_far, pair_own, pair_far, down_own, down_far, hidden_ref, slopes_ref = refs[37:45]
    sems, local, fill, save = refs[45:]
    experts = down_own.shape[0]
    split = experts // 2
    rows, part = h2.shape
    place = Place()
    step = pl.program_id(0)
    t = Transfers(sems)
    x, c = place.x(), place.c()
    z = [None] + [place.z(k) for k in range(1, ZPARTS)]
    t.add((H, X), h2, h_far_all.at[0, 0], x)
    t.add((H, C, 0), h2, h_own_all.at[0, 1], c)
    t.add((H, FAR_C, 0), h_far_all.at[0, 0], h_far_all.at[0, 1], c)
    for k in range(1, ZPARTS):
        t.add((H, Z, k), h2, h_own_all.at[k, 0], z[k])
        if k == 1:
            t.add((H, FAR_X, 1), h_far_all.at[0, 0], h_far_all.at[1, 0], z[1])
        else:
            t.add((H, FAR_X, k), h_own_all.at[k, 0], h_far_all.at[k, 0], x)
        t.add((H, C, k), h_own_all.at[k, 0], h_own_all.at[k, 1], c)
        t.add((H, FAR_C, k), h_far_all.at[k, 0], h_far_all.at[k, 1], c)
    for k in range(ZPARTS):
        t.add((BACK, C, k), give_own, got_own.at[k], c)
        t.add((BACK, FAR_C, k), give_far, got_far.at[k], c)
    t.add((BACK, Z), got_own.at[1], z1_own, z[1])
    t.add((BACK, FAR_Z), got_far.at[1], z1_far, z[1])
    t.add((BACK, FAR_X), got_far.at[2], got_x, x)
    t.add((BACK, X), got_far.at[0], x0_far, x)
    t.add((UP, Y), up_got, up_other, place.y())
    width = out_far.shape[0]
    there = pl.ds(pl.multiple_of((1 - place.col) * width, LANES), width)
    t.add((OUT, X), w_out.at[there], out_far, x)

    def join(k):
        for name in ((BACK, C, k), (BACK, FAR_C, k)):
            t.copy(name).wait_send()
        t.arrived((BACK, C, k), (BACK, FAR_C, k))
        for got, keep in ((got_own, keep_own), (got_far, keep_far)):
            total = got[k].astype(jnp.float32) + keep[...].astype(jnp.float32)
            got[k] = total.astype(jnp.bfloat16)

    @pl.when(step == 0)
    def _():
        greet([x, c, place.y(), *z[1:]])
        t.start((H, X), (H, C, 0), (UP, Y), (H, Z, 1), (H, Z, 2))
        cut = functools.partial(weight_slice, which=place.col, split=split, zed=place.zed)
        fills, late = [], []
        for i, half in enumerate((place.side, 1 - place.side)):
            gates = (cut(w_gate, half=half, wide=False), (gate_got, gate_other)[i])
            ups = (cut(w_up, half=half, wide=False), (up_got, up_other)[i])
            downs = (cut(w_down, half=half, wide=True), (down_got, down_other)[i])
            for n, (pair, down) in enumerate(((pair_own, down_own), (pair_far, down_far))):
                for e in range(split):
                    for m, src in enumerate((gates[n], ups[n])):
                        cols = pl.ds(LANES * (2 * e + m), LANES)
                        into = late if src is up_other else fills
                        into.append((src.at[e], pair.at[i, :, cols]))
                fills.append((downs[n], down.at[pl.ds(split * i, split)]))
        moves(fill, (h2, h_own_all.at[0, 0]), *fills)
        t.arrived((H, X))
        t.start((H, FAR_C, 0), (H, FAR_X, 1))
        t.arrived((UP, Y))
        moves(fill, *late)

    @pl.when(step == 1)
    def _():
        t.arrived((H, C, 0), (H, FAR_C, 0), (H, Z, 1))
        t.start((H, C, 1), (OUT, X))

    @pl.when(step == 2)
    def _():
        t.start((H, Z, 3))
        t.arrived((H, FAR_X, 1))
        t.start((H, FAR_C, 1))
        join(0)
        t.arrived((H, Z, 2))
        t.start((H, FAR_X, 2), (H, C, 2))

    @pl.when(step == 3)
    def _():
        t.arrived((H, C, 1), (H, FAR_C, 1))

    @pl.when(step == 4)
    def _():
        join(1)
        t.start((BACK, Z), (BACK, FAR_Z))
        t.arrived((H, FAR_X, 2))
        t.start((H, FAR_C, 2))
        t.arrived((H, Z, 3))
        t.start((H, FAR_X, 3), (H, C, 3))

    @pl.when(step == 5)
    def _():
        t.arrived((H, C, 2), (H, FAR_C, 2))

    @pl.when(step == 6)
    def _():
        join(2)
        t.start((BACK, FAR_X))
        t.arrived((H, FAR_X, 3))
        t.start((H, FAR_C, 3))

    @pl.when(step == 7)
    def _():
        t.arrived((H, C, 3), (H, FAR_C, 3))
        t.arrived((BACK, FAR_X))
        got_own[2] = low(add_wide(got_own[2], got_x[...]))
        t.arrived((BACK, FAR_Z))
        got_far[0] = low(add_wide(got_far[0], z1_far[...]))
        t.start((BACK, X))

    def saved(i):
        k, p = i // 2, i % 2
        pairs = ((h_own_all, h_own_out), (h_far_all, h_far_out))
        return [
            pltpu.make_async_copy(src.at[k, p], dst.at[k, p], save.at[n, i])
            for n, (src, dst) in enumerate(pairs)
        ]

    def written(i):
        cut = pl.ds(rows * i, rows)
        return [
            pltpu.make_async_copy(src, dst.at[cut], save.at[2 + n, i])
            for n, (src, dst) in enumerate(((hidden_ref, hidden_out), (slopes_ref, slopes_out)))
        ]

    for i in range(2 * ZPARTS):

        @pl.when(step == i)
        def _():
            for copy in saved(i):
                copy.start()
            if i > 0:
                for copy in written(i - 1):
                    copy.wait()

    h_own, h_far = h_own_all.at[step // 2, step % 2], h_far_all.at[step // 2, step % 2]

    first = (place.core * 2 + place.col) * experts
    lane = lax.broadcasted_iota(jnp.int32, (rows, LANES), 1)
    chosen = lane == routes_ref[:, 0:1]
    for k in range(1, routes_ref.shape[1]):
        chosen = chosen | (lane == routes_ref[:, k : k + 1])
    logits = dot_nn(h_own[...], router_own[...]) + dot_nn(h_far[...], router_far[...])
    peak = jnp.max(jnp.where(chosen, logits, -jnp.inf), axis=1, keepdims=True)
    expo = jnp.where(chosen, jnp.exp(logits - peak), 0.0)
    gates = expo / jnp.sum(expo, axis=1, keepdims=True)
    grad_gates = jnp.zeros((rows, LANES), jnp.float32)
    for e in range(experts):
        here = lane == first + (e + place.side * split) % experts
        gate = jnp.sum(jnp.where(here, gates, 0.0), axis=1, keepdims=True)
        cols = slice(2 * LANES * (e % split), 2 * LANES * (e % split + 1))
        pair = dot_nn(h_own[...], pair_own[e // split, :, cols]) + dot_nn(
            h_far[...], pair_far[e // split, :, cols]
        )
        slope = grad_ref[:, LANES * e : LANES * (e + 1)].astype(jnp.float32)
        gate_val = pair[:, :LANES]
        up_val = pair[:, LANES:]
        sigma = jax.nn.sigmoid(gate_val)
        silu = gate_val * sigma
        hidden = silu * up_val
        dgate = jnp.sum(hidden * slope, axis=1, keepdims=True)
        grad_gates = jnp.where(here, dgate, grad_gates)
        dz = gate * slope
        hidden_ref[:, LANES * e : LANES * (e + 1)] = (gate * hidden).astype(jnp.bfloat16)
        slopes_ref[:, 2 * LANES * e : 2 * LANES * e + LANES] = (
            dz * up_val * (sigma + silu * (1.0 - sigma))
        ).astype(jnp.bfloat16)
        slopes_ref[:, 2 * LANES * e + LANES : 2 * LANES * (e + 1)] = (dz * silu).astype(
            jnp.bfloat16
        )
    dlog = gates * (grad_gates - jnp.sum(gates * grad_gates, axis=1, keepdims=True))
    dlog_high = dlog.astype(jnp.bfloat16)
    dlog_low = (dlog - dlog_high.astype(jnp.float32)).astype(jnp.bfloat16)
    dlog_ref[:, :LANES] = dlog_high
    dlog_ref[:, LANES:] = dlog_low

    def back(pairs, router):
        total = dot_nt(dlog_high, router[...]) + dot_nt(dlog_low, router[...])
        for i in range(2):
            cols = slice(2 * LANES * split * i, 2 * LANES * split * (i + 1))
            total = total + dot_nt(slopes_ref[:, cols], pairs[i])
        return total.astype(jnp.bfloat16)

    back_own, back_far = back(pair_own, router_own), back(pair_far, router_far)
    last = pl.num_programs(0) - 1

    @pl.when(step % 2 == 0)
    def _():
        keep_own[...] = back_own
        keep_far[...] = back_far

    @pl.when(step % 2 == 1)
    def _():
        give_own[...] = back_own
        give_far[...] = back_far

    for k in range(ZPARTS):

        @pl.when(step == 2 * k + 1)
        def _():
            t.start((BACK, C, k), (BACK, FAR_C, k))

    for i in range(2 * ZPARTS):

        @pl.when(step == i)
        def _():
            for copy in written(i):
                copy.start()

    moe_own[...] = low(dot_nn(hidden_ref[...], down_own[...].reshape(-1, part)))
    moe_far[...] = low(dot_nn(hidden_ref[...], down_far[...].reshape(-1, part)))

    @pl.when(step == last)
    def _():
        join(ZPARTS - 1)
        moves(
            local,
            (got_own.at[0], s0_own),
            (got_own.at[2], piece2),
            (got_own.at[3], s3_own),
            (got_far.at[3], s3_far),
        )
        for copy in written(2 * ZPARTS - 1):
            copy.wait()
        for i in range(2 * ZPARTS):
            for copy in saved(i):
                copy.wait()
        t.finish(*[(BACK, hop, k) for hop in (C, FAR_C) for k in range(ZPARTS)])


def moe_layer(routes, grad_hidden, routers, h2, weights, up_got, width):
    tile, part = h2.shape
    rows = grad_hidden.shape[0]
    experts = grad_hidden.shape[1] // LANES
    by_row = lambda width: pl.BlockSpec((tile, width), lambda i: (i, 0))
    stack = jax.ShapeDtypeStruct((ZPARTS, 2, tile, part), jnp.bfloat16)
    one = jax.ShapeDtypeStruct((tile, part), jnp.bfloat16)
    widths = [part, part, experts * LANES, 2 * experts * LANES, 2 * LANES]
    buffer = pltpu.VMEM((tile, part), jnp.bfloat16)
    stacked = pltpu.VMEM((ZPARTS, tile, part), jnp.bfloat16)
    pieces = pltpu.VMEM((ZPARTS, 2, tile, part), jnp.bfloat16)
    pair = pltpu.VMEM((2, part, experts * LANES), jnp.bfloat16)
    down = pltpu.VMEM((experts, LANES, part), jnp.bfloat16)
    extra = [like_of(up_got), jax.ShapeDtypeStruct((width, part), jnp.bfloat16)]
    count = 3 + 4 * (ZPARTS - 1) + 2 * ZPARTS + 6
    return pl.pallas_call(
        moe_kernel,
        out_shape=[stack, stack]
        + [jax.ShapeDtypeStruct((rows, w), jnp.bfloat16) for w in widths]
        + extra
        + [one] * 6,
        grid=(rows // tile,),
        in_specs=[by_row(routes.shape[1]), by_row(experts * LANES)]
        + [whole_block(r) for r in routers]
        + [ANY] * (1 + len(weights)),
        out_specs=[ANY, ANY, by_row(part), by_row(part), ANY, ANY, by_row(2 * LANES)]
        + [ANY] * 8,
        scratch_shapes=[pieces] * 2
        + [buffer] * 4
        + [stacked] * 2
        + [buffer, buffer, pair, pair, down, down]
        + [pltpu.VMEM((tile, w), jnp.bfloat16) for w in widths[2:4]]
        + [
            pltpu.SemaphoreType.DMA((2, count)),
            pltpu.SemaphoreType.DMA((5,)),
            pltpu.SemaphoreType.DMA((5 + 4 * experts,)),
            pltpu.SemaphoreType.DMA((4, 2 * ZPARTS)),
        ],
        compiler_params=pltpu.CompilerParams(
            collective_id=1, has_side_effects=True, vmem_limit_bytes=60 * 1024 * 1024
        ),
        name="moe_layer",
    )(routes, grad_hidden, *routers, h2, *weights)


def weight_kernel(cargo, streamed, *refs):
    n_cargo = len(cargo)
    h_own, h_far, c_own, c_far, hidden, slopes = refs[:6]
    sources = refs[6 : 6 + n_cargo]
    keep_own, keep_far, give_own, rest_far = refs[6 + n_cargo : 10 + n_cargo]
    landed = refs[10 + n_cargo : 10 + 2 * n_cargo]
    if streamed:
        far_land = refs[10 + 2 * n_cargo]
    give_far, sems, local = refs[-3:]
    place = Place()
    step = pl.program_id(0)
    t = Transfers(sems)
    partners = {X: place.x(), Y: place.y(), C: place.c()}
    partners.update({(Z, k): place.z(k) for k in range(1, ZPARTS)})
    to = {name: partners[name] for name, _ in cargo}
    for i, (name, views) in enumerate(cargo):
        for n, view in enumerate(views):
            t.add((i, n), sources[i].at[view], landed[i].at[n], to[name])
    first_keys = list(t.table)
    for e in range(streamed):
        t.add((GRADS, e), give_far.at[e], far_land.at[e], partners[Y])
    if streamed:
        to[Y] = partners[Y]

    @pl.when(step == 0)
    def _():
        greet(list(to.values()))
        t.start(*first_keys)

    half = LANES // 2
    tile = h_own.shape[2]
    first = place.side == 0
    for keep, give, at, rows_h, rows_c in (
        (keep_far, give_far, step, h_far, c_far),
        (keep_own, give_own, 0, h_own, c_own),
    ):
        pair, down = 0.0, 0.0
        for i in range(2 * ZPARTS):
            rows = slice(tile * i, tile * (i + 1))
            pair = pair + dot_tn(slopes[rows, :], rows_h[i // 2, i % 2])
            down = down + dot_tn(hidden[rows, :], rows_c[i // 2, i % 2])
        for i, block in enumerate((pair[:LANES], pair[LANES:], RESIDUAL * down)):
            begin, end = block[:half], block[half:]
            cut = slice(half * i, half * (i + 1))
            keep[0, cut, :] = jnp.where(first, begin, end)
            give[at, cut, :] = low(jnp.where(first, end, begin))
        if keep is keep_far:
            for e in range(streamed):

                @pl.when(step == e)
                def _():
                    t.start((GRADS, e))

    @pl.when(step == pl.num_programs(0) - 1)
    def _():
        rest = rest_far.shape[0]
        moves(local, (give_far.at[pl.ds(streamed, rest)], rest_far))
        t.finish()


def weight_grads(number, start, count, streamed, resident, hidden, slopes, cargo):
    part = resident[0].shape[-1]
    rows = hidden.shape[0]
    out = pl.BlockSpec((1, 3 * LANES // 2, part), lambda e: (e, 0, 0))
    block = (3 * LANES // 2, part)
    shape = (count, *block)
    arrays = [array for _, array, _ in cargo]
    views = tuple((name, tuple(where)) for name, _, where in cargo)
    landed = []
    for _, array, where in cargo:
        dims = (len(where), *array.shape[len(where[0]) :])
        landed.append(jax.ShapeDtypeStruct(dims, array.dtype))
    rest = jax.ShapeDtypeStruct((count - streamed, *block), jnp.bfloat16)
    if streamed:
        landed.append(jax.ShapeDtypeStruct((streamed, *block), jnp.bfloat16))
    transfers = sum(len(where) for _, _, where in cargo) + streamed
    return pl.pallas_call(
        functools.partial(weight_kernel, views, streamed),
        out_shape=[jax.ShapeDtypeStruct(shape, jnp.float32)] * 2
        + [jax.ShapeDtypeStruct(shape, jnp.bfloat16), rest]
        + landed,
        grid=(count,),
        in_specs=[whole_block(a) for a in resident]
        + [
            pl.BlockSpec((rows, LANES), lambda e: (0, e + start)),
            pl.BlockSpec((rows, 2 * LANES), lambda e: (0, e + start)),
        ]
        + [ANY] * len(arrays),
        out_specs=[out] * 3 + [ANY] * (1 + len(landed)),
        scratch_shapes=[
            pltpu.VMEM(shape, jnp.bfloat16),
            pltpu.SemaphoreType.DMA((2, transfers)),
            pltpu.SemaphoreType.DMA((1,)),
        ],
        compiler_params=pltpu.CompilerParams(
            collective_id=2 + number, has_side_effects=True, vmem_limit_bytes=60 * 1024 * 1024
        ),
        name="expert_weight_grads",
    )(*resident, hidden, slopes, *arrays)


def unturn(block, cosine, sine):
    return block * cosine + turn(block, jnp.zeros_like(cosine), -sine)


def attend_back_rows(
    q_ref, keys_ref, values_ref, grad_ref, allowed_ref, out_ref, dk, dv, cosine, sine, base, blocks
):
    rows = allowed_ref.shape[0]
    dk[...] = jnp.zeros_like(dk)
    dv[...] = jnp.zeros_like(dv)

    def body(j, carry):
        cols = pl.ds(pl.multiple_of(j * LANES, LANES), LANES)
        for start, stop, keys in score_tiles(rows):
            cut = slice(base + start, base + stop)
            lane = lax.broadcasted_iota(jnp.int32, (stop - start, LANES), 1)
            query, grad = q_ref[cut, cols], grad_ref[cut, cols]
            allowed = allowed_ref[:keys, start:stop] > 0
            dqs = []
            for side, part in enumerate((lane < HEAD_WIDTH, lane >= HEAD_WIDTH)):
                other = (2 * j + side) // blocks
                other = other + side - 2 * other * side
                key_rows = keys_ref[other, base : base + keys, :]
                value_rows = values_ref[other, base : base + keys, :]
                one_query = jnp.where(part, query, jnp.zeros_like(query))
                one_grad = jnp.where(part, grad, jnp.zeros_like(grad))
                scores = jnp.where(allowed, dot_nt(key_rows, one_query) * SCORE_SCALE, NEG)
                expo = jnp.exp(scores - jnp.max(scores, axis=0, keepdims=True))
                probs = expo * (1.0 / jnp.sum(expo, axis=0, keepdims=True))
                slope = dot_nt(value_rows, one_grad)
                delta = jnp.sum(probs * slope, axis=0, keepdims=True)
                dscore = low(probs * (slope - delta))
                dv[other, :keys, :] = dv[other, :keys, :] + dot_nn(low(probs), one_grad)
                dk[other, :keys, :] = dk[other, :keys, :] + dot_nn(dscore, one_query)
                dqs.append(dot_tn(dscore, key_rows))
            dq = jnp.where(lane < HEAD_WIDTH, dqs[0], dqs[1]) * SCORE_SCALE
            out_ref[cut, cols] = low(unturn(dq, cosine[cut, :], sine[cut, :]))
        return carry

    lax.fori_loop(0, blocks, body, 0)
    cut = slice(base, base + rows)
    width = blocks * LANES
    total = (dk[0] + pltpu.roll(dk[1], HEAD_WIDTH, 1)) * SCORE_SCALE
    out_ref[cut, width : width + LANES] = low(unturn(total, cosine[cut, :], sine[cut, :]))
    out_ref[cut, width + LANES :] = low(dv[0] + pltpu.roll(dv[1], HEAD_WIDTH, 1))


class WholeSum:
    def __init__(self, t, name, ref, levels, stages, lands, swap=None):
        self.t, self.name, self.ref = t, name, ref
        self.stages, self.lands, self.count = stages, lands, len(levels)
        offset, rows = 0, ref.shape[0]
        self.kept, self.other = [], []
        ways = []
        for i, (partner, bit) in enumerate(levels):
            rows = rows // 2
            self.other.append((offset + (1 - bit) * rows, rows))
            offset = offset + bit * rows
            self.kept.append((offset, rows))
            ways.append((i, i, self.other[i], self.kept[i], partner))
        last = self.count - 1
        back = [
            (i, self.count + i, self.kept[i], self.other[i], levels[i][0])
            for i in range(last, -1, -1)
        ]
        if swap is not None:
            ways.append((last, 2 * self.count, self.kept[last], self.kept[last], swap))
        self.ways = ways + back
        for i, (stage, land, _, _, partner) in enumerate(self.ways):
            t.add((SUM, name, i), stages[stage], lands[land], partner)

    def rows(self, place):
        return pl.ds(pl.multiple_of(place[0], 8), place[1])

    def send(self, i):
        stage, _, place, _, _ = self.ways[i]
        for j in range(i - 1, -1, -1):
            if self.ways[j][0] == stage:
                self.t.sent((SUM, self.name, j))
                break
        self.stages[stage][...] = low(self.ref[self.rows(place), :])
        self.t.start((SUM, self.name, i))

    def land(self, i):
        self.t.arrived((SUM, self.name, i))
        _, land, _, place, _ = self.ways[i]
        cut = self.rows(place)
        total = self.lands[land][...].astype(jnp.float32)
        if i < self.count:
            total = self.ref[cut, :] + total
            if i == self.count - 1:
                total = low(total).astype(jnp.float32)
        self.ref[cut, :] = total

    def next(self, i):
        if 0 <= i < len(self.ways):
            self.land(i)
            if i + 1 < len(self.ways):
                self.send(i + 1)

    def keys(self):
        done = []
        for i, way in enumerate(self.ways):
            if any(later[0] == way[0] for later in self.ways[i + 1 :]):
                done.append((SUM, self.name, i))
        return done


class SmallSum:
    def __init__(self, t, name, ref, partners, lands):
        self.t, self.name, self.ref, self.lands = t, name, ref, lands
        for i, partner in enumerate(partners):
            t.add((SMALL, name, i), ref, lands.at[i], partner)

    def send(self, i):
        self.t.start((SMALL, self.name, i))

    def land(self, i):
        self.t.sent((SMALL, self.name, i))
        self.t.arrived((SMALL, self.name, i))
        self.ref[...] = self.ref[...] + self.lands[i]

    def next(self, i):
        if 0 <= i < self.lands.shape[0]:
            self.land(i)
            if i + 1 < self.lands.shape[0]:
                self.send(i + 1)

    def keys(self):
        return [(SMALL, self.name, i) for i in range(self.lands.shape[0])]


SUMMED = 40


def back_kernel(count, with_grads, *refs):
    refs = list(refs)
    take = lambda n: [refs.pop(0) for _ in range(n)]
    qkv = take(3)
    moe_srcs = take(4)
    tokens, cot, middle, inv_first, inv_second, gain, gain_moe = take(7)
    parts = take(5)
    q_ref, keys, values, mixed, mixed_far, normed, normed_far = take(7)
    cosine, sine, seg_row, seg_col = take(4)
    w_out, out_far, small_own, small_there = take(4)
    if with_grads:
        grad_srcs, keep_first = take(3), take(1)[0]
    moe_lands = take(4)
    if with_grads:
        grad_lands = take(3)
    grad_tokens, grad_q, grad_k, grad_v, grad_out, small, small_last = take(7)
    qkv_here, qkv_there, da_own, da_far, grad_mixed, dqkv, dqkv_far, give, got = take(9)
    grad_middle, grad_here, grad_there, allowed, dk, dv, square, square_far = take(8)
    small_land, small_lands, last_lands = take(3)
    stages, lands = [], []
    for _ in range(3):
        stages.append(take(count))
        lands.append(take(2 * count + 1))
    if with_grads:
        first_land, first_sum = take(2)
    sems, local = take(2)
    place = Place()
    t = Transfers(sems)
    x, c, y = place.x(), place.c(), place.y()
    rows, part = tokens.shape
    width = q_ref.shape[1]
    low_levels, high_levels = place.bits()
    partners = [partner for partner, _ in low_levels + high_levels]
    t.add((INNER, 0), square.at[0], square_far.at[0], x)
    t.add((INNER, 1), square.at[1], square_far.at[1], x)
    t.add((SMALL, X), small_there, small_land, x)
    first, second = pl.ds(0, rows), pl.ds(rows, rows)
    t.add((DA, X), da_own.at[first], da_far.at[first], x)
    t.add((DA, C), da_own.at[first], da_own.at[second], c)
    t.add((DA, FAR_C), da_far.at[first], da_far.at[second], c)
    for i, cut in enumerate((first, second)):
        t.add((DQKV, i), dqkv.at[cut], dqkv_far.at[cut], x)
    t.add((ATTN, C), give, got, c)
    for i, partner in enumerate((place.z(1), place.z(2), place.z(3), x)):
        t.add((MOE, i), moe_srcs[i], moe_lands[i], partner)
    if with_grads:
        t.add((GRADS, Y, 0), grad_srcs[0], first_land, y)
        t.add((GRADS, Y, 1), grad_srcs[1], grad_lands[0], y)
        t.add((GRADS, X, 0), grad_srcs[2], grad_lands[1], x)
        t.add((GRADS, X, 1), first_sum, grad_lands[2], x)
    up, down = high_levels + low_levels, low_levels + high_levels
    sum_out = WholeSum(t, 0, grad_out, up, stages[0], lands[0])
    sum_here = WholeSum(t, 1, grad_here, down, stages[1], lands[1])
    sum_there = WholeSum(t, 2, grad_there, up, stages[2], lands[2], x)
    small_sum = SmallSum(t, 0, small, [c] + partners, small_lands)
    last_sum = SmallSum(t, 1, small_last, [c] + partners, last_lands)

    greet([x, c, place.z(3)] + partners)
    t.start((SMALL, X), (MOE, 1), (MOE, 2))
    if with_grads:
        t.start((GRADS, Y, 0))
    here, there = qkv_slices(qkv, place.col), qkv_slices(qkv, 1 - place.col)
    targets = [*qkv_targets(qkv_here, qkv), *qkv_targets(qkv_there, qkv)]
    moves(local, *zip([*here, *there], targets))

    def masks(b):
        allowed[...] = allowed_tile(seg_row[b : b + 1, :], seg_col[:, b : b + 1], True)

    def exchange_sum(i, total):
        square[i] = jnp.broadcast_to(total, (rows, LANES)).T[:8, :]
        t.start((INNER, i))

    def exchanged(i, total):
        t.arrived((INNER, i))
        return total + jnp.broadcast_to(square_far[i, :1, :], (LANES, rows)).T[:, :1]

    def norm_back(grad, value, inv, gain_row, inner):
        return inv * (grad * gain_row) - value * (inv * inv * inv * inner / (2 * part))

    grad = add_wide(*[p[...] for p in parts])
    inv = inv_second[:, :1]
    inner = jnp.sum(middle[...] * grad * gain_moe[...], 1, keepdims=True)
    exchange_sum(0, inner)
    small[...] = small_own[...]
    small[SUMMED : SUMMED + 1, :] = jnp.sum(grad * middle[...] * inv, 0, keepdims=True)
    inner = exchanged(0, inner)
    total = cot[...].astype(jnp.float32)
    total = total + norm_back(grad, middle[...], inv, gain_moe[...], inner)
    grad_middle[...] = total
    da_own[:rows, :] = low(RESIDUAL * total)
    t.start((DA, X), (DA, C))
    masks(1)
    t.arrived((SMALL, X))
    small[...] = small[...] + small_land[...]
    small_sum.send(0)
    t.arrived((DA, C))
    at_here = pl.ds(pl.multiple_of(place.col * width, LANES), width)
    at_there = pl.ds(pl.multiple_of((1 - place.col) * width, LANES), width)
    grad_out[at_here, :] = dot_tn(mixed[...], da_own[...])
    grad_out[at_there, :] = dot_tn(mixed_far[...], da_own[...])
    sum_out.send(0)
    small_sum.next(0)
    t.arrived((DA, X))
    t.start((DA, FAR_C))
    if with_grads:
        t.start((GRADS, X, 0))

    def mixed_back(cut):
        total = dot_nt(da_own[cut, :], w_out[at_here, :]) + dot_nt(da_far[cut, :], out_far[...])
        grad_mixed[cut, :] = low(total)

    mixed_back(slice(0, rows))
    t.arrived((DA, FAR_C))
    mixed_back(slice(rows, 2 * rows))
    attend = functools.partial(
        attend_back_rows, q_ref, keys, values, grad_mixed, allowed, dqkv, dk, dv, cosine, sine
    )
    attend(rows, width // LANES)
    t.start((DQKV, 1))
    sum_out.next(0)
    small_sum.next(1)
    if with_grads:
        t.arrived((GRADS, Y, 0))
        t.start((GRADS, Y, 1))
        first_sum[...] = low(keep_first[...] + first_land[...].astype(jnp.float32))
    t.start((MOE, 0))
    masks(0)
    attend(0, width // LANES)
    t.start((DQKV, 0))
    grad_here[...] = dot_tn(normed[...], dqkv[...])
    sum_here.send(0)
    grad_there[...] = dot_tn(normed_far[...], dqkv[...])
    sum_there.send(0)
    sum_out.next(1)
    t.arrived((DQKV, 1))

    def tokens_back(cut):
        return dot_nt(dqkv[cut, :], qkv_here[...]) + dot_nt(dqkv_far[cut, :], qkv_there[...])

    give[...] = tokens_back(slice(rows, 2 * rows))
    t.start((ATTN, C))
    sum_here.next(0)
    sum_there.next(0)
    sum_out.next(2)
    small_sum.next(2)
    t.arrived((DQKV, 0))
    if with_grads:
        t.start((GRADS, X, 1))
    grad = tokens_back(slice(0, rows))
    t.arrived((ATTN, C))
    grad = grad + got[...]
    got[...] = grad
    value = tokens[...].astype(jnp.float32)
    inv = inv_first[:, :1]
    inner = jnp.sum(value * grad * gain[...], 1, keepdims=True)
    exchange_sum(1, inner)
    small_last[...] = jnp.zeros_like(small_last)
    small_last[0:1, :] = jnp.sum(grad * value * inv, 0, keepdims=True)
    last_sum.send(0)
    sum_here.next(1)
    sum_there.next(1)
    sum_out.next(3)
    inner = exchanged(1, inner)
    t.start((MOE, 3))
    grad = norm_back(got[...], tokens[...].astype(jnp.float32), inv, gain[...], inner)
    grad_tokens[...] = grad_middle[...] + grad
    last_sum.next(0)
    for i in range(2, 2 * count + 1):
        sum_here.next(i)
        sum_there.next(i)
        sum_out.next(i + 2)
        small_sum.next(i + 1)
        last_sum.next(i - 1)
    for i in range(2 * count, small_lands.shape[0]):
        small_sum.next(i + 1)
        last_sum.next(i)
    start = 0
    for out in (grad_q, grad_k, grad_v):
        size = out.shape[1] // 2
        cut = slice(start, start + size)
        out[:, pl.ds(pl.multiple_of(place.col * size, LANES), size)] = grad_here[:, cut]
        out[:, pl.ds(pl.multiple_of((1 - place.col) * size, LANES), size)] = grad_there[:, cut]
        start += size
    done = [key for each in (sum_out, sum_here, sum_there, small_sum, last_sum) for key in each.keys()]
    t.finish(*done)


def back(levels, qkv, moe_srcs, vmem_ins, grads):
    tokens, middle, q = vmem_ins[0], vmem_ins[2], vmem_ins[12]
    w_out, small_own = vmem_ins[23], vmem_ins[25]
    rows, part = tokens.shape
    width, kv = q.shape[1], qkv[1].shape[1] // 2
    both = width + 2 * kv
    vmem = pl.BlockSpec(memory_space=pltpu.VMEM)
    bf16, f32 = jnp.bfloat16, jnp.float32
    shape = jax.ShapeDtypeStruct
    like = lambda a: shape(a.shape, a.dtype)
    hbm_outs = [like(a) for a in moe_srcs]
    extra_ins, extra_specs, extra_scratch = [], [], []
    if grads:
        extra_ins = list(grads)
        extra_specs = [ANY] * 3 + [vmem]
        hbm_outs += [like(a) for a in (*grads[1:3], grads[0])]
        extra_scratch = [pltpu.VMEM(grads[0].shape, bf16)] * 2
    small_last = shape((8, part), f32)
    vmem_outs = [shape((rows, part), f32)]
    vmem_outs += [shape((part, w.shape[1]), f32) for w in qkv]
    vmem_outs += [shape(w_out.shape, f32), like(small_own), small_last]
    twice = lambda w, dtype=bf16: pltpu.VMEM((2 * rows, w), dtype)
    wide = pltpu.VMEM((rows, part), f32)
    pair = pltpu.VMEM((2, rows, LANES), f32)
    flat = pltpu.VMEM((2, 8, rows), f32)
    scratch = [pltpu.VMEM((part, both), bf16)] * 2
    scratch += [twice(part), twice(part), twice(width), twice(both), twice(both), wide, wide]
    scratch += [wide, pltpu.VMEM((part, both), f32), pltpu.VMEM((part, both), f32)]
    scratch += [pltpu.VMEM((rows, rows), f32), pair, pair, flat, flat]
    scratch += [pltpu.VMEM(small_own.shape, f32)]
    scratch += [pltpu.VMEM((levels + 1, *small_own.shape), f32)]
    scratch += [pltpu.VMEM((levels + 1, 8, part), f32)]
    for high, wide_cols in ((w_out.shape[0], part), (part, both), (part, both)):
        sizes = [pltpu.VMEM((high >> (i + 1), wide_cols), bf16) for i in range(levels)]
        scratch += sizes * 3 + sizes[-1:]
    scratch += extra_scratch
    count = 9 + 4 + 4 + 3 * 2 * levels + 1 + 2 * (levels + 1)
    scratch += [pltpu.SemaphoreType.DMA((2, count)), pltpu.SemaphoreType.DMA((6,))]
    return pl.pallas_call(
        functools.partial(back_kernel, levels, bool(grads)),
        out_shape=hbm_outs + vmem_outs,
        in_specs=[ANY] * (len(qkv) + len(moe_srcs)) + [vmem] * len(vmem_ins) + extra_specs,
        out_specs=[ANY] * len(hbm_outs) + [vmem] * len(vmem_outs),
        scratch_shapes=scratch,
        compiler_params=pltpu.CompilerParams(
            collective_id=4, has_side_effects=True, vmem_limit_bytes=63 * 1024 * 1024
        ),
        name="back",
    )(*qkv, *moe_srcs, *vmem_ins, *extra_ins)


def halve(value, index, mask, axis):
    first, last = jnp.split(value, 2, axis)
    upper = (index & mask) != 0
    send = low(jnp.where(upper, first, last))
    return jnp.where(upper, last, first) + flip(send, "dp", mask).astype(jnp.float32)


def on_device(
    tokens,
    gain_attn,
    w_query,
    key_matrix,
    value_matrix,
    w_out,
    gain_moe,
    w_router,
    w_gate,
    w_up,
    w_down,
    segments,
    routes,
    cotangent,
):
    col = lax.axis_index("col")
    core = lax.axis_index("expert")
    group = lax.axis_index("dp")
    dp_size = lax.axis_size("dp")
    step = dp_size // ZPARTS
    member = group % step
    levels = dp_size.bit_length() - 1
    half_mask = step // 2
    side = (member // half_mask) % 2

    local, part, ffn = w_gate.shape
    split = local // 4
    units = ffn // ZPARTS
    experts = local * lax.axis_size("expert")
    rows = tokens.shape[0]
    width = w_query.shape[1] // 2

    router_own = jnp.pad(w_router, ((0, 0), (0, LANES - experts)))
    seg_rows = jnp.where(core == 0, segments, segments[::-1])
    positions = jax.vmap(doc_positions)(seg_rows).reshape(-1, 1).astype(jnp.float32)
    half = HEAD_WIDTH // 2
    slot = jnp.arange(LANES, dtype=jnp.int32)
    freq = jnp.exp((slot % half).astype(jnp.float32) * (-2.0 * math.log(THETA) / HEAD_WIDTH))
    sign = jnp.where(slot % HEAD_WIDTH < half, -1.0, 1.0)
    cosine, sine = jnp.cos(positions * freq), jnp.sin(positions * freq) * sign
    qkv = [w_query, key_matrix, value_matrix]
    gain, gain_second = gain_attn[None], gain_moe[None]
    (
        down_got,
        down_other,
        gate_got,
        gate_other,
        up_got,
        router_far,
        c_own,
        c_far,
        route_all,
        grad_hidden,
        q,
        keys,
        values,
        mixed,
        mixed_far,
        normed,
        normed_far,
        inv_first,
        middle,
        inv_second,
        h2,
    ) = front(
        tokens,
        cotangent,
        w_down,
        w_gate,
        w_up,
        router_own,
        routes.T,
        qkv,
        gain,
        gain_second,
        w_out,
        cosine,
        sine,
        seg_rows,
        seg_rows.T,
    )
    route_rows = jnp.swapaxes(route_all, 2, 3).reshape(2 * ZPARTS * rows, -1)
    (
        h_own,
        h_far,
        moe_own,
        moe_far,
        hidden,
        slopes,
        dlog,
        _,
        out_far,
        s0_own,
        z1_own,
        x0_far,
        piece2,
        s3_own,
        s3_far,
    ) = moe_layer(
        route_rows,
        grad_hidden,
        [router_own, router_far],
        h2,
        [w_gate, w_up, w_down, w_out, gate_got, gate_other, up_got, down_got, down_other],
        up_got,
        width,
    )
    resident = [h_own, h_far, c_own, c_far]
    moe_own, moe_far = (a.reshape(ZPARTS, 2, rows, part) for a in (moe_own, moe_far))
    seconds = tuple((k, 1) for k in range(ZPARTS))
    cargo = [
        ((Z, 2), piece2[None], ((0,),)),
        (X, s3_far[None], ((0,),)),
        (C, moe_own, seconds),
        (C, moe_far, seconds),
    ]
    streamed = split - 1 if half_mask == 1 else 0
    first_outs = weight_grads(0, 0, split, streamed, resident, hidden, slopes, cargo)
    first_part, (z2_piece, x3_far, sib_own, sib_far) = first_outs[:4], first_outs[4:8]
    far_early = first_outs[8:]
    moe_own = low(add_wide(moe_own[:, 0], sib_own))
    moe_far = low(add_wide(moe_far[:, 0], sib_far))
    cargo = [
        ((Z, 3), low(add_wide(s3_own[None], x3_far)), ((0,),)),
        (Y, first_part[3][None], ((0,),)),
        (Y, first_part[2][None], ((0,),)),
        (X, moe_far, ((2,), (3,))),
        ((Z, 1), moe_far, ((1,),)),
    ]
    *second_part, z3_piece, far_late, got_second, moe_x, moe_z1_far = weight_grads(
        1, split, split, 0, resident, hidden, slopes, cargo
    )
    z2_piece, z3_piece, got_second = z2_piece[0], z3_piece[0], got_second[0]
    moe_srcs = [
        moe_own[1],
        low(add_wide(moe_own[2], moe_x[0])),
        low(add_wide(moe_own[3], moe_x[1])),
        low(add_wide(moe_far[0], moe_z1_far[0])),
    ]

    def router_term(h_rows):
        total = dot_tn(dlog, h_rows.reshape(-1, part))
        total = total[:experts] + total[LANES : LANES + experts]
        return jnp.pad(total, ((0, 8), (0, 0)))

    vmem_ins = [
        tokens,
        cotangent,
        middle,
        inv_first,
        inv_second,
        gain,
        gain_second,
        s0_own,
        z1_own,
        z2_piece,
        x0_far,
        z3_piece,
        q,
        keys,
        values,
        mixed,
        mixed_far,
        normed,
        normed_far,
        cosine,
        sine,
        seg_rows,
        seg_rows.T,
        w_out,
        out_far,
        router_term(h_own),
        router_term(h_far),
    ]
    swap = lambda a: flip(a, "dp", half_mask)
    plain = half_mask == 1
    grads = []
    y_far = jnp.concatenate([*far_early, far_late[0]], 0)
    if plain:
        second_far = low(add_wide(second_part[1], y_far))
        grads = [second_part[3], second_part[2], second_far, first_part[1]]
    outs = back(levels, qkv, moe_srcs, vmem_ins, grads)
    moe_parts, outs = outs[:4], outs[4:]
    own_second = add_wide(second_part[0], got_second)
    if plain:
        (got_first, far_second, far_first), outs = outs[:3], outs[3:]
        own_first = add_wide(first_part[0], got_first)
    else:

        def finish_grads(keep_own, keep_far):
            shape = (split, 3, units // 2, part)
            keep_own, keep_far = keep_own.reshape(shape), keep_far.reshape(shape)
            mask = half_mask // 2
            while mask:
                keep_own = halve(keep_own, member, mask, 2)
                keep_far = halve(keep_far, member, mask, 2)
                mask //= 2
            return keep_own, flip(low(keep_far), "col")

        own_second, far_second = finish_grads(own_second, add_wide(second_part[1], y_far))
        own_first, far_first = finish_grads(
            add_wide(first_part[0], swap(second_part[2])),
            add_wide(first_part[1], swap(second_part[3])),
        )
    grad_tokens, grad_query, grad_key, grad_value, grad_out, small, small_last = outs

    def in_order(a, b, index):
        a, b = a.astype(jnp.float32), b.astype(jnp.float32)
        return jnp.concatenate([jnp.where(index == 0, a, b), jnp.where(index == 0, b, a)], 0)

    expert_grads = in_order(
        in_order(own_first, own_second, side), in_order(far_first, far_second, side), col
    )
    expert_grads = expert_grads.reshape(local, 3, -1, part)
    output = middle + RESIDUAL * add_wide(moe_own[0], *moe_parts)
    return (
        output,
        grad_tokens,
        small_last[0],
        grad_query,
        grad_key,
        grad_value,
        grad_out,
        small[SUMMED],
        small[:experts].T,
        jnp.swapaxes(expert_grads[:, 0], 1, 2),
        jnp.swapaxes(expert_grads[:, 1], 1, 2),
        expert_grads[:, 2],
    )


def solution(mesh):
    in_specs = (
        P(("dp", "expert"), "col"),
        P("col"),
        P("col", "expert"),
        P("col", "expert"),
        P("col", "expert"),
        P("expert", "col"),
        P("col"),
        P("col", None),
        P("expert", "col", None),
        P("expert", "col", None),
        P("expert", None, "col"),
        P("dp", None),
        P(("dp", "expert"), None),
        P(("dp", "expert"), "col"),
    )
    out_specs = (
        P(("dp", "expert"), "col"),
        P(("dp", "expert"), "col"),
        P("col"),
        P("col", "expert"),
        P("col", "expert"),
        P("col", "expert"),
        P("expert", "col"),
        P("col"),
        P("col", None),
        P("expert", "col", "dp"),
        P("expert", "col", "dp"),
        P("expert", "dp", "col"),
    )
    return jax.shard_map(
        on_device, mesh=mesh, in_specs=in_specs, out_specs=out_specs, check_vma=False
    )
```

```python
import functools
import math

import jax
import jax.numpy as jnp
from jax import lax
from jax.experimental import pallas as pl
from jax.experimental.pallas import tpu as pltpu
from jax.sharding import PartitionSpec as P

HEAD_WIDTH = 64
(
    COT,
    TOK,
    DOWN,
    QKV,
    GATE,
    UP,
    ROUTER,
    GAIN,
    ROUTES,
    MIXED,
    ATTN,
    SQUARE,
    H,
    BACK,
    DA,
    DQKV,
    INNER,
    GRADS,
    MOE,
    SMALL,
    SUM,
    OUT,
) = range(22)
X, C, Y, Z, FAR_X, FAR_C, FAR_Z = range(7)
ZPARTS = 4
EARLY = 6
LANES = 128


EPS = 1e-06
RESIDUAL = 0.22
SCORE_SCALE = 0.015625
THETA = 10000.0
NEG = -1000000000.0


def doc_positions(seg_row):
    length_total = seg_row.shape[0]
    index = jnp.arange(length_total, dtype=jnp.int32)
    before = jnp.concatenate([jnp.full((1,), -1, jnp.int32), seg_row[:-1]])
    starts = jnp.where(seg_row != before, index, 0)
    return index - lax.cummax(starts, axis=0)


def flip(value, axis, mask=1):
    size = lax.axis_size(axis)
    return lax.ppermute(value, axis, [(i, i ^ mask) for i in range(size)])


def dot_nn(a, b):
    return jnp.dot(a, b, preferred_element_type=jnp.float32)


def dot_nt(a, b):
    return lax.dot_general(a, b, (((1,), (1,)), ((), ())), preferred_element_type=jnp.float32)


def dot_tn(a, b):
    return lax.dot_general(a, b, (((0,), (0,)), ((), ())), preferred_element_type=jnp.float32)


def add_wide(*parts):
    return sum(p.astype(jnp.float32) for p in parts)


def low(value):
    return value.astype(jnp.bfloat16)


class Place:
    def __init__(self):
        self.col = lax.axis_index("col")
        self.core = lax.axis_index("expert")
        group = lax.axis_index("dp")
        self.step = lax.axis_size("dp") // ZPARTS
        self.zed, self.member = group // self.step, group % self.step
        self.half = self.step // 2
        self.side = (self.member // self.half) % 2

    def x(self):
        return {"col": 1 - self.col}

    def c(self):
        return {"expert": 1 - self.core}

    def y(self):
        return {"dp": self.zed * self.step + self.member + self.half * (1 - 2 * self.side)}

    def z(self, k):
        zed = self.zed
        other = (zed + 1 - 2 * (zed % 2), (zed + 2) % ZPARTS, ZPARTS - 1 - zed)[k - 1]
        return {"dp": other * self.step + self.member}

    def bits(self):
        levels = []
        mask = self.half
        while mask:
            bit = (self.member // mask) % 2
            partner = self.zed * self.step + self.member + mask * (1 - 2 * bit)
            levels.append(({"dp": partner}, bit))
            mask //= 2
        return levels, [(self.z(1), self.zed % 2), (self.z(2), self.zed // 2)]


def greet(partners):
    barrier = pltpu.get_barrier_semaphore()
    for partner in partners:
        pl.semaphore_signal(
            barrier, inc=1, device_id=partner, device_id_type=pl.DeviceIdType.MESH
        )
    pl.semaphore_wait(barrier, len(partners))


class Transfers:
    def __init__(self, sems):
        self.sems, self.table, self.waited = sems, {}, set()

    def add(self, key, src, dst, partner):
        self.table[key] = (len(self.table), src, dst, partner)

    def copy(self, key):
        i, src, dst, partner = self.table[key]
        return pltpu.make_async_remote_copy(
            src_ref=src,
            dst_ref=dst,
            send_sem=self.sems.at[0, i],
            recv_sem=self.sems.at[1, i],
            device_id=partner,
            device_id_type=pl.DeviceIdType.MESH,
        )

    def start(self, *keys):
        for key in keys:
            self.copy(key).start()

    def arrived(self, *keys):
        for key in keys:
            self.waited.add(key)
            self.copy(key).wait_recv()

    def sent(self, *keys):
        for key in keys:
            self.copy(key).wait_send()

    def finish(self, *sent):
        for key in self.table:
            if key not in sent:
                self.copy(key).wait_send()
        for key in self.table:
            if key not in self.waited:
                self.copy(key).wait_recv()


def moves(sems, *pairs):
    copies = [pltpu.make_async_copy(src, dst, sems.at[i]) for i, (src, dst) in enumerate(pairs)]
    for copy in copies:
        copy.start()
    for copy in copies:
        copy.wait()


ANY = pl.BlockSpec(memory_space=pl.ANY)


def like_of(a):
    return jax.ShapeDtypeStruct(a.shape, a.dtype)


def whole_block(a):
    return pl.BlockSpec(a.shape, lambda *_: (0,) * a.ndim, pipeline_mode=pl.Buffered(1))


def turn(block, cosine, sine):
    lane = lax.broadcasted_iota(jnp.int32, block.shape, 1) % HEAD_WIDTH
    ahead = pltpu.roll(block, LANES - HEAD_WIDTH // 2, 1)
    behind = pltpu.roll(block, HEAD_WIDTH // 2, 1)
    return block * cosine + jnp.where(lane < HEAD_WIDTH // 2, ahead, behind) * sine


def score_tiles(rows):
    half = rows // 2
    return ((0, half, half), (half, rows, rows))


def allowed_tile(seg_row, seg_col, across_keys):
    shape = (seg_col.shape[0], seg_row.shape[1])
    down, along = (lax.broadcasted_iota(jnp.int32, shape, axis) for axis in (0, 1))
    order = down <= along if across_keys else along <= down
    return jnp.where((seg_row == seg_col) & order, 1.0, 0.0)


def swap_heads(value):
    return pltpu.roll(value.astype(jnp.float32), HEAD_WIDTH, 1).astype(value.dtype)


def attend_rows(q_ref, keys_ref, values_ref, allowed_ref, out_ref, base, blocks):
    rows = allowed_ref.shape[0]
    group = blocks

    def body(j, carry):
        cols = pl.ds(pl.multiple_of(j * LANES, LANES), LANES)
        for start, stop, keys in score_tiles(rows):
            lane = lax.broadcasted_iota(jnp.int32, (stop - start, LANES), 1)
            query = q_ref[base + start : base + stop, cols]
            allowed = allowed_ref[start:stop, :keys] > 0
            outs = []
            for side, part in enumerate((lane < HEAD_WIDTH, lane >= HEAD_WIDTH)):
                other = (2 * j + side) // group
                other = other + side - 2 * other * side
                key_rows = keys_ref[other, base : base + keys, :]
                scores = dot_nt(jnp.where(part, query, jnp.zeros_like(query)), key_rows)
                scores = jnp.where(allowed, scores * SCORE_SCALE, NEG)
                expo = jnp.exp(scores - jnp.max(scores, axis=1, keepdims=True))
                probs = expo * (1.0 / jnp.sum(expo, axis=1, keepdims=True))
                outs.append(dot_nn(low(probs), values_ref[other, base : base + keys, :]))
            mixed = jnp.where(lane < HEAD_WIDTH, outs[0], outs[1])
            out_ref[base + start : base + stop, cols] = low(mixed)
        return carry

    lax.fori_loop(0, blocks, body, 0)


def weight_slice(ref, which, half, split, zed, wide):
    first = (2 * which + half) * split
    units = pl.ds(pl.multiple_of(zed * LANES, LANES), LANES)
    if wide:
        return ref.at[pl.ds(first, split), units, :]
    return ref.at[pl.ds(first, split), :, units]


def qkv_slices(refs, which):
    widths = [ref.shape[1] // 2 for ref in refs]
    return [
        ref.at[:, pl.ds(pl.multiple_of(which * w, LANES), w)] for ref, w in zip(refs, widths)
    ]


def qkv_targets(target, refs):
    widths = [ref.shape[1] // 2 for ref in refs]
    starts = [sum(widths[:i]) for i in range(len(widths))]
    return [target.at[:, pl.ds(start, w)] for start, w in zip(starts, widths)]


def front_kernel(*refs):
    tokens, cot, w_down, w_gate, w_up, router, routes = refs[:7]
    qkv = refs[7:10]
    gain, gain_moe, w_out, cosine, sine, seg_row, seg_col = refs[10:17]
    (
        down_got,
        down_other,
        gate_got,
        gate_other,
        up_got,
        router_far,
        c_own,
        c_far,
        route_all,
        grad_hidden,
        q_ref,
        keys,
        values,
        mixed,
        mixed_far,
        normed,
        normed_far,
        inv_first,
        middle_ref,
        inv_second,
        h2_ref,
    ) = refs[17:38]
    tok, qkv_here, qkv_far, gain_far, give, got, square, square_far = refs[38:46]
    own_buf, far_buf, down_own, down_buf, grad_buf, allowed, pair_stage, qkv_stage, sems, local = refs[46:]
    place = Place()
    t = Transfers(sems)
    x, c, y = place.x(), place.c(), place.y()
    z = [None] + [place.z(k) for k in range(1, ZPARTS)]
    rows, part = tokens.shape
    ks = range(1, ZPARTS)
    t.add((TOK, X), tokens, tok.at[0], x)
    t.add((TOK, C), tokens, tok.at[1], c)
    t.add((TOK, FAR_C), tok.at[0], tok.at[2], c)
    there = qkv_slices(qkv, 1 - place.col)
    half = part // 2
    halves = [pl.ds(pl.multiple_of(i * half, half), half) for i in (place.side, 1 - place.side)]
    t.add((QKV, X), qkv_stage, qkv_far.at[0], x)
    t.add((QKV, Y), qkv_far.at[0], qkv_far.at[1], y)
    t.add((GAIN, X), gain, gain_far, x)
    t.add((ROUTER, X), router, router_far, x)
    t.add((COT, X), cot, c_far.at[0, 0], x)
    t.add((COT, C, 0), cot, c_own.at[0, 1], c)
    t.add((COT, FAR_C, 0), c_far.at[0, 0], c_far.at[0, 1], c)
    t.add((ROUTES, C, 0), routes, route_all.at[0, 1], c)
    for k in ks:
        t.add((COT, Z, k), cot, c_own.at[k, 0], z[k])
        t.add((COT, FAR_Z, k), c_far.at[0, 0], c_far.at[k, 0], z[k])
        t.add((COT, C, k), c_own.at[k, 0], c_own.at[k, 1], c)
        t.add((COT, FAR_C, k), c_far.at[k, 0], c_far.at[k, 1], c)
        t.add((ROUTES, Z, k), routes, route_all.at[k, 0], z[k])
        t.add((ROUTES, C, k), route_all.at[k, 0], route_all.at[k, 1], c)
    split = down_got.shape[0]
    staged = []
    for key, ref, land, other in (
        (DOWN, w_down, down_got, down_other),
        (GATE, w_gate, gate_got, gate_other),
        (UP, w_up, up_got, None),
    ):
        src = weight_slice(ref, 1 - place.col, place.side, split, place.zed, key == DOWN)
        if key != DOWN:
            staged.append((src, pair_stage.at[len(staged)]))
            src = staged[-1][1]
        t.add((key, X), src, land, x)
        if key != UP:
            t.add((key, Y), land, other, y)
    for i in range(2):
        cut = pl.ds(rows * i, rows)
        t.add((MIXED, X, i), mixed.at[cut], mixed_far.at[cut], x)
    t.add((ATTN, C), give, got, c)
    t.add((SQUARE, X), square, square_far, x)

    greet([x, c, y, *z[1:]])
    t.start((TOK, X), (GAIN, X))
    targets = [target.at[pl.ds(0, half)] for target in qkv_targets(qkv_stage, qkv)]
    moves(local, *[(src.at[halves[0]], target) for src, target in zip(there, targets)])
    t.start((QKV, X))
    t.start((TOK, C), (COT, C, 0), (ROUTES, C, 0), *[(ROUTES, Z, k) for k in ks])
    t.start((COT, Z, 1), (COT, Z, 2), (COT, Z, 3))
    own_cut = functools.partial(weight_slice, w_down, place.col, split=split, zed=place.zed)
    moves(
        local,
        (cot, c_own.at[0, 0]),
        (routes, route_all.at[0, 0]),
        (own_cut(half=place.side, wide=True), down_own.at[pl.ds(0, split)]),
        (own_cut(half=1 - place.side, wide=True), down_own.at[pl.ds(split, split)]),
        *zip(qkv_slices(qkv, place.col), qkv_targets(qkv_here, qkv)),
        *staged,
    )

    def norm(own, far, base):
        own, far = own.astype(jnp.float32), far.astype(jnp.float32)
        total = jnp.sum(own * own, 1, keepdims=True) + jnp.sum(far * far, 1, keepdims=True)
        inv = lax.rsqrt(total / (2 * part) + EPS)
        normed[base : base + rows, :] = (own * inv * gain[...]).astype(jnp.bfloat16)
        normed_far[base : base + rows, :] = (far * inv * gain_far[...]).astype(jnp.bfloat16)
        return inv

    def masks(b):
        allowed[...] = allowed_tile(seg_row[b : b + 1, :], seg_col[:, b : b + 1], False)

    masks(1)
    t.arrived((QKV, X))
    t.start((QKV, Y))
    t.arrived((TOK, X), (GAIN, X))
    t.start((TOK, FAR_C), (COT, X), (ROUTER, X))
    inv = norm(tokens[...], tok[0], 0)
    inv_first[...] = jnp.broadcast_to(inv, inv_first.shape)
    t.arrived((TOK, C), (TOK, FAR_C))
    norm(tok[1], tok[2], rows)
    for k in ks:
        t.arrived((ROUTES, Z, k))
        t.start((ROUTES, C, k))
    t.arrived((COT, Z, 1))
    t.start((COT, C, 1))
    t.arrived((QKV, Y))
    t.start((DOWN, X))

    width = q_ref.shape[1]
    for base in (rows, 0):
        cut = slice(base, base + rows)
        qkv_rows = dot_nn(normed[cut, :], qkv_here[...])
        for i in range(2):
            qkv_rows = qkv_rows + dot_nn(normed_far[cut, halves[i]], qkv_far[i])
        for i in range(width // LANES + 1):
            block = qkv_rows[:, LANES * i : LANES * (i + 1)]
            block = turn(block, cosine[cut, :], sine[cut, :])
            if i < width // LANES:
                q_ref[cut, LANES * i : LANES * (i + 1)] = low(block)
            else:
                keys[0, cut, :] = low(block)
                keys[1, cut, :] = swap_heads(low(block))
        block = low(qkv_rows[:, width + LANES :])
        values[0, cut, :] = block
        values[1, cut, :] = swap_heads(block)
    attend_rows(q_ref, keys, values, allowed, mixed, rows, width // LANES)
    t.start((MIXED, X, 1))
    t.arrived((COT, X))
    t.start((COT, FAR_C, 0), (COT, FAR_Z, 1), (COT, FAR_Z, 2))
    masks(0)
    attend_rows(q_ref, keys, values, allowed, mixed, 0, width // LANES)
    t.start((MIXED, X, 0))
    t.start((COT, FAR_Z, 3))
    t.arrived((COT, Z, 2))
    t.start((COT, C, 2))
    t.arrived((DOWN, X))
    t.start((DOWN, Y))

    def project(base):
        cut = slice(base, base + rows)
        first = pl.ds(pl.multiple_of(place.col * width, LANES), width)
        second = pl.ds(pl.multiple_of((1 - place.col) * width, LANES), width)
        return dot_nn(mixed[cut, :], w_out[first, :]) + dot_nn(mixed_far[cut, :], w_out[second, :])

    def stored(i):
        out = grad_hidden.at[pl.ds(rows * i, rows)]
        return pltpu.make_async_copy(grad_buf.at[i % 2], out, local.at[9 + i % 2])

    def hidden_grads(i):
        k, p = i // 2, i % 2
        if p == 1:
            t.arrived((COT, C, k), (COT, FAR_C, k))
        moves(local, (c_own.at[k, p], own_buf), (c_far.at[k, p], far_buf))
        if i > 1:
            stored(i - 2).wait()
        size = split * LANES
        for n in range(2):
            own_rows = down_own[split * n : split * (n + 1)].reshape(size, part)
            far_rows = down_buf[n].reshape(size, part)
            total = dot_nt(own_buf[...], own_rows) + dot_nt(far_buf[...], far_rows)
            grad_buf[i % 2, :, size * n : size * (n + 1)] = low(RESIDUAL * total)
        stored(i).start()

    t.arrived((MIXED, X, 1))
    give[...] = project(rows)
    t.start((ATTN, C), (GATE, X))
    t.arrived((MIXED, X, 0))
    t.start((UP, X))
    attn = project(0)
    t.arrived((ATTN, C))
    middle = tokens[...].astype(jnp.float32) + RESIDUAL * (attn + got[...])
    middle_ref[...] = middle
    total = jnp.sum(middle * middle, 1, keepdims=True)
    square[...] = jnp.broadcast_to(total, (rows, LANES)).T[:8, :]
    t.start((SQUARE, X))
    t.arrived((DOWN, Y))
    moves(local, (down_got, down_buf.at[0]), (down_other, down_buf.at[1]))
    hidden_grads(0)
    t.arrived((SQUARE, X))
    total = total + jnp.broadcast_to(square_far[:1, :], (LANES, rows)).T[:, :1]
    inv = lax.rsqrt(total / (2 * part) + EPS)
    inv_second[...] = jnp.broadcast_to(inv, inv_second.shape)
    h2_ref[...] = low(middle_ref[...] * inv * gain_moe[...])

    hidden_grads(1)
    t.arrived((COT, FAR_Z, 1))
    t.start((COT, FAR_C, 1))
    hidden_grads(2)
    t.arrived((GATE, X))
    t.start((GATE, Y))
    hidden_grads(3)
    t.arrived((COT, FAR_Z, 2), (COT, Z, 3))
    t.start((COT, FAR_C, 2), (COT, C, 3))
    hidden_grads(4)
    hidden_grads(5)
    t.arrived((COT, FAR_Z, 3))
    t.start((COT, FAR_C, 3))
    stored(EARLY - 2).wait()
    stored(EARLY - 1).wait()
    t.finish()


def front(tokens, cot, w_down, w_gate, w_up, router, routes, qkv, *others):
    rows, part = tokens.shape
    gain, w_out = others[0], others[2]
    vmem = pl.BlockSpec(memory_space=pltpu.VMEM)
    shape = lambda dims, dtype=jnp.bfloat16: jax.ShapeDtypeStruct(dims, dtype)
    like = lambda a: shape(a.shape, a.dtype)
    stack = lambda a: shape((ZPARTS, 2, *a.shape), a.dtype)
    mine = w_down.shape[0] // 2
    width, kv = qkv[0].shape[1] // 2, qkv[1].shape[1] // 2
    down, pair = shape((mine // 2, LANES, part)), shape((mine // 2, part, LANES))
    hbm_outs = [down, down, pair, pair, pair, like(router)]
    hbm_outs += [stack(cot), stack(cot), stack(routes)]
    hbm_outs += [shape((EARLY * rows, mine * LANES))]
    vmem_outs = [
        shape((2 * rows, width)),
        shape((2, 2 * rows, kv)),
        shape((2, 2 * rows, kv)),
        shape((2 * rows, width)),
        shape((2 * rows, width)),
        shape((2 * rows, part)),
        shape((2 * rows, part)),
        shape((rows, LANES), jnp.float32),
        shape((rows, part), jnp.float32),
        shape((rows, LANES), jnp.float32),
        shape((rows, part)),
    ]
    buffer = pltpu.VMEM((rows, part), jnp.bfloat16)
    wide = pltpu.VMEM((rows, part), jnp.float32)
    small = pltpu.VMEM((8, rows), jnp.float32)
    weights = pltpu.VMEM((part, width + 2 * kv), jnp.bfloat16)
    half_weights = pltpu.VMEM((part // 2, width + 2 * kv), jnp.bfloat16)
    count = 15 + 6 * (ZPARTS - 1) + 5 + 2 + 2
    return pl.pallas_call(
        front_kernel,
        out_shape=hbm_outs + vmem_outs,
        in_specs=[vmem] + [ANY] * 9 + [vmem] * len(others),
        out_specs=[ANY] * len(hbm_outs) + [vmem] * len(vmem_outs),
        scratch_shapes=[
            pltpu.VMEM((3, rows, part), jnp.bfloat16),
            weights,
            pltpu.VMEM((2, part // 2, width + 2 * kv), jnp.bfloat16),
            pltpu.VMEM(gain.shape, jnp.float32),
            wide,
            wide,
            small,
            small,
            buffer,
            buffer,
            pltpu.VMEM((mine, LANES, part), jnp.bfloat16),
            pltpu.VMEM((2, mine // 2, LANES, part), jnp.bfloat16),
            pltpu.VMEM((2, rows, mine * LANES), jnp.bfloat16),
            pltpu.VMEM((rows, rows), jnp.float32),
            pltpu.VMEM((2, *pair.shape), jnp.bfloat16),
            half_weights,
            pltpu.SemaphoreType.DMA((2, count)),
            pltpu.SemaphoreType.DMA((11,)),
        ],
        compiler_params=pltpu.CompilerParams(
            collective_id=0, has_side_effects=True, vmem_limit_bytes=58 * 1024 * 1024
        ),
        name="front",
    )(tokens, cot, w_down, w_gate, w_up, router, routes, *qkv, *others)


def moe_kernel(*refs):
    routes_ref, grad_ref, router_own, router_far, h2, c_own, c_far = refs[:7]
    w_gate, w_up, w_down, w_out, gate_got, gate_other, up_got, down_got, down_other = refs[7:16]
    (
        h_own_out,
        h_far_out,
        moe_own,
        moe_far,
        hidden_out,
        slopes_out,
        dlog_ref,
        up_other,
        out_far,
        s0_own,
        z1_own,
        x0_far,
        piece2,
        s3_own,
        s3_far,
    ) = refs[16:31]
    h_own_all, h_far_all, keep_own, keep_far, give_own, give_far, got_own, got_far = refs[31:39]
    got_x, z1_far, pair_own, pair_far, down_own, down_far, hidden_ref, slopes_ref = refs[39:47]
    grad_late, sems, local, fill, save = refs[47:]
    experts = down_own.shape[0]
    split = experts // 2
    rows, part = h2.shape
    place = Place()
    step = pl.program_id(0)
    t = Transfers(sems)
    x, c = place.x(), place.c()
    z = [None] + [place.z(k) for k in range(1, ZPARTS)]
    t.add((H, X), h2, h_far_all.at[0, 0], x)
    t.add((H, C, 0), h2, h_own_all.at[0, 1], c)
    t.add((H, FAR_C, 0), h_far_all.at[0, 0], h_far_all.at[0, 1], c)
    for k in range(1, ZPARTS):
        t.add((H, Z, k), h2, h_own_all.at[k, 0], z[k])
        if k == 1:
            t.add((H, FAR_X, 1), h_far_all.at[0, 0], h_far_all.at[1, 0], z[1])
        else:
            t.add((H, FAR_X, k), h_own_all.at[k, 0], h_far_all.at[k, 0], x)
        t.add((H, C, k), h_own_all.at[k, 0], h_own_all.at[k, 1], c)
        t.add((H, FAR_C, k), h_far_all.at[k, 0], h_far_all.at[k, 1], c)
    for k in range(ZPARTS):
        t.add((BACK, C, k), give_own, got_own.at[k], c)
        t.add((BACK, FAR_C, k), give_far, got_far.at[k], c)
    t.add((BACK, Z), got_own.at[1], z1_own, z[1])
    t.add((BACK, FAR_Z), got_far.at[1], z1_far, z[1])
    t.add((BACK, FAR_X), got_far.at[2], got_x, x)
    t.add((BACK, X), got_far.at[0], x0_far, x)
    t.add((UP, Y), up_got, up_other, place.y())
    width = out_far.shape[0]
    there = pl.ds(pl.multiple_of((1 - place.col) * width, LANES), width)
    t.add((OUT, X), w_out.at[there], out_far, x)

    def join(k):
        for name in ((BACK, C, k), (BACK, FAR_C, k)):
            t.copy(name).wait_send()
        t.arrived((BACK, C, k), (BACK, FAR_C, k))
        for got, keep in ((got_own, keep_own), (got_far, keep_far)):
            total = got[k].astype(jnp.float32) + keep[...].astype(jnp.float32)
            got[k] = total.astype(jnp.bfloat16)

    @pl.when(step == 0)
    def _():
        greet([x, c, place.y(), *z[1:]])
        t.start((H, X), (H, C, 0), (UP, Y), (H, Z, 1), (H, Z, 2))
        cut = functools.partial(weight_slice, which=place.col, split=split, zed=place.zed)
        fills, late = [], []
        for i, half in enumerate((place.side, 1 - place.side)):
            gates = (cut(w_gate, half=half, wide=False), (gate_got, gate_other)[i])
            ups = (cut(w_up, half=half, wide=False), (up_got, up_other)[i])
            downs = (cut(w_down, half=half, wide=True), (down_got, down_other)[i])
            for n, (pair, down) in enumerate(((pair_own, down_own), (pair_far, down_far))):
                for e in range(split):
                    for m, src in enumerate((gates[n], ups[n])):
                        cols = pl.ds(LANES * (2 * e + m), LANES)
                        into = late if src is up_other else fills
                        into.append((src.at[e], pair.at[i, :, cols]))
                fills.append((downs[n], down.at[pl.ds(split * i, split)]))
        moves(fill, (h2, h_own_all.at[0, 0]), *fills)

        def hidden_grads(i):
            k, p = (EARLY + i) // 2, (EARLY + i) % 2
            moves(local, (c_own.at[k, p], give_own), (c_far.at[k, p], give_far))
            total = dot_nt(give_own[...], down_own[...].reshape(-1, part))
            total = total + dot_nt(give_far[...], down_far[...].reshape(-1, part))
            grad_late[i] = low(RESIDUAL * total)

        for i in range(ZPARTS - EARLY // 2):
            hidden_grads(i)
        t.arrived((H, X))
        t.start((H, FAR_C, 0), (H, FAR_X, 1))
        for i in range(ZPARTS - EARLY // 2, 2 * ZPARTS - EARLY):
            hidden_grads(i)
        t.arrived((UP, Y))
        moves(fill, *late)

    @pl.when(step == 1)
    def _():
        t.arrived((H, C, 0), (H, FAR_C, 0), (H, Z, 1))
        t.start((H, C, 1), (OUT, X))

    @pl.when(step == 2)
    def _():
        t.start((H, Z, 3))
        t.arrived((H, FAR_X, 1))
        t.start((H, FAR_C, 1))
        join(0)
        t.arrived((H, Z, 2))
        t.start((H, FAR_X, 2), (H, C, 2))

    @pl.when(step == 3)
    def _():
        t.arrived((H, C, 1), (H, FAR_C, 1))

    @pl.when(step == 4)
    def _():
        join(1)
        t.start((BACK, Z), (BACK, FAR_Z))
        t.arrived((H, FAR_X, 2))
        t.start((H, FAR_C, 2))
        t.arrived((H, Z, 3))
        t.start((H, FAR_X, 3), (H, C, 3))

    @pl.when(step == 5)
    def _():
        t.arrived((H, C, 2), (H, FAR_C, 2))

    @pl.when(step == 6)
    def _():
        join(2)
        t.start((BACK, FAR_X))
        t.arrived((H, FAR_X, 3))
        t.start((H, FAR_C, 3))

    @pl.when(step == 7)
    def _():
        t.arrived((H, C, 3), (H, FAR_C, 3))
        t.arrived((BACK, FAR_X))
        got_own[2] = low(add_wide(got_own[2], got_x[...]))
        t.arrived((BACK, FAR_Z))
        got_far[0] = low(add_wide(got_far[0], z1_far[...]))
        t.start((BACK, X))

    def saved(i):
        k, p = i // 2, i % 2
        pairs = ((h_own_all, h_own_out), (h_far_all, h_far_out))
        return [
            pltpu.make_async_copy(src.at[k, p], dst.at[k, p], save.at[n, i])
            for n, (src, dst) in enumerate(pairs)
        ]

    def written(i):
        cut = pl.ds(rows * i, rows)
        return [
            pltpu.make_async_copy(src, dst.at[cut], save.at[2 + n, i])
            for n, (src, dst) in enumerate(((hidden_ref, hidden_out), (slopes_ref, slopes_out)))
        ]

    for i in range(2 * ZPARTS):

        @pl.when(step == i)
        def _():
            for copy in saved(i):
                copy.start()
            if i > 0:
                for copy in written(i - 1):
                    copy.wait()

    h_own, h_far = h_own_all.at[step // 2, step % 2], h_far_all.at[step // 2, step % 2]

    first = (place.core * 2 + place.col) * experts
    lane = lax.broadcasted_iota(jnp.int32, (rows, LANES), 1)
    chosen = lane == routes_ref[:, 0:1]
    for k in range(1, routes_ref.shape[1]):
        chosen = chosen | (lane == routes_ref[:, k : k + 1])
    logits = dot_nn(h_own[...], router_own[...]) + dot_nn(h_far[...], router_far[...])
    peak = jnp.max(jnp.where(chosen, logits, -jnp.inf), axis=1, keepdims=True)
    expo = jnp.where(chosen, jnp.exp(logits - peak), 0.0)
    gates = expo / jnp.sum(expo, axis=1, keepdims=True)
    grad_gates = jnp.zeros((rows, LANES), jnp.float32)
    at_late = jnp.maximum(step - EARLY, 0)
    for e in range(experts):
        here = lane == first + (e + place.side * split) % experts
        gate = jnp.sum(jnp.where(here, gates, 0.0), axis=1, keepdims=True)
        cols = slice(2 * LANES * (e % split), 2 * LANES * (e % split + 1))
        pair = dot_nn(h_own[...], pair_own[e // split, :, cols]) + dot_nn(
            h_far[...], pair_far[e // split, :, cols]
        )
        cut = slice(LANES * e, LANES * (e + 1))
        slope = jnp.where(step < EARLY, grad_ref[:, cut], grad_late[at_late, :, cut])
        slope = slope.astype(jnp.float32)
        gate_val = pair[:, :LANES]
        up_val = pair[:, LANES:]
        sigma = jax.nn.sigmoid(gate_val)
        silu = gate_val * sigma
        hidden = silu * up_val
        dgate = jnp.sum(hidden * slope, axis=1, keepdims=True)
        grad_gates = jnp.where(here, dgate, grad_gates)
        dz = gate * slope
        hidden_ref[:, LANES * e : LANES * (e + 1)] = (gate * hidden).astype(jnp.bfloat16)
        slopes_ref[:, 2 * LANES * e : 2 * LANES * e + LANES] = (
            dz * up_val * (sigma + silu * (1.0 - sigma))
        ).astype(jnp.bfloat16)
        slopes_ref[:, 2 * LANES * e + LANES : 2 * LANES * (e + 1)] = (dz * silu).astype(
            jnp.bfloat16
        )
    dlog = gates * (grad_gates - jnp.sum(gates * grad_gates, axis=1, keepdims=True))
    dlog_high = dlog.astype(jnp.bfloat16)
    dlog_low = (dlog - dlog_high.astype(jnp.float32)).astype(jnp.bfloat16)
    dlog_ref[:, :LANES] = dlog_high
    dlog_ref[:, LANES:] = dlog_low

    def back(pairs, router):
        total = dot_nt(dlog_high, router[...]) + dot_nt(dlog_low, router[...])
        for i in range(2):
            cols = slice(2 * LANES * split * i, 2 * LANES * split * (i + 1))
            total = total + dot_nt(slopes_ref[:, cols], pairs[i])
        return total.astype(jnp.bfloat16)

    back_own, back_far = back(pair_own, router_own), back(pair_far, router_far)
    last = pl.num_programs(0) - 1

    @pl.when(step % 2 == 0)
    def _():
        keep_own[...] = back_own
        keep_far[...] = back_far

    @pl.when(step % 2 == 1)
    def _():
        give_own[...] = back_own
        give_far[...] = back_far

    for k in range(ZPARTS):

        @pl.when(step == 2 * k + 1)
        def _():
            t.start((BACK, C, k), (BACK, FAR_C, k))

    for i in range(2 * ZPARTS):

        @pl.when(step == i)
        def _():
            for copy in written(i):
                copy.start()

    moe_own[...] = low(dot_nn(hidden_ref[...], down_own[...].reshape(-1, part)))
    moe_far[...] = low(dot_nn(hidden_ref[...], down_far[...].reshape(-1, part)))

    @pl.when(step == last)
    def _():
        join(ZPARTS - 1)
        moves(
            local,
            (got_own.at[0], s0_own),
            (got_own.at[2], piece2),
            (got_own.at[3], s3_own),
            (got_far.at[3], s3_far),
        )
        for copy in written(2 * ZPARTS - 1):
            copy.wait()
        for i in range(2 * ZPARTS):
            for copy in saved(i):
                copy.wait()
        t.finish(*[(BACK, hop, k) for hop in (C, FAR_C) for k in range(ZPARTS)])


def moe_layer(routes, grad_hidden, routers, h2, c_rows, weights, up_got, width):
    tile, part = h2.shape
    rows = routes.shape[0]
    experts = grad_hidden.shape[1] // LANES
    by_row = lambda width: pl.BlockSpec((tile, width), lambda i: (i, 0))
    stack = jax.ShapeDtypeStruct((ZPARTS, 2, tile, part), jnp.bfloat16)
    one = jax.ShapeDtypeStruct((tile, part), jnp.bfloat16)
    widths = [part, part, experts * LANES, 2 * experts * LANES, 2 * LANES]
    buffer = pltpu.VMEM((tile, part), jnp.bfloat16)
    stacked = pltpu.VMEM((ZPARTS, tile, part), jnp.bfloat16)
    pieces = pltpu.VMEM((ZPARTS, 2, tile, part), jnp.bfloat16)
    pair = pltpu.VMEM((2, part, experts * LANES), jnp.bfloat16)
    down = pltpu.VMEM((experts, LANES, part), jnp.bfloat16)
    extra = [like_of(up_got), jax.ShapeDtypeStruct((width, part), jnp.bfloat16)]
    count = 3 + 4 * (ZPARTS - 1) + 2 * ZPARTS + 6
    return pl.pallas_call(
        moe_kernel,
        out_shape=[stack, stack]
        + [jax.ShapeDtypeStruct((rows, w), jnp.bfloat16) for w in widths]
        + extra
        + [one] * 6,
        grid=(rows // tile,),
        in_specs=[
            by_row(routes.shape[1]),
            pl.BlockSpec((tile, experts * LANES), lambda i: (jnp.minimum(i, EARLY - 1), 0)),
        ]
        + [whole_block(r) for r in routers]
        + [ANY] * (3 + len(weights)),
        out_specs=[ANY, ANY, by_row(part), by_row(part), ANY, ANY, by_row(2 * LANES)]
        + [ANY] * 8,
        scratch_shapes=[pieces] * 2
        + [buffer] * 4
        + [stacked] * 2
        + [buffer, buffer, pair, pair, down, down]
        + [pltpu.VMEM((tile, w), jnp.bfloat16) for w in widths[2:4]]
        + [pltpu.VMEM((2 * ZPARTS - EARLY, tile, widths[2]), jnp.bfloat16)]
        + [
            pltpu.SemaphoreType.DMA((2, count)),
            pltpu.SemaphoreType.DMA((5,)),
            pltpu.SemaphoreType.DMA((5 + 4 * experts,)),
            pltpu.SemaphoreType.DMA((4, 2 * ZPARTS)),
        ],
        compiler_params=pltpu.CompilerParams(
            collective_id=1, has_side_effects=True, vmem_limit_bytes=63 * 1024 * 1024
        ),
        name="moe_layer",
    )(routes, grad_hidden, *routers, h2, *c_rows, *weights)


def weight_kernel(cargo, streamed, *refs):
    n_cargo = len(cargo)
    h_own, h_far, c_own, c_far, hidden, slopes = refs[:6]
    sources = refs[6 : 6 + n_cargo]
    keep_own, keep_far, give_own, rest_far = refs[6 + n_cargo : 10 + n_cargo]
    landed = refs[10 + n_cargo : 10 + 2 * n_cargo]
    if streamed:
        far_land = refs[10 + 2 * n_cargo]
    give_far, sems, local = refs[-3:]
    place = Place()
    step = pl.program_id(0)
    t = Transfers(sems)
    partners = {X: place.x(), Y: place.y(), C: place.c()}
    partners.update({(Z, k): place.z(k) for k in range(1, ZPARTS)})
    to = {name: partners[name] for name, _ in cargo}
    for i, (name, views) in enumerate(cargo):
        for n, view in enumerate(views):
            t.add((i, n), sources[i].at[view], landed[i].at[n], to[name])
    first_keys = list(t.table)
    for e in range(streamed):
        t.add((GRADS, e), give_far.at[e], far_land.at[e], partners[Y])
    if streamed:
        to[Y] = partners[Y]

    @pl.when(step == 0)
    def _():
        greet(list(to.values()))
        t.start(*first_keys)

    half = LANES // 2
    tile = h_own.shape[2]
    first = place.side == 0
    for keep, give, at, rows_h, rows_c in (
        (keep_far, give_far, step, h_far, c_far),
        (keep_own, give_own, 0, h_own, c_own),
    ):
        pair, down = 0.0, 0.0
        for i in range(2 * ZPARTS):
            rows = slice(tile * i, tile * (i + 1))
            pair = pair + dot_tn(slopes[rows, :], rows_h[i // 2, i % 2])
            down = down + dot_tn(hidden[rows, :], rows_c[i // 2, i % 2])
        for i, block in enumerate((pair[:LANES], pair[LANES:], RESIDUAL * down)):
            begin, end = block[:half], block[half:]
            cut = slice(half * i, half * (i + 1))
            keep[0, cut, :] = jnp.where(first, begin, end)
            give[at, cut, :] = low(jnp.where(first, end, begin))
        if keep is keep_far:
            for e in range(streamed):

                @pl.when(step == e)
                def _():
                    t.start((GRADS, e))

    @pl.when(step == pl.num_programs(0) - 1)
    def _():
        rest = rest_far.shape[0]
        moves(local, (give_far.at[pl.ds(streamed, rest)], rest_far))
        t.finish()


def weight_grads(number, start, count, streamed, resident, hidden, slopes, cargo):
    part = resident[0].shape[-1]
    rows = hidden.shape[0]
    out = pl.BlockSpec((1, 3 * LANES // 2, part), lambda e: (e, 0, 0))
    block = (3 * LANES // 2, part)
    shape = (count, *block)
    arrays = [array for _, array, _ in cargo]
    views = tuple((name, tuple(where)) for name, _, where in cargo)
    landed = []
    for _, array, where in cargo:
        dims = (len(where), *array.shape[len(where[0]) :])
        landed.append(jax.ShapeDtypeStruct(dims, array.dtype))
    rest = jax.ShapeDtypeStruct((count - streamed, *block), jnp.bfloat16)
    if streamed:
        landed.append(jax.ShapeDtypeStruct((streamed, *block), jnp.bfloat16))
    transfers = sum(len(where) for _, _, where in cargo) + streamed
    return pl.pallas_call(
        functools.partial(weight_kernel, views, streamed),
        out_shape=[jax.ShapeDtypeStruct(shape, jnp.float32)] * 2
        + [jax.ShapeDtypeStruct(shape, jnp.bfloat16), rest]
        + landed,
        grid=(count,),
        in_specs=[whole_block(a) for a in resident]
        + [
            pl.BlockSpec((rows, LANES), lambda e: (0, e + start)),
            pl.BlockSpec((rows, 2 * LANES), lambda e: (0, e + start)),
        ]
        + [ANY] * len(arrays),
        out_specs=[out] * 3 + [ANY] * (1 + len(landed)),
        scratch_shapes=[
            pltpu.VMEM(shape, jnp.bfloat16),
            pltpu.SemaphoreType.DMA((2, transfers)),
            pltpu.SemaphoreType.DMA((1,)),
        ],
        compiler_params=pltpu.CompilerParams(
            collective_id=2 + number, has_side_effects=True, vmem_limit_bytes=60 * 1024 * 1024
        ),
        name="expert_weight_grads",
    )(*resident, hidden, slopes, *arrays)


def unturn(block, cosine, sine):
    return block * cosine + turn(block, jnp.zeros_like(cosine), -sine)


def attend_back_rows(
    q_ref, keys_ref, values_ref, grad_ref, allowed_ref, out_ref, dk, dv, cosine, sine, base, blocks
):
    rows = allowed_ref.shape[0]
    dk[...] = jnp.zeros_like(dk)
    dv[...] = jnp.zeros_like(dv)

    def body(j, carry):
        cols = pl.ds(pl.multiple_of(j * LANES, LANES), LANES)
        for start, stop, keys in score_tiles(rows):
            cut = slice(base + start, base + stop)
            lane = lax.broadcasted_iota(jnp.int32, (stop - start, LANES), 1)
            query, grad = q_ref[cut, cols], grad_ref[cut, cols]
            allowed = allowed_ref[:keys, start:stop] > 0
            dqs = []
            for side, part in enumerate((lane < HEAD_WIDTH, lane >= HEAD_WIDTH)):
                other = (2 * j + side) // blocks
                other = other + side - 2 * other * side
                key_rows = keys_ref[other, base : base + keys, :]
                value_rows = values_ref[other, base : base + keys, :]
                one_query = jnp.where(part, query, jnp.zeros_like(query))
                one_grad = jnp.where(part, grad, jnp.zeros_like(grad))
                scores = jnp.where(allowed, dot_nt(key_rows, one_query) * SCORE_SCALE, NEG)
                expo = jnp.exp(scores - jnp.max(scores, axis=0, keepdims=True))
                probs = expo * (1.0 / jnp.sum(expo, axis=0, keepdims=True))
                slope = dot_nt(value_rows, one_grad)
                delta = jnp.sum(probs * slope, axis=0, keepdims=True)
                dscore = low(probs * (slope - delta))
                dv[other, :keys, :] = dv[other, :keys, :] + dot_nn(low(probs), one_grad)
                dk[other, :keys, :] = dk[other, :keys, :] + dot_nn(dscore, one_query)
                dqs.append(dot_tn(dscore, key_rows))
            dq = jnp.where(lane < HEAD_WIDTH, dqs[0], dqs[1]) * SCORE_SCALE
            out_ref[cut, cols] = low(unturn(dq, cosine[cut, :], sine[cut, :]))
        return carry

    lax.fori_loop(0, blocks, body, 0)
    cut = slice(base, base + rows)
    width = blocks * LANES
    total = (dk[0] + pltpu.roll(dk[1], HEAD_WIDTH, 1)) * SCORE_SCALE
    out_ref[cut, width : width + LANES] = low(unturn(total, cosine[cut, :], sine[cut, :]))
    out_ref[cut, width + LANES :] = low(dv[0] + pltpu.roll(dv[1], HEAD_WIDTH, 1))


class WholeSum:
    def __init__(self, t, name, ref, levels, stages, lands, swap=None):
        self.t, self.name, self.ref = t, name, ref
        self.stages, self.lands, self.count = stages, lands, len(levels)
        offset, rows = 0, ref.shape[0]
        self.kept, self.other = [], []
        ways = []
        for i, (partner, bit) in enumerate(levels):
            rows = rows // 2
            self.other.append((offset + (1 - bit) * rows, rows))
            offset = offset + bit * rows
            self.kept.append((offset, rows))
            ways.append((i, i, self.other[i], self.kept[i], partner))
        last = self.count - 1
        back = [
            (i, self.count + i, self.kept[i], self.other[i], levels[i][0])
            for i in range(last, -1, -1)
        ]
        if swap is not None:
            ways.append((last, 2 * self.count, self.kept[last], self.kept[last], swap))
        self.ways = ways + back
        for i, (stage, land, _, _, partner) in enumerate(self.ways):
            t.add((SUM, name, i), stages[stage], lands[land], partner)

    def rows(self, place):
        return pl.ds(pl.multiple_of(place[0], 8), place[1])

    def send(self, i):
        stage, _, place, _, _ = self.ways[i]
        for j in range(i - 1, -1, -1):
            if self.ways[j][0] == stage:
                self.t.sent((SUM, self.name, j))
                break
        self.stages[stage][...] = low(self.ref[self.rows(place), :])
        self.t.start((SUM, self.name, i))

    def land(self, i):
        self.t.arrived((SUM, self.name, i))
        _, land, _, place, _ = self.ways[i]
        cut = self.rows(place)
        total = self.lands[land][...].astype(jnp.float32)
        if i < self.count:
            total = self.ref[cut, :] + total
            if i == self.count - 1:
                total = low(total).astype(jnp.float32)
        self.ref[cut, :] = total

    def next(self, i):
        if 0 <= i < len(self.ways):
            self.land(i)
            if i + 1 < len(self.ways):
                self.send(i + 1)

    def keys(self):
        done = []
        for i, way in enumerate(self.ways):
            if any(later[0] == way[0] for later in self.ways[i + 1 :]):
                done.append((SUM, self.name, i))
        return done


class SmallSum:
    def __init__(self, t, name, ref, partners, lands):
        self.t, self.name, self.ref, self.lands = t, name, ref, lands
        for i, partner in enumerate(partners):
            t.add((SMALL, name, i), ref, lands.at[i], partner)

    def send(self, i):
        self.t.start((SMALL, self.name, i))

    def land(self, i):
        self.t.sent((SMALL, self.name, i))
        self.t.arrived((SMALL, self.name, i))
        self.ref[...] = self.ref[...] + self.lands[i]

    def next(self, i):
        if 0 <= i < self.lands.shape[0]:
            self.land(i)
            if i + 1 < self.lands.shape[0]:
                self.send(i + 1)

    def keys(self):
        return [(SMALL, self.name, i) for i in range(self.lands.shape[0])]


SUMMED = 40


def back_kernel(count, with_grads, *refs):
    refs = list(refs)
    take = lambda n: [refs.pop(0) for _ in range(n)]
    qkv = take(3)
    moe_srcs = take(4)
    tokens, cot, middle, inv_first, inv_second, gain, gain_moe = take(7)
    parts = take(5)
    q_ref, keys, values, mixed, mixed_far, normed, normed_far = take(7)
    cosine, sine, seg_row, seg_col = take(4)
    w_out, out_far, small_own, small_there = take(4)
    if with_grads:
        grad_srcs, keep_first = take(3), take(1)[0]
    moe_lands = take(4)
    if with_grads:
        grad_lands = take(3)
    grad_tokens, grad_q, grad_k, grad_v, grad_out, small, small_last = take(7)
    qkv_here, qkv_there, da_own, da_far, grad_mixed, dqkv, dqkv_far, give, got = take(9)
    grad_middle, grad_here, grad_there, allowed, dk, dv, square, square_far = take(8)
    small_land, small_lands, last_lands = take(3)
    stages, lands = [], []
    for _ in range(3):
        stages.append(take(count))
        lands.append(take(2 * count + 1))
    if with_grads:
        first_land, first_sum = take(2)
    sems, local = take(2)
    place = Place()
    t = Transfers(sems)
    x, c, y = place.x(), place.c(), place.y()
    rows, part = tokens.shape
    width = q_ref.shape[1]
    low_levels, high_levels = place.bits()
    partners = [partner for partner, _ in low_levels + high_levels]
    t.add((INNER, 0), square.at[0], square_far.at[0], x)
    t.add((INNER, 1), square.at[1], square_far.at[1], x)
    t.add((SMALL, X), small_there, small_land, x)
    first, second = pl.ds(0, rows), pl.ds(rows, rows)
    t.add((DA, X), da_own.at[first], da_far.at[first], x)
    t.add((DA, C), da_own.at[first], da_own.at[second], c)
    t.add((DA, FAR_C), da_far.at[first], da_far.at[second], c)
    for i, cut in enumerate((first, second)):
        t.add((DQKV, i), dqkv.at[cut], dqkv_far.at[cut], x)
    t.add((ATTN, C), give, got, c)
    for i, partner in enumerate((place.z(1), place.z(2), place.z(3), x)):
        t.add((MOE, i), moe_srcs[i], moe_lands[i], partner)
    if with_grads:
        t.add((GRADS, Y, 0), grad_srcs[0], first_land, y)
        t.add((GRADS, Y, 1), grad_srcs[1], grad_lands[0], y)
        t.add((GRADS, X, 0), grad_srcs[2], grad_lands[1], x)
        t.add((GRADS, X, 1), first_sum, grad_lands[2], x)
    levels = low_levels + high_levels
    sum_out = WholeSum(t, 0, grad_out, levels, stages[0], lands[0])
    sum_here = WholeSum(t, 1, grad_here, levels, stages[1], lands[1])
    sum_there = WholeSum(t, 2, grad_there, levels, stages[2], lands[2], x)
    small_sum = SmallSum(t, 0, small, [c] + partners, small_lands)
    last_sum = SmallSum(t, 1, small_last, [c] + partners, last_lands)

    greet([x, c, place.z(3)] + partners)
    t.start((SMALL, X), (MOE, 1), (MOE, 2))
    if with_grads:
        t.start((GRADS, Y, 0))
    here, there = qkv_slices(qkv, place.col), qkv_slices(qkv, 1 - place.col)
    targets = [*qkv_targets(qkv_here, qkv), *qkv_targets(qkv_there, qkv)]
    moves(local, *zip([*here, *there], targets))

    def masks(b):
        allowed[...] = allowed_tile(seg_row[b : b + 1, :], seg_col[:, b : b + 1], True)

    def exchange_sum(i, total):
        square[i] = jnp.broadcast_to(total, (rows, LANES)).T[:8, :]
        t.start((INNER, i))

    def exchanged(i, total):
        t.arrived((INNER, i))
        return total + jnp.broadcast_to(square_far[i, :1, :], (LANES, rows)).T[:, :1]

    def norm_back(grad, value, inv, gain_row, inner):
        return inv * (grad * gain_row) - value * (inv * inv * inv * inner / (2 * part))

    grad = add_wide(*[p[...] for p in parts])
    inv = inv_second[:, :1]
    inner = jnp.sum(middle[...] * grad * gain_moe[...], 1, keepdims=True)
    exchange_sum(0, inner)
    small[...] = small_own[...]
    small[SUMMED : SUMMED + 1, :] = jnp.sum(grad * middle[...] * inv, 0, keepdims=True)
    inner = exchanged(0, inner)
    total = cot[...].astype(jnp.float32)
    total = total + norm_back(grad, middle[...], inv, gain_moe[...], inner)
    grad_middle[...] = total
    da_own[:rows, :] = low(RESIDUAL * total)
    t.start((DA, X), (DA, C))
    masks(1)
    t.arrived((SMALL, X))
    small[...] = small[...] + small_land[...]
    small_sum.send(0)
    t.arrived((DA, C))
    at_here = pl.ds(pl.multiple_of(place.col * width, LANES), width)
    at_there = pl.ds(pl.multiple_of((1 - place.col) * width, LANES), width)
    grad_out[at_here, :] = dot_tn(mixed[...], da_own[...])
    grad_out[at_there, :] = dot_tn(mixed_far[...], da_own[...])
    sum_out.send(0)
    small_sum.next(0)
    t.arrived((DA, X))
    t.start((DA, FAR_C))
    if with_grads:
        t.start((GRADS, X, 0))

    def mixed_back(cut):
        total = dot_nt(da_own[cut, :], w_out[at_here, :]) + dot_nt(da_far[cut, :], out_far[...])
        grad_mixed[cut, :] = low(total)

    mixed_back(slice(0, rows))
    t.arrived((DA, FAR_C))
    mixed_back(slice(rows, 2 * rows))
    attend = functools.partial(
        attend_back_rows, q_ref, keys, values, grad_mixed, allowed, dqkv, dk, dv, cosine, sine
    )
    attend(rows, width // LANES)
    t.start((DQKV, 1))
    sum_out.next(0)
    small_sum.next(1)
    if with_grads:
        t.arrived((GRADS, Y, 0))
        t.start((GRADS, Y, 1))
        first_sum[...] = low(keep_first[...] + first_land[...].astype(jnp.float32))
    t.start((MOE, 0))
    masks(0)
    attend(0, width // LANES)
    t.start((DQKV, 0))
    grad_here[...] = dot_tn(normed[...], dqkv[...])
    sum_here.send(0)
    grad_there[...] = dot_tn(normed_far[...], dqkv[...])
    sum_there.send(0)
    sum_out.next(1)
    t.arrived((DQKV, 1))

    def tokens_back(cut):
        return dot_nt(dqkv[cut, :], qkv_here[...]) + dot_nt(dqkv_far[cut, :], qkv_there[...])

    give[...] = tokens_back(slice(rows, 2 * rows))
    t.start((ATTN, C))
    sum_here.next(0)
    sum_there.next(0)
    sum_out.next(2)
    small_sum.next(2)
    t.arrived((DQKV, 0))
    if with_grads:
        t.start((GRADS, X, 1))
    grad = tokens_back(slice(0, rows))
    t.arrived((ATTN, C))
    grad = grad + got[...]
    got[...] = grad
    value = tokens[...].astype(jnp.float32)
    inv = inv_first[:, :1]
    inner = jnp.sum(value * grad * gain[...], 1, keepdims=True)
    exchange_sum(1, inner)
    small_last[...] = jnp.zeros_like(small_last)
    small_last[0:1, :] = jnp.sum(grad * value * inv, 0, keepdims=True)
    last_sum.send(0)
    sum_here.next(1)
    sum_there.next(1)
    sum_out.next(3)
    inner = exchanged(1, inner)
    t.start((MOE, 3))
    grad = norm_back(got[...], tokens[...].astype(jnp.float32), inv, gain[...], inner)
    grad_tokens[...] = grad_middle[...] + grad
    last_sum.next(0)
    for i in range(2, 2 * count + 1):
        sum_here.next(i)
        sum_there.next(i)
        sum_out.next(i + 2)
        small_sum.next(i + 1)
        last_sum.next(i - 1)
    for i in range(2 * count, small_lands.shape[0]):
        small_sum.next(i + 1)
        last_sum.next(i)
    start = 0
    for out in (grad_q, grad_k, grad_v):
        size = out.shape[1] // 2
        cut = slice(start, start + size)
        out[:, pl.ds(pl.multiple_of(place.col * size, LANES), size)] = grad_here[:, cut]
        out[:, pl.ds(pl.multiple_of((1 - place.col) * size, LANES), size)] = grad_there[:, cut]
        start += size
    done = [key for each in (sum_out, sum_here, sum_there, small_sum, last_sum) for key in each.keys()]
    t.finish(*done)


def back(levels, qkv, moe_srcs, vmem_ins, grads):
    tokens, middle, q = vmem_ins[0], vmem_ins[2], vmem_ins[12]
    w_out, small_own = vmem_ins[23], vmem_ins[25]
    rows, part = tokens.shape
    width, kv = q.shape[1], qkv[1].shape[1] // 2
    both = width + 2 * kv
    vmem = pl.BlockSpec(memory_space=pltpu.VMEM)
    bf16, f32 = jnp.bfloat16, jnp.float32
    shape = jax.ShapeDtypeStruct
    like = lambda a: shape(a.shape, a.dtype)
    hbm_outs = [like(a) for a in moe_srcs]
    extra_ins, extra_specs, extra_scratch = [], [], []
    if grads:
        extra_ins = list(grads)
        extra_specs = [ANY] * 3 + [vmem]
        hbm_outs += [like(a) for a in (*grads[1:3], grads[0])]
        extra_scratch = [pltpu.VMEM(grads[0].shape, bf16)] * 2
    small_last = shape((8, part), f32)
    vmem_outs = [shape((rows, part), f32)]
    vmem_outs += [shape((part, w.shape[1]), f32) for w in qkv]
    vmem_outs += [shape(w_out.shape, f32), like(small_own), small_last]
    twice = lambda w, dtype=bf16: pltpu.VMEM((2 * rows, w), dtype)
    wide = pltpu.VMEM((rows, part), f32)
    pair = pltpu.VMEM((2, rows, LANES), f32)
    flat = pltpu.VMEM((2, 8, rows), f32)
    scratch = [pltpu.VMEM((part, both), bf16)] * 2
    scratch += [twice(part), twice(part), twice(width), twice(both), twice(both), wide, wide]
    scratch += [wide, pltpu.VMEM((part, both), f32), pltpu.VMEM((part, both), f32)]
    scratch += [pltpu.VMEM((rows, rows), f32), pair, pair, flat, flat]
    scratch += [pltpu.VMEM(small_own.shape, f32)]
    scratch += [pltpu.VMEM((levels + 1, *small_own.shape), f32)]
    scratch += [pltpu.VMEM((levels + 1, 8, part), f32)]
    for high, wide_cols in ((w_out.shape[0], part), (part, both), (part, both)):
        sizes = [pltpu.VMEM((high >> (i + 1), wide_cols), bf16) for i in range(levels)]
        scratch += sizes * 3 + sizes[-1:]
    scratch += extra_scratch
    count = 9 + 4 + 4 + 3 * 2 * levels + 1 + 2 * (levels + 1)
    scratch += [pltpu.SemaphoreType.DMA((2, count)), pltpu.SemaphoreType.DMA((6,))]
    return pl.pallas_call(
        functools.partial(back_kernel, levels, bool(grads)),
        out_shape=hbm_outs + vmem_outs,
        in_specs=[ANY] * (len(qkv) + len(moe_srcs)) + [vmem] * len(vmem_ins) + extra_specs,
        out_specs=[ANY] * len(hbm_outs) + [vmem] * len(vmem_outs),
        scratch_shapes=scratch,
        compiler_params=pltpu.CompilerParams(
            collective_id=4, has_side_effects=True, vmem_limit_bytes=63 * 1024 * 1024
        ),
        name="back",
    )(*qkv, *moe_srcs, *vmem_ins, *extra_ins)


def halve(value, index, mask, axis):
    first, last = jnp.split(value, 2, axis)
    upper = (index & mask) != 0
    send = low(jnp.where(upper, first, last))
    return jnp.where(upper, last, first) + flip(send, "dp", mask).astype(jnp.float32)


def on_device(
    tokens,
    gain_attn,
    w_query,
    key_matrix,
    value_matrix,
    w_out,
    gain_moe,
    w_router,
    w_gate,
    w_up,
    w_down,
    segments,
    routes,
    cotangent,
):
    col = lax.axis_index("col")
    core = lax.axis_index("expert")
    group = lax.axis_index("dp")
    dp_size = lax.axis_size("dp")
    step = dp_size // ZPARTS
    member = group % step
    levels = dp_size.bit_length() - 1
    half_mask = step // 2
    side = (member // half_mask) % 2

    local, part, ffn = w_gate.shape
    split = local // 4
    units = ffn // ZPARTS
    experts = local * lax.axis_size("expert")
    rows = tokens.shape[0]
    width = w_query.shape[1] // 2

    router_own = jnp.pad(w_router, ((0, 0), (0, LANES - experts)))
    seg_rows = jnp.where(core == 0, segments, segments[::-1])
    positions = jax.vmap(doc_positions)(seg_rows).reshape(-1, 1).astype(jnp.float32)
    half = HEAD_WIDTH // 2
    slot = jnp.arange(LANES, dtype=jnp.int32)
    freq = jnp.exp((slot % half).astype(jnp.float32) * (-2.0 * math.log(THETA) / HEAD_WIDTH))
    sign = jnp.where(slot % HEAD_WIDTH < half, -1.0, 1.0)
    cosine, sine = jnp.cos(positions * freq), jnp.sin(positions * freq) * sign
    qkv = [w_query, key_matrix, value_matrix]
    gain, gain_second = gain_attn[None], gain_moe[None]
    (
        down_got,
        down_other,
        gate_got,
        gate_other,
        up_got,
        router_far,
        c_own,
        c_far,
        route_all,
        grad_hidden,
        q,
        keys,
        values,
        mixed,
        mixed_far,
        normed,
        normed_far,
        inv_first,
        middle,
        inv_second,
        h2,
    ) = front(
        tokens,
        cotangent,
        w_down,
        w_gate,
        w_up,
        router_own,
        routes.T,
        qkv,
        gain,
        gain_second,
        w_out,
        cosine,
        sine,
        seg_rows,
        seg_rows.T,
    )
    route_rows = jnp.swapaxes(route_all, 2, 3).reshape(2 * ZPARTS * rows, -1)
    (
        h_own,
        h_far,
        moe_own,
        moe_far,
        hidden,
        slopes,
        dlog,
        _,
        out_far,
        s0_own,
        z1_own,
        x0_far,
        piece2,
        s3_own,
        s3_far,
    ) = moe_layer(
        route_rows,
        grad_hidden,
        [router_own, router_far],
        h2,
        [c_own, c_far],
        [w_gate, w_up, w_down, w_out, gate_got, gate_other, up_got, down_got, down_other],
        up_got,
        width,
    )
    resident = [h_own, h_far, c_own, c_far]
    moe_own, moe_far = (a.reshape(ZPARTS, 2, rows, part) for a in (moe_own, moe_far))
    seconds = tuple((k, 1) for k in range(ZPARTS))
    cargo = [
        ((Z, 2), piece2[None], ((0,),)),
        (X, s3_far[None], ((0,),)),
        (C, moe_own, seconds),
        (C, moe_far, seconds),
    ]
    streamed = split - 1 if half_mask == 1 else 0
    first_outs = weight_grads(0, 0, split, streamed, resident, hidden, slopes, cargo)
    first_part, (z2_piece, x3_far, sib_own, sib_far) = first_outs[:4], first_outs[4:8]
    far_early = first_outs[8:]
    moe_own = low(add_wide(moe_own[:, 0], sib_own))
    moe_far = low(add_wide(moe_far[:, 0], sib_far))
    cargo = [
        ((Z, 3), low(add_wide(s3_own[None], x3_far)), ((0,),)),
        (Y, first_part[3][None], ((0,),)),
        (Y, first_part[2][None], ((0,),)),
        (X, moe_far, ((2,), (3,))),
        ((Z, 1), moe_far, ((1,),)),
    ]
    *second_part, z3_piece, far_late, got_second, moe_x, moe_z1_far = weight_grads(
        1, split, split, 0, resident, hidden, slopes, cargo
    )
    z2_piece, z3_piece, got_second = z2_piece[0], z3_piece[0], got_second[0]
    moe_srcs = [
        moe_own[1],
        low(add_wide(moe_own[2], moe_x[0])),
        low(add_wide(moe_own[3], moe_x[1])),
        low(add_wide(moe_far[0], moe_z1_far[0])),
    ]

    def router_term(h_rows):
        total = dot_tn(dlog, h_rows.reshape(-1, part))
        total = total[:experts] + total[LANES : LANES + experts]
        return jnp.pad(total, ((0, 8), (0, 0)))

    vmem_ins = [
        tokens,
        cotangent,
        middle,
        inv_first,
        inv_second,
        gain,
        gain_second,
        s0_own,
        z1_own,
        z2_piece,
        x0_far,
        z3_piece,
        q,
        keys,
        values,
        mixed,
        mixed_far,
        normed,
        normed_far,
        cosine,
        sine,
        seg_rows,
        seg_rows.T,
        w_out,
        out_far,
        router_term(h_own),
        router_term(h_far),
    ]
    swap = lambda a: flip(a, "dp", half_mask)
    plain = half_mask == 1
    grads = []
    y_far = jnp.concatenate([*far_early, far_late[0]], 0)
    if plain:
        second_far = low(add_wide(second_part[1], y_far))
        grads = [second_part[3], second_part[2], second_far, first_part[1]]
    outs = back(levels, qkv, moe_srcs, vmem_ins, grads)
    moe_parts, outs = outs[:4], outs[4:]
    own_second = add_wide(second_part[0], got_second)
    if plain:
        (got_first, far_second, far_first), outs = outs[:3], outs[3:]
        own_first = add_wide(first_part[0], got_first)
    else:

        def finish_grads(keep_own, keep_far):
            shape = (split, 3, units // 2, part)
            keep_own, keep_far = keep_own.reshape(shape), keep_far.reshape(shape)
            mask = half_mask // 2
            while mask:
                keep_own = halve(keep_own, member, mask, 2)
                keep_far = halve(keep_far, member, mask, 2)
                mask //= 2
            return keep_own, flip(low(keep_far), "col")

        own_second, far_second = finish_grads(own_second, add_wide(second_part[1], y_far))
        own_first, far_first = finish_grads(
            add_wide(first_part[0], swap(second_part[2])),
            add_wide(first_part[1], swap(second_part[3])),
        )
    grad_tokens, grad_query, grad_key, grad_value, grad_out, small, small_last = outs

    def in_order(a, b, index):
        a, b = a.astype(jnp.float32), b.astype(jnp.float32)
        return jnp.concatenate([jnp.where(index == 0, a, b), jnp.where(index == 0, b, a)], 0)

    expert_grads = in_order(
        in_order(own_first, own_second, side), in_order(far_first, far_second, side), col
    )
    expert_grads = expert_grads.reshape(local, 3, -1, part)
    output = middle + RESIDUAL * add_wide(moe_own[0], *moe_parts)
    return (
        output,
        grad_tokens,
        small_last[0],
        grad_query,
        grad_key,
        grad_value,
        grad_out,
        small[SUMMED],
        small[:experts].T,
        jnp.swapaxes(expert_grads[:, 0], 1, 2),
        jnp.swapaxes(expert_grads[:, 1], 1, 2),
        expert_grads[:, 2],
    )


def solution(mesh):
    in_specs = (
        P(("dp", "expert"), "col"),
        P("col"),
        P("col", "expert"),
        P("col", "expert"),
        P("col", "expert"),
        P("expert", "col"),
        P("col"),
        P("col", None),
        P("expert", "col", None),
        P("expert", "col", None),
        P("expert", None, "col"),
        P("dp", None),
        P(("dp", "expert"), None),
        P(("dp", "expert"), "col"),
    )
    out_specs = (
        P(("dp", "expert"), "col"),
        P(("dp", "expert"), "col"),
        P("col"),
        P("col", "expert"),
        P("col", "expert"),
        P("col", "expert"),
        P("expert", "col"),
        P("col"),
        P("col", None),
        P("expert", "col", "dp"),
        P("expert", "col", "dp"),
        P("expert", "dp", "col"),
    )
    return jax.shard_map(
        on_device, mesh=mesh, in_specs=in_specs, out_specs=out_specs, check_vma=False
    )
```

```python
import functools
import math

import jax
import jax.numpy as jnp
from jax import lax
from jax.experimental import pallas as pl
from jax.experimental.pallas import tpu as pltpu
from jax.sharding import PartitionSpec as P

HEAD_WIDTH = 64
(
    COT,
    TOK,
    DOWN,
    QKV,
    GATE,
    UP,
    ROUTER,
    GAIN,
    ROUTES,
    MIXED,
    ATTN,
    SQUARE,
    H,
    BACK,
    DA,
    DQKV,
    INNER,
    GRADS,
    MOE,
    SMALL,
    SUM,
    OUT,
) = range(22)
X, C, Y, Z, FAR_X, FAR_C, FAR_Z = range(7)
ZPARTS = 4
EARLY = 6
LANES = 128


EPS = 1e-06
RESIDUAL = 0.22
SCORE_SCALE = 0.015625
THETA = 10000.0
NEG = -1000000000.0


def doc_positions(seg_row):
    length_total = seg_row.shape[0]
    index = jnp.arange(length_total, dtype=jnp.int32)
    before = jnp.concatenate([jnp.full((1,), -1, jnp.int32), seg_row[:-1]])
    starts = jnp.where(seg_row != before, index, 0)
    return index - lax.cummax(starts, axis=0)


def flip(value, axis, mask=1):
    size = lax.axis_size(axis)
    return lax.ppermute(value, axis, [(i, i ^ mask) for i in range(size)])


def dot_nn(a, b):
    return jnp.dot(a, b, preferred_element_type=jnp.float32)


def dot_nt(a, b):
    return lax.dot_general(a, b, (((1,), (1,)), ((), ())), preferred_element_type=jnp.float32)


def dot_tn(a, b):
    return lax.dot_general(a, b, (((0,), (0,)), ((), ())), preferred_element_type=jnp.float32)


def add_wide(*parts):
    return sum(p.astype(jnp.float32) for p in parts)


def low(value):
    return value.astype(jnp.bfloat16)


class Place:
    def __init__(self):
        self.col = lax.axis_index("col")
        self.core = lax.axis_index("expert")
        group = lax.axis_index("dp")
        self.step = lax.axis_size("dp") // ZPARTS
        self.zed, self.member = group // self.step, group % self.step
        self.half = self.step // 2
        self.side = (self.member // self.half) % 2

    def x(self):
        return {"col": 1 - self.col}

    def c(self):
        return {"expert": 1 - self.core}

    def y(self):
        return {"dp": self.zed * self.step + self.member + self.half * (1 - 2 * self.side)}

    def z(self, k):
        zed = self.zed
        other = (zed + 1 - 2 * (zed % 2), (zed + 2) % ZPARTS, ZPARTS - 1 - zed)[k - 1]
        return {"dp": other * self.step + self.member}

    def bits(self):
        levels = []
        mask = self.half
        while mask:
            bit = (self.member // mask) % 2
            partner = self.zed * self.step + self.member + mask * (1 - 2 * bit)
            levels.append(({"dp": partner}, bit))
            mask //= 2
        return levels, [(self.z(1), self.zed % 2), (self.z(2), self.zed // 2)]


def greet(partners):
    barrier = pltpu.get_barrier_semaphore()
    for partner in partners:
        pl.semaphore_signal(
            barrier, inc=1, device_id=partner, device_id_type=pl.DeviceIdType.MESH
        )
    pl.semaphore_wait(barrier, len(partners))


class Transfers:
    def __init__(self, sems):
        self.sems, self.table, self.waited = sems, {}, set()

    def add(self, key, src, dst, partner):
        self.table[key] = (len(self.table), src, dst, partner)

    def copy(self, key):
        i, src, dst, partner = self.table[key]
        return pltpu.make_async_remote_copy(
            src_ref=src,
            dst_ref=dst,
            send_sem=self.sems.at[0, i],
            recv_sem=self.sems.at[1, i],
            device_id=partner,
            device_id_type=pl.DeviceIdType.MESH,
        )

    def start(self, *keys):
        for key in keys:
            self.copy(key).start()

    def arrived(self, *keys):
        for key in keys:
            self.waited.add(key)
            self.copy(key).wait_recv()

    def sent(self, *keys):
        for key in keys:
            self.copy(key).wait_send()

    def finish(self, *sent):
        for key in self.table:
            if key not in sent:
                self.copy(key).wait_send()
        for key in self.table:
            if key not in self.waited:
                self.copy(key).wait_recv()


def moves(sems, *pairs):
    copies = [pltpu.make_async_copy(src, dst, sems.at[i]) for i, (src, dst) in enumerate(pairs)]
    for copy in copies:
        copy.start()
    for copy in copies:
        copy.wait()


ANY = pl.BlockSpec(memory_space=pl.ANY)


def like_of(a):
    return jax.ShapeDtypeStruct(a.shape, a.dtype)


def whole_block(a):
    return pl.BlockSpec(a.shape, lambda *_: (0,) * a.ndim, pipeline_mode=pl.Buffered(1))


def turn(block, cosine, sine):
    lane = lax.broadcasted_iota(jnp.int32, block.shape, 1) % HEAD_WIDTH
    ahead = pltpu.roll(block, LANES - HEAD_WIDTH // 2, 1)
    behind = pltpu.roll(block, HEAD_WIDTH // 2, 1)
    return block * cosine + jnp.where(lane < HEAD_WIDTH // 2, ahead, behind) * sine


def score_tiles(rows):
    half = rows // 2
    return ((0, half, half), (half, rows, rows))


def allowed_tile(seg_row, seg_col, across_keys):
    shape = (seg_col.shape[0], seg_row.shape[1])
    down, along = (lax.broadcasted_iota(jnp.int32, shape, axis) for axis in (0, 1))
    order = down <= along if across_keys else along <= down
    return jnp.where((seg_row == seg_col) & order, 1.0, 0.0)


def swap_heads(value):
    return pltpu.roll(value.astype(jnp.float32), HEAD_WIDTH, 1).astype(value.dtype)


def attend_rows(q_ref, keys_ref, values_ref, allowed_ref, out_ref, base, blocks):
    rows = allowed_ref.shape[0]
    group = blocks

    def body(j, carry):
        cols = pl.ds(pl.multiple_of(j * LANES, LANES), LANES)
        for start, stop, keys in score_tiles(rows):
            lane = lax.broadcasted_iota(jnp.int32, (stop - start, LANES), 1)
            query = q_ref[base + start : base + stop, cols]
            allowed = allowed_ref[start:stop, :keys] > 0
            outs = []
            for side, part in enumerate((lane < HEAD_WIDTH, lane >= HEAD_WIDTH)):
                other = (2 * j + side) // group
                other = other + side - 2 * other * side
                key_rows = keys_ref[other, base : base + keys, :]
                scores = dot_nt(jnp.where(part, query, jnp.zeros_like(query)), key_rows)
                scores = jnp.where(allowed, scores * SCORE_SCALE, NEG)
                expo = jnp.exp(scores - jnp.max(scores, axis=1, keepdims=True))
                probs = expo * (1.0 / jnp.sum(expo, axis=1, keepdims=True))
                outs.append(dot_nn(low(probs), values_ref[other, base : base + keys, :]))
            mixed = jnp.where(lane < HEAD_WIDTH, outs[0], outs[1])
            out_ref[base + start : base + stop, cols] = low(mixed)
        return carry

    lax.fori_loop(0, blocks, body, 0)


def weight_slice(ref, which, half, split, zed, wide):
    first = (2 * which + half) * split
    units = pl.ds(pl.multiple_of(zed * LANES, LANES), LANES)
    if wide:
        return ref.at[pl.ds(first, split), units, :]
    return ref.at[pl.ds(first, split), :, units]


def qkv_slices(refs, which):
    widths = [ref.shape[1] // 2 for ref in refs]
    return [
        ref.at[:, pl.ds(pl.multiple_of(which * w, LANES), w)] for ref, w in zip(refs, widths)
    ]


def qkv_targets(target, refs):
    widths = [ref.shape[1] // 2 for ref in refs]
    starts = [sum(widths[:i]) for i in range(len(widths))]
    return [target.at[:, pl.ds(start, w)] for start, w in zip(starts, widths)]


def front_kernel(*refs):
    tokens, cot, w_down, w_gate, w_up, router, routes = refs[:7]
    qkv = refs[7:10]
    gain, gain_moe, w_out, cosine, sine, seg_row, seg_col = refs[10:17]
    (
        down_got,
        down_other,
        gate_got,
        gate_other,
        up_got,
        router_far,
        c_own,
        c_far,
        route_all,
        grad_hidden,
        q_ref,
        keys,
        values,
        mixed,
        mixed_far,
        normed,
        normed_far,
        inv_first,
        middle_ref,
        inv_second,
        h2_ref,
    ) = refs[17:38]
    tok, qkv_here, qkv_far, gain_far, give, got, square, square_far = refs[38:46]
    own_buf, far_buf, down_own, down_buf, grad_buf, allowed, pair_stage, qkv_stage, sems, local = refs[46:]
    place = Place()
    t = Transfers(sems)
    x, c, y = place.x(), place.c(), place.y()
    z = [None] + [place.z(k) for k in range(1, ZPARTS)]
    rows, part = tokens.shape
    ks = range(1, ZPARTS)
    t.add((TOK, X), tokens, tok.at[0], x)
    t.add((TOK, C), tokens, tok.at[1], c)
    t.add((TOK, FAR_C), tok.at[0], tok.at[2], c)
    there = qkv_slices(qkv, 1 - place.col)
    half = part // 2
    halves = [pl.ds(pl.multiple_of(i * half, half), half) for i in (place.side, 1 - place.side)]
    t.add((QKV, X), qkv_stage, qkv_far.at[0], x)
    t.add((QKV, Y), qkv_far.at[0], qkv_far.at[1], y)
    t.add((GAIN, X), gain, gain_far, x)
    t.add((ROUTER, X), router, router_far, x)
    t.add((COT, X), cot, c_far.at[0, 0], x)
    t.add((COT, C, 0), cot, c_own.at[0, 1], c)
    t.add((COT, FAR_C, 0), c_far.at[0, 0], c_far.at[0, 1], c)
    t.add((ROUTES, C, 0), routes, route_all.at[0, 1], c)
    for k in ks:
        t.add((COT, Z, k), cot, c_own.at[k, 0], z[k])
        t.add((COT, FAR_Z, k), c_far.at[0, 0], c_far.at[k, 0], z[k])
        t.add((COT, C, k), c_own.at[k, 0], c_own.at[k, 1], c)
        t.add((COT, FAR_C, k), c_far.at[k, 0], c_far.at[k, 1], c)
        t.add((ROUTES, Z, k), routes, route_all.at[k, 0], z[k])
        t.add((ROUTES, C, k), route_all.at[k, 0], route_all.at[k, 1], c)
    split = down_got.shape[0]
    staged = []
    for key, ref, land, other in (
        (DOWN, w_down, down_got, down_other),
        (GATE, w_gate, gate_got, gate_other),
        (UP, w_up, up_got, None),
    ):
        src = weight_slice(ref, 1 - place.col, place.side, split, place.zed, key == DOWN)
        if key != DOWN:
            staged.append((src, pair_stage.at[len(staged)]))
            src = staged[-1][1]
        t.add((key, X), src, land, x)
        if key != UP:
            t.add((key, Y), land, other, y)
    for i in range(2):
        cut = pl.ds(rows * i, rows)
        t.add((MIXED, X, i), mixed.at[cut], mixed_far.at[cut], x)
    t.add((ATTN, C), give, got, c)
    t.add((SQUARE, X), square, square_far, x)

    greet([x, c, y, *z[1:]])
    t.start((TOK, X), (GAIN, X))
    targets = [target.at[pl.ds(0, half)] for target in qkv_targets(qkv_stage, qkv)]
    moves(local, *[(src.at[halves[0]], target) for src, target in zip(there, targets)])
    t.start((QKV, X))
    t.start((TOK, C), (COT, C, 0), (ROUTES, C, 0), *[(ROUTES, Z, k) for k in ks])
    t.start((COT, Z, 1), (COT, Z, 2), (COT, Z, 3))
    own_cut = functools.partial(weight_slice, w_down, place.col, split=split, zed=place.zed)
    moves(
        local,
        (cot, c_own.at[0, 0]),
        (routes, route_all.at[0, 0]),
        (own_cut(half=place.side, wide=True), down_own.at[pl.ds(0, split)]),
        (own_cut(half=1 - place.side, wide=True), down_own.at[pl.ds(split, split)]),
        *zip(qkv_slices(qkv, place.col), qkv_targets(qkv_here, qkv)),
        *staged,
    )

    def norm(own, far, base):
        own, far = own.astype(jnp.float32), far.astype(jnp.float32)
        total = jnp.sum(own * own, 1, keepdims=True) + jnp.sum(far * far, 1, keepdims=True)
        inv = lax.rsqrt(total / (2 * part) + EPS)
        normed[base : base + rows, :] = (own * inv * gain[...]).astype(jnp.bfloat16)
        normed_far[base : base + rows, :] = (far * inv * gain_far[...]).astype(jnp.bfloat16)
        return inv

    def masks(b):
        allowed[...] = allowed_tile(seg_row[b : b + 1, :], seg_col[:, b : b + 1], False)

    masks(1)
    t.arrived((QKV, X))
    t.start((QKV, Y))
    t.arrived((TOK, X), (GAIN, X))
    t.start((TOK, FAR_C), (COT, X), (ROUTER, X))
    inv = norm(tokens[...], tok[0], 0)
    inv_first[...] = jnp.broadcast_to(inv, inv_first.shape)
    t.arrived((TOK, C), (TOK, FAR_C))
    norm(tok[1], tok[2], rows)
    for k in ks:
        t.arrived((ROUTES, Z, k))
        t.start((ROUTES, C, k))
    t.arrived((COT, Z, 1))
    t.start((COT, C, 1))
    t.arrived((QKV, Y))
    t.start((DOWN, X))

    width = q_ref.shape[1]
    for base in (rows, 0):
        cut = slice(base, base + rows)
        qkv_rows = dot_nn(normed[cut, :], qkv_here[...])
        for i in range(2):
            qkv_rows = qkv_rows + dot_nn(normed_far[cut, halves[i]], qkv_far[i])
        for i in range(width // LANES + 1):
            block = qkv_rows[:, LANES * i : LANES * (i + 1)]
            block = turn(block, cosine[cut, :], sine[cut, :])
            if i < width // LANES:
                q_ref[cut, LANES * i : LANES * (i + 1)] = low(block)
            else:
                keys[0, cut, :] = low(block)
                keys[1, cut, :] = swap_heads(low(block))
        block = low(qkv_rows[:, width + LANES :])
        values[0, cut, :] = block
        values[1, cut, :] = swap_heads(block)
    attend_rows(q_ref, keys, values, allowed, mixed, rows, width // LANES)
    t.start((MIXED, X, 1))
    t.arrived((COT, X))
    t.start((COT, FAR_C, 0), (COT, FAR_Z, 1), (COT, FAR_Z, 2))
    masks(0)
    attend_rows(q_ref, keys, values, allowed, mixed, 0, width // LANES)
    t.start((MIXED, X, 0))
    t.start((COT, FAR_Z, 3))
    t.arrived((COT, Z, 2))
    t.start((COT, C, 2))
    t.arrived((DOWN, X))
    t.start((DOWN, Y))

    def project(base):
        cut = slice(base, base + rows)
        first = pl.ds(pl.multiple_of(place.col * width, LANES), width)
        second = pl.ds(pl.multiple_of((1 - place.col) * width, LANES), width)
        return dot_nn(mixed[cut, :], w_out[first, :]) + dot_nn(mixed_far[cut, :], w_out[second, :])

    def stored(i):
        out = grad_hidden.at[pl.ds(rows * i, rows)]
        return pltpu.make_async_copy(grad_buf.at[i % 2], out, local.at[9 + i % 2])

    def hidden_grads(i):
        k, p = i // 2, i % 2
        if p == 1:
            t.arrived((COT, C, k), (COT, FAR_C, k))
        moves(local, (c_own.at[k, p], own_buf), (c_far.at[k, p], far_buf))
        if i > 1:
            stored(i - 2).wait()
        size = split * LANES
        for n in range(2):
            own_rows = down_own[split * n : split * (n + 1)].reshape(size, part)
            far_rows = down_buf[n].reshape(size, part)
            total = dot_nt(own_buf[...], own_rows) + dot_nt(far_buf[...], far_rows)
            grad_buf[i % 2, :, size * n : size * (n + 1)] = low(RESIDUAL * total)
        stored(i).start()

    t.arrived((MIXED, X, 1))
    give[...] = project(rows)
    t.start((ATTN, C), (GATE, X))
    t.arrived((MIXED, X, 0))
    t.start((UP, X))
    attn = project(0)
    t.arrived((ATTN, C))
    middle = tokens[...].astype(jnp.float32) + RESIDUAL * (attn + got[...])
    middle_ref[...] = middle
    total = jnp.sum(middle * middle, 1, keepdims=True)
    square[...] = jnp.broadcast_to(total, (rows, LANES)).T[:8, :]
    t.start((SQUARE, X))
    t.arrived((DOWN, Y))
    moves(local, (down_got, down_buf.at[0]), (down_other, down_buf.at[1]))
    hidden_grads(0)
    t.arrived((SQUARE, X))
    total = total + jnp.broadcast_to(square_far[:1, :], (LANES, rows)).T[:, :1]
    inv = lax.rsqrt(total / (2 * part) + EPS)
    inv_second[...] = jnp.broadcast_to(inv, inv_second.shape)
    h2_ref[...] = low(middle_ref[...] * inv * gain_moe[...])

    hidden_grads(1)
    t.arrived((COT, FAR_Z, 1))
    t.start((COT, FAR_C, 1))
    hidden_grads(2)
    t.arrived((GATE, X))
    t.start((GATE, Y))
    hidden_grads(3)
    t.arrived((COT, FAR_Z, 2), (COT, Z, 3))
    t.start((COT, FAR_C, 2), (COT, C, 3))
    hidden_grads(4)
    hidden_grads(5)
    t.arrived((COT, FAR_Z, 3))
    t.start((COT, FAR_C, 3))
    stored(EARLY - 2).wait()
    stored(EARLY - 1).wait()
    t.finish()


def front(tokens, cot, w_down, w_gate, w_up, router, routes, qkv, *others):
    rows, part = tokens.shape
    gain, w_out = others[0], others[2]
    vmem = pl.BlockSpec(memory_space=pltpu.VMEM)
    shape = lambda dims, dtype=jnp.bfloat16: jax.ShapeDtypeStruct(dims, dtype)
    like = lambda a: shape(a.shape, a.dtype)
    stack = lambda a: shape((ZPARTS, 2, *a.shape), a.dtype)
    mine = w_down.shape[0] // 2
    width, kv = qkv[0].shape[1] // 2, qkv[1].shape[1] // 2
    down, pair = shape((mine // 2, LANES, part)), shape((mine // 2, part, LANES))
    hbm_outs = [down, down, pair, pair, pair, like(router)]
    hbm_outs += [stack(cot), stack(cot), stack(routes)]
    hbm_outs += [shape((EARLY * rows, mine * LANES))]
    vmem_outs = [
        shape((2 * rows, width)),
        shape((2, 2 * rows, kv)),
        shape((2, 2 * rows, kv)),
        shape((2 * rows, width)),
        shape((2 * rows, width)),
        shape((2 * rows, part)),
        shape((2 * rows, part)),
        shape((rows, LANES), jnp.float32),
        shape((rows, part), jnp.float32),
        shape((rows, LANES), jnp.float32),
        shape((rows, part)),
    ]
    buffer = pltpu.VMEM((rows, part), jnp.bfloat16)
    wide = pltpu.VMEM((rows, part), jnp.float32)
    small = pltpu.VMEM((8, rows), jnp.float32)
    weights = pltpu.VMEM((part, width + 2 * kv), jnp.bfloat16)
    half_weights = pltpu.VMEM((part // 2, width + 2 * kv), jnp.bfloat16)
    count = 15 + 6 * (ZPARTS - 1) + 5 + 2 + 2
    return pl.pallas_call(
        front_kernel,
        out_shape=hbm_outs + vmem_outs,
        in_specs=[vmem] + [ANY] * 9 + [vmem] * len(others),
        out_specs=[ANY] * len(hbm_outs) + [vmem] * len(vmem_outs),
        scratch_shapes=[
            pltpu.VMEM((3, rows, part), jnp.bfloat16),
            weights,
            pltpu.VMEM((2, part // 2, width + 2 * kv), jnp.bfloat16),
            pltpu.VMEM(gain.shape, jnp.float32),
            wide,
            wide,
            small,
            small,
            buffer,
            buffer,
            pltpu.VMEM((mine, LANES, part), jnp.bfloat16),
            pltpu.VMEM((2, mine // 2, LANES, part), jnp.bfloat16),
            pltpu.VMEM((2, rows, mine * LANES), jnp.bfloat16),
            pltpu.VMEM((rows, rows), jnp.float32),
            pltpu.VMEM((2, *pair.shape), jnp.bfloat16),
            half_weights,
            pltpu.SemaphoreType.DMA((2, count)),
            pltpu.SemaphoreType.DMA((11,)),
        ],
        compiler_params=pltpu.CompilerParams(
            collective_id=0, has_side_effects=True, vmem_limit_bytes=58 * 1024 * 1024
        ),
        name="front",
    )(tokens, cot, w_down, w_gate, w_up, router, routes, *qkv, *others)


def moe_kernel(*refs):
    routes_ref, grad_ref, router_own, router_far, h2, c_own, c_far = refs[:7]
    w_gate, w_up, w_down, w_out, gate_got, gate_other, up_got, down_got, down_other = refs[7:16]
    (
        h_own_out,
        h_far_out,
        moe_own,
        moe_far,
        hidden_out,
        slopes_out,
        dlog_ref,
        up_other,
        out_far,
        s0_own,
        z1_own,
        x0_far,
        piece2,
        s3_own,
        s3_far,
    ) = refs[16:31]
    h_own_all, h_far_all, keep_own, keep_far, give_own, give_far, got_own, got_far = refs[31:39]
    got_x, z1_far, pair_own, pair_far, down_own, down_far, hidden_ref, slopes_ref = refs[39:47]
    grad_late, sems, local, fill, save = refs[47:]
    experts = down_own.shape[0]
    split = experts // 2
    rows, part = h2.shape
    place = Place()
    step = pl.program_id(0)
    t = Transfers(sems)
    x, c = place.x(), place.c()
    z = [None] + [place.z(k) for k in range(1, ZPARTS)]
    t.add((H, X), h2, h_far_all.at[0, 0], x)
    t.add((H, C, 0), h2, h_own_all.at[0, 1], c)
    t.add((H, FAR_C, 0), h_far_all.at[0, 0], h_far_all.at[0, 1], c)
    for k in range(1, ZPARTS):
        t.add((H, Z, k), h2, h_own_all.at[k, 0], z[k])
        if k == 1:
            t.add((H, FAR_X, 1), h_far_all.at[0, 0], h_far_all.at[1, 0], z[1])
        else:
            t.add((H, FAR_X, k), h_own_all.at[k, 0], h_far_all.at[k, 0], x)
        t.add((H, C, k), h_own_all.at[k, 0], h_own_all.at[k, 1], c)
        t.add((H, FAR_C, k), h_far_all.at[k, 0], h_far_all.at[k, 1], c)
    for k in range(ZPARTS):
        t.add((BACK, C, k), give_own, got_own.at[k], c)
        t.add((BACK, FAR_C, k), give_far, got_far.at[k], c)
    t.add((BACK, Z), got_own.at[1], z1_own, z[1])
    t.add((BACK, FAR_Z), got_far.at[1], z1_far, z[1])
    t.add((BACK, FAR_X), got_far.at[2], got_x, x)
    t.add((BACK, X), got_far.at[0], x0_far, x)
    t.add((UP, Y), up_got, up_other, place.y())
    width = out_far.shape[0]
    there = pl.ds(pl.multiple_of((1 - place.col) * width, LANES), width)
    t.add((OUT, X), w_out.at[there], out_far, x)

    def join(k):
        for name in ((BACK, C, k), (BACK, FAR_C, k)):
            t.copy(name).wait_send()
        t.arrived((BACK, C, k), (BACK, FAR_C, k))
        for got, keep in ((got_own, keep_own), (got_far, keep_far)):
            total = got[k].astype(jnp.float32) + keep[...].astype(jnp.float32)
            got[k] = total.astype(jnp.bfloat16)

    @pl.when(step == 0)
    def _():
        greet([x, c, place.y(), *z[1:]])
        t.start((H, X), (H, C, 0), (UP, Y), (H, Z, 1), (H, Z, 2))
        cut = functools.partial(weight_slice, which=place.col, split=split, zed=place.zed)
        fills, late = [], []
        for i, half in enumerate((place.side, 1 - place.side)):
            gates = (cut(w_gate, half=half, wide=False), (gate_got, gate_other)[i])
            ups = (cut(w_up, half=half, wide=False), (up_got, up_other)[i])
            downs = (cut(w_down, half=half, wide=True), (down_got, down_other)[i])
            for n, (pair, down) in enumerate(((pair_own, down_own), (pair_far, down_far))):
                for e in range(split):
                    for m, src in enumerate((gates[n], ups[n])):
                        cols = pl.ds(LANES * (2 * e + m), LANES)
                        into = late if src is up_other else fills
                        into.append((src.at[e], pair.at[i, :, cols]))
                fills.append((downs[n], down.at[pl.ds(split * i, split)]))
        moves(fill, (h2, h_own_all.at[0, 0]), *fills)

        def hidden_grads(i):
            k, p = (EARLY + i) // 2, (EARLY + i) % 2
            moves(local, (c_own.at[k, p], give_own), (c_far.at[k, p], give_far))
            total = dot_nt(give_own[...], down_own[...].reshape(-1, part))
            total = total + dot_nt(give_far[...], down_far[...].reshape(-1, part))
            grad_late[i] = low(RESIDUAL * total)

        for i in range(ZPARTS - EARLY // 2):
            hidden_grads(i)
        t.arrived((H, X))
        t.start((H, FAR_C, 0), (H, FAR_X, 1))
        for i in range(ZPARTS - EARLY // 2, 2 * ZPARTS - EARLY):
            hidden_grads(i)
        t.arrived((UP, Y))
        moves(fill, *late)

    @pl.when(step == 1)
    def _():
        t.arrived((H, C, 0), (H, FAR_C, 0), (H, Z, 1))
        t.start((H, C, 1), (OUT, X))

    @pl.when(step == 2)
    def _():
        t.start((H, Z, 3))
        t.arrived((H, FAR_X, 1))
        t.start((H, FAR_C, 1))
        join(0)
        t.arrived((H, Z, 2))
        t.start((H, FAR_X, 2), (H, C, 2))

    @pl.when(step == 3)
    def _():
        t.arrived((H, C, 1), (H, FAR_C, 1))

    @pl.when(step == 4)
    def _():
        join(1)
        t.start((BACK, Z), (BACK, FAR_Z))
        t.arrived((H, FAR_X, 2))
        t.start((H, FAR_C, 2))
        t.arrived((H, Z, 3))
        t.start((H, FAR_X, 3), (H, C, 3))

    @pl.when(step == 5)
    def _():
        t.arrived((H, C, 2), (H, FAR_C, 2))

    @pl.when(step == 6)
    def _():
        join(2)
        t.start((BACK, FAR_X))
        t.arrived((H, FAR_X, 3))
        t.start((H, FAR_C, 3))

    @pl.when(step == 7)
    def _():
        t.arrived((H, C, 3), (H, FAR_C, 3))
        t.arrived((BACK, FAR_X))
        got_own[2] = low(add_wide(got_own[2], got_x[...]))
        t.arrived((BACK, FAR_Z))
        got_far[0] = low(add_wide(got_far[0], z1_far[...]))
        t.start((BACK, X))

    def saved(i):
        k, p = i // 2, i % 2
        pairs = ((h_own_all, h_own_out), (h_far_all, h_far_out))
        return [
            pltpu.make_async_copy(src.at[k, p], dst.at[k, p], save.at[n, i])
            for n, (src, dst) in enumerate(pairs)
        ]

    def written(i):
        cut = pl.ds(rows * i, rows)
        return [
            pltpu.make_async_copy(src, dst.at[cut], save.at[2 + n, i])
            for n, (src, dst) in enumerate(((hidden_ref, hidden_out), (slopes_ref, slopes_out)))
        ]

    for i in range(2 * ZPARTS):

        @pl.when(step == i)
        def _():
            for copy in saved(i):
                copy.start()
            if i > 0:
                for copy in written(i - 1):
                    copy.wait()

    h_own, h_far = h_own_all.at[step // 2, step % 2], h_far_all.at[step // 2, step % 2]

    first = (place.core * 2 + place.col) * experts
    lane = lax.broadcasted_iota(jnp.int32, (rows, LANES), 1)
    chosen = lane == routes_ref[:, 0:1]
    for k in range(1, routes_ref.shape[1]):
        chosen = chosen | (lane == routes_ref[:, k : k + 1])
    logits = dot_nn(h_own[...], router_own[...]) + dot_nn(h_far[...], router_far[...])
    peak = jnp.max(jnp.where(chosen, logits, -jnp.inf), axis=1, keepdims=True)
    expo = jnp.where(chosen, jnp.exp(logits - peak), 0.0)
    gates = expo / jnp.sum(expo, axis=1, keepdims=True)
    grad_gates = jnp.zeros((rows, LANES), jnp.float32)
    at_late = jnp.maximum(step - EARLY, 0)
    for e in range(experts):
        here = lane == first + (e + place.side * split) % experts
        gate = jnp.sum(jnp.where(here, gates, 0.0), axis=1, keepdims=True)
        cols = slice(2 * LANES * (e % split), 2 * LANES * (e % split + 1))
        pair = dot_nn(h_own[...], pair_own[e // split, :, cols]) + dot_nn(
            h_far[...], pair_far[e // split, :, cols]
        )
        cut = slice(LANES * e, LANES * (e + 1))
        slope = jnp.where(step < EARLY, grad_ref[:, cut], grad_late[at_late, :, cut])
        slope = slope.astype(jnp.float32)
        gate_val = pair[:, :LANES]
        up_val = pair[:, LANES:]
        sigma = jax.nn.sigmoid(gate_val)
        silu = gate_val * sigma
        hidden = silu * up_val
        dgate = jnp.sum(hidden * slope, axis=1, keepdims=True)
        grad_gates = jnp.where(here, dgate, grad_gates)
        dz = gate * slope
        hidden_ref[:, LANES * e : LANES * (e + 1)] = (gate * hidden).astype(jnp.bfloat16)
        slopes_ref[:, 2 * LANES * e : 2 * LANES * e + LANES] = (
            dz * up_val * (sigma + silu * (1.0 - sigma))
        ).astype(jnp.bfloat16)
        slopes_ref[:, 2 * LANES * e + LANES : 2 * LANES * (e + 1)] = (dz * silu).astype(
            jnp.bfloat16
        )
    dlog = gates * (grad_gates - jnp.sum(gates * grad_gates, axis=1, keepdims=True))
    dlog_high = dlog.astype(jnp.bfloat16)
    dlog_low = (dlog - dlog_high.astype(jnp.float32)).astype(jnp.bfloat16)
    dlog_ref[:, :LANES] = dlog_high
    dlog_ref[:, LANES:] = dlog_low

    def back(pairs, router):
        total = dot_nt(dlog_high, router[...]) + dot_nt(dlog_low, router[...])
        for i in range(2):
            cols = slice(2 * LANES * split * i, 2 * LANES * split * (i + 1))
            total = total + dot_nt(slopes_ref[:, cols], pairs[i])
        return total.astype(jnp.bfloat16)

    back_own, back_far = back(pair_own, router_own), back(pair_far, router_far)
    last = pl.num_programs(0) - 1

    @pl.when(step % 2 == 0)
    def _():
        keep_own[...] = back_own
        keep_far[...] = back_far

    @pl.when(step % 2 == 1)
    def _():
        give_own[...] = back_own
        give_far[...] = back_far

    for k in range(ZPARTS):

        @pl.when(step == 2 * k + 1)
        def _():
            t.start((BACK, C, k), (BACK, FAR_C, k))

    for i in range(2 * ZPARTS):

        @pl.when(step == i)
        def _():
            for copy in written(i):
                copy.start()

    moe_own[...] = low(dot_nn(hidden_ref[...], down_own[...].reshape(-1, part)))
    moe_far[...] = low(dot_nn(hidden_ref[...], down_far[...].reshape(-1, part)))

    @pl.when(step == last)
    def _():
        join(ZPARTS - 1)
        moves(
            local,
            (got_own.at[0], s0_own),
            (got_own.at[2], piece2),
            (got_own.at[3], s3_own),
            (got_far.at[3], s3_far),
        )
        for copy in written(2 * ZPARTS - 1):
            copy.wait()
        for i in range(2 * ZPARTS):
            for copy in saved(i):
                copy.wait()
        t.finish(*[(BACK, hop, k) for hop in (C, FAR_C) for k in range(ZPARTS)])


def moe_layer(routes, grad_hidden, routers, h2, c_rows, weights, up_got, width):
    tile, part = h2.shape
    rows = routes.shape[0]
    experts = grad_hidden.shape[1] // LANES
    by_row = lambda width: pl.BlockSpec((tile, width), lambda i: (i, 0))
    stack = jax.ShapeDtypeStruct((ZPARTS, 2, tile, part), jnp.bfloat16)
    one = jax.ShapeDtypeStruct((tile, part), jnp.bfloat16)
    widths = [part, part, experts * LANES, 2 * experts * LANES, 2 * LANES]
    buffer = pltpu.VMEM((tile, part), jnp.bfloat16)
    stacked = pltpu.VMEM((ZPARTS, tile, part), jnp.bfloat16)
    pieces = pltpu.VMEM((ZPARTS, 2, tile, part), jnp.bfloat16)
    pair = pltpu.VMEM((2, part, experts * LANES), jnp.bfloat16)
    down = pltpu.VMEM((experts, LANES, part), jnp.bfloat16)
    extra = [like_of(up_got), jax.ShapeDtypeStruct((width, part), jnp.bfloat16)]
    count = 3 + 4 * (ZPARTS - 1) + 2 * ZPARTS + 6
    return pl.pallas_call(
        moe_kernel,
        out_shape=[stack, stack]
        + [jax.ShapeDtypeStruct((rows, w), jnp.bfloat16) for w in widths]
        + extra
        + [one] * 6,
        grid=(rows // tile,),
        in_specs=[
            by_row(routes.shape[1]),
            pl.BlockSpec((tile, experts * LANES), lambda i: (jnp.minimum(i, EARLY - 1), 0)),
        ]
        + [whole_block(r) for r in routers]
        + [ANY] * (3 + len(weights)),
        out_specs=[ANY, ANY, by_row(part), by_row(part), ANY, ANY, by_row(2 * LANES)]
        + [ANY] * 8,
        scratch_shapes=[pieces] * 2
        + [buffer] * 4
        + [stacked] * 2
        + [buffer, buffer, pair, pair, down, down]
        + [pltpu.VMEM((tile, w), jnp.bfloat16) for w in widths[2:4]]
        + [pltpu.VMEM((2 * ZPARTS - EARLY, tile, widths[2]), jnp.bfloat16)]
        + [
            pltpu.SemaphoreType.DMA((2, count)),
            pltpu.SemaphoreType.DMA((5,)),
            pltpu.SemaphoreType.DMA((5 + 4 * experts,)),
            pltpu.SemaphoreType.DMA((4, 2 * ZPARTS)),
        ],
        compiler_params=pltpu.CompilerParams(
            collective_id=1, has_side_effects=True, vmem_limit_bytes=63 * 1024 * 1024
        ),
        name="moe_layer",
    )(routes, grad_hidden, *routers, h2, *c_rows, *weights)


def weight_kernel(cargo, streamed, *refs):
    n_cargo = len(cargo)
    h_own, h_far, c_own, c_far, hidden, slopes = refs[:6]
    sources = refs[6 : 6 + n_cargo]
    keep_own, keep_far, give_own, rest_far = refs[6 + n_cargo : 10 + n_cargo]
    landed = refs[10 + n_cargo : 10 + 2 * n_cargo]
    if streamed:
        far_land = refs[10 + 2 * n_cargo]
    give_far, sems, local = refs[-3:]
    place = Place()
    step = pl.program_id(0)
    t = Transfers(sems)
    partners = {X: place.x(), Y: place.y(), C: place.c()}
    partners.update({(Z, k): place.z(k) for k in range(1, ZPARTS)})
    to = {name: partners[name] for name, _ in cargo}
    for i, (name, views) in enumerate(cargo):
        for n, view in enumerate(views):
            t.add((i, n), sources[i].at[view], landed[i].at[n], to[name])
    first_keys = list(t.table)
    for e in range(streamed):
        t.add((GRADS, e), give_far.at[e], far_land.at[e], partners[Y])
    if streamed:
        to[Y] = partners[Y]

    @pl.when(step == 0)
    def _():
        greet(list(to.values()))
        t.start(*first_keys)

    half = LANES // 2
    tile = h_own.shape[2]
    first = place.side == 0
    for keep, give, at, rows_h, rows_c in (
        (keep_far, give_far, step, h_far, c_far),
        (keep_own, give_own, 0, h_own, c_own),
    ):
        pair, down = 0.0, 0.0
        for i in range(2 * ZPARTS):
            rows = slice(tile * i, tile * (i + 1))
            pair = pair + dot_tn(slopes[rows, :], rows_h[i // 2, i % 2])
            down = down + dot_tn(hidden[rows, :], rows_c[i // 2, i % 2])
        for i, block in enumerate((pair[:LANES], pair[LANES:], RESIDUAL * down)):
            begin, end = block[:half], block[half:]
            cut = slice(half * i, half * (i + 1))
            keep[0, cut, :] = jnp.where(first, begin, end)
            give[at, cut, :] = low(jnp.where(first, end, begin))
        if keep is keep_far:
            for e in range(streamed):

                @pl.when(step == e)
                def _():
                    t.start((GRADS, e))

    @pl.when(step == pl.num_programs(0) - 1)
    def _():
        rest = rest_far.shape[0]
        moves(local, (give_far.at[pl.ds(streamed, rest)], rest_far))
        t.finish()


def weight_grads(number, start, count, streamed, resident, hidden, slopes, cargo):
    part = resident[0].shape[-1]
    rows = hidden.shape[0]
    out = pl.BlockSpec((1, 3 * LANES // 2, part), lambda e: (e, 0, 0))
    block = (3 * LANES // 2, part)
    shape = (count, *block)
    arrays = [array for _, array, _ in cargo]
    views = tuple((name, tuple(where)) for name, _, where in cargo)
    landed = []
    for _, array, where in cargo:
        dims = (len(where), *array.shape[len(where[0]) :])
        landed.append(jax.ShapeDtypeStruct(dims, array.dtype))
    rest = jax.ShapeDtypeStruct((count - streamed, *block), jnp.bfloat16)
    if streamed:
        landed.append(jax.ShapeDtypeStruct((streamed, *block), jnp.bfloat16))
    transfers = sum(len(where) for _, _, where in cargo) + streamed
    return pl.pallas_call(
        functools.partial(weight_kernel, views, streamed),
        out_shape=[jax.ShapeDtypeStruct(shape, jnp.float32)] * 2
        + [jax.ShapeDtypeStruct(shape, jnp.bfloat16), rest]
        + landed,
        grid=(count,),
        in_specs=[whole_block(a) for a in resident]
        + [
            pl.BlockSpec((rows, LANES), lambda e: (0, e + start)),
            pl.BlockSpec((rows, 2 * LANES), lambda e: (0, e + start)),
        ]
        + [ANY] * len(arrays),
        out_specs=[out] * 3 + [ANY] * (1 + len(landed)),
        scratch_shapes=[
            pltpu.VMEM(shape, jnp.bfloat16),
            pltpu.SemaphoreType.DMA((2, transfers)),
            pltpu.SemaphoreType.DMA((1,)),
        ],
        compiler_params=pltpu.CompilerParams(
            collective_id=2 + number, has_side_effects=True, vmem_limit_bytes=60 * 1024 * 1024
        ),
        name="expert_weight_grads",
    )(*resident, hidden, slopes, *arrays)


def unturn(block, cosine, sine):
    return block * cosine + turn(block, jnp.zeros_like(cosine), -sine)


def attend_back_rows(
    q_ref, keys_ref, values_ref, grad_ref, allowed_ref, out_ref, dk, dv, cosine, sine, base, blocks
):
    rows = allowed_ref.shape[0]
    dk[...] = jnp.zeros_like(dk)
    dv[...] = jnp.zeros_like(dv)

    def body(j, carry):
        cols = pl.ds(pl.multiple_of(j * LANES, LANES), LANES)
        for start, stop, keys in score_tiles(rows):
            cut = slice(base + start, base + stop)
            lane = lax.broadcasted_iota(jnp.int32, (stop - start, LANES), 1)
            query, grad = q_ref[cut, cols], grad_ref[cut, cols]
            allowed = allowed_ref[:keys, start:stop] > 0
            dqs = []
            for side, part in enumerate((lane < HEAD_WIDTH, lane >= HEAD_WIDTH)):
                other = (2 * j + side) // blocks
                other = other + side - 2 * other * side
                key_rows = keys_ref[other, base : base + keys, :]
                value_rows = values_ref[other, base : base + keys, :]
                one_query = jnp.where(part, query, jnp.zeros_like(query))
                one_grad = jnp.where(part, grad, jnp.zeros_like(grad))
                scores = jnp.where(allowed, dot_nt(key_rows, one_query) * SCORE_SCALE, NEG)
                expo = jnp.exp(scores - jnp.max(scores, axis=0, keepdims=True))
                probs = expo * (1.0 / jnp.sum(expo, axis=0, keepdims=True))
                slope = dot_nt(value_rows, one_grad)
                delta = jnp.sum(probs * slope, axis=0, keepdims=True)
                dscore = low(probs * (slope - delta))
                dv[other, :keys, :] = dv[other, :keys, :] + dot_nn(low(probs), one_grad)
                dk[other, :keys, :] = dk[other, :keys, :] + dot_nn(dscore, one_query)
                dqs.append(dot_tn(dscore, key_rows))
            dq = jnp.where(lane < HEAD_WIDTH, dqs[0], dqs[1]) * SCORE_SCALE
            out_ref[cut, cols] = low(unturn(dq, cosine[cut, :], sine[cut, :]))
        return carry

    lax.fori_loop(0, blocks, body, 0)
    cut = slice(base, base + rows)
    width = blocks * LANES
    total = (dk[0] + pltpu.roll(dk[1], HEAD_WIDTH, 1)) * SCORE_SCALE
    out_ref[cut, width : width + LANES] = low(unturn(total, cosine[cut, :], sine[cut, :]))
    out_ref[cut, width + LANES :] = low(dv[0] + pltpu.roll(dv[1], HEAD_WIDTH, 1))


class WholeSum:
    def __init__(self, t, name, ref, levels, stages, lands, swap=None):
        self.t, self.name, self.ref = t, name, ref
        self.stages, self.lands, self.count = stages, lands, len(levels)
        offset, rows = 0, ref.shape[0]
        self.kept, self.other = [], []
        ways = []
        for i, (partner, bit) in enumerate(levels):
            rows = rows // 2
            self.other.append((offset + (1 - bit) * rows, rows))
            offset = offset + bit * rows
            self.kept.append((offset, rows))
            ways.append((i, i, self.other[i], self.kept[i], partner))
        last = self.count - 1
        back = [
            (i, self.count + i, self.kept[i], self.other[i], levels[i][0])
            for i in range(last, -1, -1)
        ]
        if swap is not None:
            ways.append((last, 2 * self.count, self.kept[last], self.kept[last], swap))
        self.ways = ways + back
        for i, (stage, land, _, _, partner) in enumerate(self.ways):
            t.add((SUM, name, i), stages[stage], lands[land], partner)

    def rows(self, place):
        return pl.ds(pl.multiple_of(place[0], 8), place[1])

    def send(self, i):
        stage, _, place, _, _ = self.ways[i]
        for j in range(i - 1, -1, -1):
            if self.ways[j][0] == stage:
                self.t.sent((SUM, self.name, j))
                break
        self.stages[stage][...] = low(self.ref[self.rows(place), :])
        self.t.start((SUM, self.name, i))

    def land(self, i):
        self.t.arrived((SUM, self.name, i))
        _, land, _, place, _ = self.ways[i]
        cut = self.rows(place)
        total = self.lands[land][...].astype(jnp.float32)
        if i < self.count:
            total = self.ref[cut, :] + total
            if i == self.count - 1:
                total = low(total).astype(jnp.float32)
        self.ref[cut, :] = total

    def next(self, i):
        if 0 <= i < len(self.ways):
            self.land(i)
            if i + 1 < len(self.ways):
                self.send(i + 1)

    def keys(self):
        done = []
        for i, way in enumerate(self.ways):
            if any(later[0] == way[0] for later in self.ways[i + 1 :]):
                done.append((SUM, self.name, i))
        return done


class SmallSum:
    def __init__(self, t, name, ref, partners, lands):
        self.t, self.name, self.ref, self.lands = t, name, ref, lands
        for i, partner in enumerate(partners):
            t.add((SMALL, name, i), ref, lands.at[i], partner)

    def send(self, i):
        self.t.start((SMALL, self.name, i))

    def land(self, i):
        self.t.sent((SMALL, self.name, i))
        self.t.arrived((SMALL, self.name, i))
        self.ref[...] = self.ref[...] + self.lands[i]

    def next(self, i):
        if 0 <= i < self.lands.shape[0]:
            self.land(i)
            if i + 1 < self.lands.shape[0]:
                self.send(i + 1)

    def keys(self):
        return [(SMALL, self.name, i) for i in range(self.lands.shape[0])]


SUMMED = 40


def back_kernel(count, with_grads, *refs):
    refs = list(refs)
    take = lambda n: [refs.pop(0) for _ in range(n)]
    qkv = take(3)
    moe_srcs = take(4)
    tokens, cot, middle, inv_first, inv_second, gain, gain_moe = take(7)
    parts = take(5)
    q_ref, keys, values, mixed, mixed_far, normed, normed_far = take(7)
    cosine, sine, seg_row, seg_col = take(4)
    w_out, out_far, small_own, small_there = take(4)
    if with_grads:
        grad_srcs, keep_first = take(3), take(1)[0]
    moe_lands = take(4)
    if with_grads:
        grad_lands = take(3)
    grad_tokens, grad_q, grad_k, grad_v, grad_out, small, small_last = take(7)
    qkv_here, qkv_there, da_own, da_far, grad_mixed, dqkv, dqkv_far, give, got = take(9)
    grad_middle, grad_here, grad_there, allowed, dk, dv, square, square_far = take(8)
    small_land, small_lands, last_lands = take(3)
    stages, lands = [], []
    for _ in range(3):
        stages.append(take(count))
        lands.append(take(2 * count + 1))
    if with_grads:
        first_land, first_sum = take(2)
    sems, local = take(2)
    place = Place()
    t = Transfers(sems)
    x, c, y = place.x(), place.c(), place.y()
    rows, part = tokens.shape
    width = q_ref.shape[1]
    low_levels, high_levels = place.bits()
    partners = [partner for partner, _ in low_levels + high_levels]
    t.add((INNER, 0), square.at[0], square_far.at[0], x)
    t.add((INNER, 1), square.at[1], square_far.at[1], x)
    t.add((SMALL, X), small_there, small_land, x)
    first, second = pl.ds(0, rows), pl.ds(rows, rows)
    t.add((DA, X), da_own.at[first], da_far.at[first], x)
    t.add((DA, C), da_own.at[first], da_own.at[second], c)
    t.add((DA, FAR_C), da_far.at[first], da_far.at[second], c)
    for i, cut in enumerate((first, second)):
        t.add((DQKV, i), dqkv.at[cut], dqkv_far.at[cut], x)
    t.add((ATTN, C), give, got, c)
    for i, partner in enumerate((place.z(1), place.z(2), place.z(3), x)):
        t.add((MOE, i), moe_srcs[i], moe_lands[i], partner)
    if with_grads:
        t.add((GRADS, Y, 0), grad_srcs[0], first_land, y)
        t.add((GRADS, Y, 1), grad_srcs[1], grad_lands[0], y)
        t.add((GRADS, X, 0), grad_srcs[2], grad_lands[1], x)
        t.add((GRADS, X, 1), first_sum, grad_lands[2], x)
    levels = low_levels + high_levels
    sum_out = WholeSum(t, 0, grad_out, levels, stages[0], lands[0])
    sum_here = WholeSum(t, 1, grad_here, levels, stages[1], lands[1])
    sum_there = WholeSum(t, 2, grad_there, levels, stages[2], lands[2], x)
    small_sum = SmallSum(t, 0, small, [c] + partners, small_lands)
    last_sum = SmallSum(t, 1, small_last, [c] + partners, last_lands)

    greet([x, c, place.z(3)] + partners)
    t.start((SMALL, X), (MOE, 1), (MOE, 2))
    if with_grads:
        t.start((GRADS, Y, 0))
    here, there = qkv_slices(qkv, place.col), qkv_slices(qkv, 1 - place.col)
    targets = [*qkv_targets(qkv_here, qkv), *qkv_targets(qkv_there, qkv)]
    moves(local, *zip([*here, *there], targets))

    def masks(b):
        allowed[...] = allowed_tile(seg_row[b : b + 1, :], seg_col[:, b : b + 1], True)

    def exchange_sum(i, total):
        square[i] = jnp.broadcast_to(total, (rows, LANES)).T[:8, :]
        t.start((INNER, i))

    def exchanged(i, total):
        t.arrived((INNER, i))
        return total + jnp.broadcast_to(square_far[i, :1, :], (LANES, rows)).T[:, :1]

    def norm_back(grad, value, inv, gain_row, inner):
        return inv * (grad * gain_row) - value * (inv * inv * inv * inner / (2 * part))

    grad = add_wide(*[p[...] for p in parts])
    inv = inv_second[:, :1]
    inner = jnp.sum(middle[...] * grad * gain_moe[...], 1, keepdims=True)
    exchange_sum(0, inner)
    small[...] = small_own[...]
    small[SUMMED : SUMMED + 1, :] = jnp.sum(grad * middle[...] * inv, 0, keepdims=True)
    inner = exchanged(0, inner)
    total = cot[...].astype(jnp.float32)
    total = total + norm_back(grad, middle[...], inv, gain_moe[...], inner)
    grad_middle[...] = total
    da_own[:rows, :] = low(RESIDUAL * total)
    t.start((DA, X), (DA, C))
    masks(1)
    t.arrived((SMALL, X))
    small[...] = small[...] + small_land[...]
    small_sum.send(0)
    t.arrived((DA, C))
    at_here = pl.ds(pl.multiple_of(place.col * width, LANES), width)
    at_there = pl.ds(pl.multiple_of((1 - place.col) * width, LANES), width)
    grad_out[at_here, :] = dot_tn(mixed[...], da_own[...])
    grad_out[at_there, :] = dot_tn(mixed_far[...], da_own[...])
    sum_out.send(0)
    small_sum.next(0)
    t.arrived((DA, X))
    t.start((DA, FAR_C))
    if with_grads:
        t.start((GRADS, X, 0))

    def mixed_back(cut):
        total = dot_nt(da_own[cut, :], w_out[at_here, :]) + dot_nt(da_far[cut, :], out_far[...])
        grad_mixed[cut, :] = low(total)

    mixed_back(slice(0, rows))
    t.arrived((DA, FAR_C))
    mixed_back(slice(rows, 2 * rows))
    attend = functools.partial(
        attend_back_rows, q_ref, keys, values, grad_mixed, allowed, dqkv, dk, dv, cosine, sine
    )
    attend(rows, width // LANES)
    t.start((DQKV, 1))
    sum_out.next(0)
    small_sum.next(1)
    if with_grads:
        t.arrived((GRADS, Y, 0))
        t.start((GRADS, Y, 1))
        first_sum[...] = low(keep_first[...] + first_land[...].astype(jnp.float32))
    t.start((MOE, 0))
    masks(0)
    attend(0, width // LANES)
    t.start((DQKV, 0))
    grad_here[...] = dot_tn(normed[...], dqkv[...])
    sum_here.send(0)
    grad_there[...] = dot_tn(normed_far[...], dqkv[...])
    sum_there.send(0)
    sum_out.next(1)
    t.arrived((DQKV, 1))

    def tokens_back(cut):
        return dot_nt(dqkv[cut, :], qkv_here[...]) + dot_nt(dqkv_far[cut, :], qkv_there[...])

    give[...] = tokens_back(slice(rows, 2 * rows))
    t.start((ATTN, C))
    sum_here.next(0)
    sum_there.next(0)
    sum_out.next(2)
    small_sum.next(2)
    t.arrived((DQKV, 0))
    if with_grads:
        t.start((GRADS, X, 1))
    grad = tokens_back(slice(0, rows))
    t.arrived((ATTN, C))
    grad = grad + got[...]
    got[...] = grad
    value = tokens[...].astype(jnp.float32)
    inv = inv_first[:, :1]
    inner = jnp.sum(value * grad * gain[...], 1, keepdims=True)
    exchange_sum(1, inner)
    small_last[...] = jnp.zeros_like(small_last)
    small_last[0:1, :] = jnp.sum(grad * value * inv, 0, keepdims=True)
    last_sum.send(0)
    sum_here.next(1)
    sum_there.next(1)
    sum_out.next(3)
    inner = exchanged(1, inner)
    t.start((MOE, 3))
    grad = norm_back(got[...], tokens[...].astype(jnp.float32), inv, gain[...], inner)
    grad_tokens[...] = grad_middle[...] + grad
    last_sum.next(0)
    for i in range(2, 2 * count + 1):
        sum_here.next(i)
        sum_there.next(i)
        sum_out.next(i + 2)
        small_sum.next(i + 1)
        last_sum.next(i - 1)
    for i in range(2 * count, small_lands.shape[0]):
        small_sum.next(i + 1)
        last_sum.next(i)
    start = 0
    for out in (grad_q, grad_k, grad_v):
        size = out.shape[1] // 2
        cut = slice(start, start + size)
        out[:, pl.ds(pl.multiple_of(place.col * size, LANES), size)] = grad_here[:, cut]
        out[:, pl.ds(pl.multiple_of((1 - place.col) * size, LANES), size)] = grad_there[:, cut]
        start += size
    done = [key for each in (sum_out, sum_here, sum_there, small_sum, last_sum) for key in each.keys()]
    t.finish(*done)


def back(levels, qkv, moe_srcs, vmem_ins, grads):
    tokens, middle, q = vmem_ins[0], vmem_ins[2], vmem_ins[12]
    w_out, small_own = vmem_ins[23], vmem_ins[25]
    rows, part = tokens.shape
    width, kv = q.shape[1], qkv[1].shape[1] // 2
    both = width + 2 * kv
    vmem = pl.BlockSpec(memory_space=pltpu.VMEM)
    bf16, f32 = jnp.bfloat16, jnp.float32
    shape = jax.ShapeDtypeStruct
    like = lambda a: shape(a.shape, a.dtype)
    hbm_outs = [like(a) for a in moe_srcs]
    extra_ins, extra_specs, extra_scratch = [], [], []
    if grads:
        extra_ins = list(grads)
        extra_specs = [ANY] * 3 + [vmem]
        hbm_outs += [like(a) for a in (*grads[1:3], grads[0])]
        extra_scratch = [pltpu.VMEM(grads[0].shape, bf16)] * 2
    small_last = shape((8, part), f32)
    vmem_outs = [shape((rows, part), f32)]
    vmem_outs += [shape((part, w.shape[1]), f32) for w in qkv]
    vmem_outs += [shape(w_out.shape, f32), like(small_own), small_last]
    twice = lambda w, dtype=bf16: pltpu.VMEM((2 * rows, w), dtype)
    wide = pltpu.VMEM((rows, part), f32)
    pair = pltpu.VMEM((2, rows, LANES), f32)
    flat = pltpu.VMEM((2, 8, rows), f32)
    scratch = [pltpu.VMEM((part, both), bf16)] * 2
    scratch += [twice(part), twice(part), twice(width), twice(both), twice(both), wide, wide]
    scratch += [wide, pltpu.VMEM((part, both), f32), pltpu.VMEM((part, both), f32)]
    scratch += [pltpu.VMEM((rows, rows), f32), pair, pair, flat, flat]
    scratch += [pltpu.VMEM(small_own.shape, f32)]
    scratch += [pltpu.VMEM((levels + 1, *small_own.shape), f32)]
    scratch += [pltpu.VMEM((levels + 1, 8, part), f32)]
    for high, wide_cols in ((w_out.shape[0], part), (part, both), (part, both)):
        sizes = [pltpu.VMEM((high >> (i + 1), wide_cols), bf16) for i in range(levels)]
        scratch += sizes * 3 + sizes[-1:]
    scratch += extra_scratch
    count = 9 + 4 + 4 + 3 * 2 * levels + 1 + 2 * (levels + 1)
    scratch += [pltpu.SemaphoreType.DMA((2, count)), pltpu.SemaphoreType.DMA((6,))]
    return pl.pallas_call(
        functools.partial(back_kernel, levels, bool(grads)),
        out_shape=hbm_outs + vmem_outs,
        in_specs=[ANY] * (len(qkv) + len(moe_srcs)) + [vmem] * len(vmem_ins) + extra_specs,
        out_specs=[ANY] * len(hbm_outs) + [vmem] * len(vmem_outs),
        scratch_shapes=scratch,
        compiler_params=pltpu.CompilerParams(
            collective_id=4, has_side_effects=True, vmem_limit_bytes=63 * 1024 * 1024
        ),
        name="back",
    )(*qkv, *moe_srcs, *vmem_ins, *extra_ins)


def halve(value, index, mask, axis):
    first, last = jnp.split(value, 2, axis)
    upper = (index & mask) != 0
    send = low(jnp.where(upper, first, last))
    return jnp.where(upper, last, first) + flip(send, "dp", mask).astype(jnp.float32)


def on_device(
    tokens,
    gain_attn,
    w_query,
    key_matrix,
    value_matrix,
    w_out,
    gain_moe,
    w_router,
    w_gate,
    w_up,
    w_down,
    segments,
    routes,
    cotangent,
):
    col = lax.axis_index("col")
    core = lax.axis_index("expert")
    group = lax.axis_index("dp")
    dp_size = lax.axis_size("dp")
    step = dp_size // ZPARTS
    member = group % step
    levels = dp_size.bit_length() - 1
    half_mask = step // 2
    side = (member // half_mask) % 2

    local, part, ffn = w_gate.shape
    split = local // 4
    units = ffn // ZPARTS
    experts = local * lax.axis_size("expert")
    rows = tokens.shape[0]
    width = w_query.shape[1] // 2

    router_own = jnp.pad(w_router, ((0, 0), (0, LANES - experts)))
    seg_rows = jnp.where(core == 0, segments, segments[::-1])
    positions = jax.vmap(doc_positions)(seg_rows).reshape(-1, 1).astype(jnp.float32)
    half = HEAD_WIDTH // 2
    slot = jnp.arange(LANES, dtype=jnp.int32)
    freq = jnp.exp((slot % half).astype(jnp.float32) * (-2.0 * math.log(THETA) / HEAD_WIDTH))
    sign = jnp.where(slot % HEAD_WIDTH < half, -1.0, 1.0)
    cosine, sine = jnp.cos(positions * freq), jnp.sin(positions * freq) * sign
    qkv = [w_query, key_matrix, value_matrix]
    gain, gain_second = gain_attn[None], gain_moe[None]
    (
        down_got,
        down_other,
        gate_got,
        gate_other,
        up_got,
        router_far,
        c_own,
        c_far,
        route_all,
        grad_hidden,
        q,
        keys,
        values,
        mixed,
        mixed_far,
        normed,
        normed_far,
        inv_first,
        middle,
        inv_second,
        h2,
    ) = front(
        tokens,
        cotangent,
        w_down,
        w_gate,
        w_up,
        router_own,
        routes.T,
        qkv,
        gain,
        gain_second,
        w_out,
        cosine,
        sine,
        seg_rows,
        seg_rows.T,
    )
    route_rows = jnp.swapaxes(route_all, 2, 3).reshape(2 * ZPARTS * rows, -1)
    (
        h_own,
        h_far,
        moe_own,
        moe_far,
        hidden,
        slopes,
        dlog,
        _,
        out_far,
        s0_own,
        z1_own,
        x0_far,
        piece2,
        s3_own,
        s3_far,
    ) = moe_layer(
        route_rows,
        grad_hidden,
        [router_own, router_far],
        h2,
        [c_own, c_far],
        [w_gate, w_up, w_down, w_out, gate_got, gate_other, up_got, down_got, down_other],
        up_got,
        width,
    )
    resident = [h_own, h_far, c_own, c_far]
    moe_own, moe_far = (a.reshape(ZPARTS, 2, rows, part) for a in (moe_own, moe_far))
    seconds = tuple((k, 1) for k in range(ZPARTS))
    cargo = [
        ((Z, 2), piece2[None], ((0,),)),
        (X, s3_far[None], ((0,),)),
        (C, moe_own, seconds),
        (C, moe_far, seconds),
    ]
    streamed = split - 1 if half_mask == 1 else 0
    first_outs = weight_grads(0, 0, split, streamed, resident, hidden, slopes, cargo)
    first_part, (z2_piece, x3_far, sib_own, sib_far) = first_outs[:4], first_outs[4:8]
    far_early = first_outs[8:]
    moe_own = low(add_wide(moe_own[:, 0], sib_own))
    moe_far = low(add_wide(moe_far[:, 0], sib_far))
    cargo = [
        ((Z, 3), low(add_wide(s3_own[None], x3_far)), ((0,),)),
        (Y, first_part[3][None], ((0,),)),
        (Y, first_part[2][None], ((0,),)),
        (X, moe_far, ((2,), (3,))),
        ((Z, 1), moe_far, ((1,),)),
    ]
    *second_part, z3_piece, far_late, got_second, moe_x, moe_z1_far = weight_grads(
        1, split, split, 0, resident, hidden, slopes, cargo
    )
    z2_piece, z3_piece, got_second = z2_piece[0], z3_piece[0], got_second[0]
    moe_srcs = [
        moe_own[1],
        low(add_wide(moe_own[2], moe_x[0])),
        low(add_wide(moe_own[3], moe_x[1])),
        low(add_wide(moe_far[0], moe_z1_far[0])),
    ]

    def router_term(h_rows):
        total = dot_tn(dlog, h_rows.reshape(-1, part))
        total = total[:experts] + total[LANES : LANES + experts]
        return jnp.pad(total, ((0, 8), (0, 0)))

    vmem_ins = [
        tokens,
        cotangent,
        middle,
        inv_first,
        inv_second,
        gain,
        gain_second,
        s0_own,
        z1_own,
        z2_piece,
        x0_far,
        z3_piece,
        q,
        keys,
        values,
        mixed,
        mixed_far,
        normed,
        normed_far,
        cosine,
        sine,
        seg_rows,
        seg_rows.T,
        w_out,
        out_far,
        router_term(h_own),
        router_term(h_far),
    ]
    swap = lambda a: flip(a, "dp", half_mask)
    plain = half_mask == 1
    grads = []
    y_far = jnp.concatenate([*far_early, far_late[0]], 0)
    if plain:
        second_far = low(add_wide(second_part[1], y_far))
        grads = [second_part[3], second_part[2], second_far, first_part[1]]
    outs = back(levels, qkv, moe_srcs, vmem_ins, grads)
    moe_parts, outs = outs[:4], outs[4:]
    own_second = add_wide(second_part[0], got_second)
    if plain:
        (got_first, far_second, far_first), outs = outs[:3], outs[3:]
        own_first = add_wide(first_part[0], got_first)
    else:

        def finish_grads(keep_own, keep_far):
            shape = (split, 3, units // 2, part)
            keep_own, keep_far = keep_own.reshape(shape), keep_far.reshape(shape)
            mask = half_mask // 2
            while mask:
                keep_own = halve(keep_own, member, mask, 2)
                keep_far = halve(keep_far, member, mask, 2)
                mask //= 2
            return keep_own, flip(low(keep_far), "col")

        own_second, far_second = finish_grads(own_second, add_wide(second_part[1], y_far))
        own_first, far_first = finish_grads(
            add_wide(first_part[0], swap(second_part[2])),
            add_wide(first_part[1], swap(second_part[3])),
        )
    grad_tokens, grad_query, grad_key, grad_value, grad_out, small, small_last = outs

    def in_order(a, b, index):
        a, b = a.astype(jnp.float32), b.astype(jnp.float32)
        return jnp.concatenate([jnp.where(index == 0, a, b), jnp.where(index == 0, b, a)], 0)

    def assemble(i, turned):
        parts = []
        for p in (own_first, own_second, far_first, far_second):
            p = p.reshape(split, 3, -1, part)[:, i]
            parts.append(jnp.swapaxes(p, 1, 2) if turned else p)
        return in_order(in_order(*parts[:2], side), in_order(*parts[2:], side), col)

    output = middle + RESIDUAL * add_wide(moe_own[0], *moe_parts)
    return (
        output,
        grad_tokens,
        small_last[0],
        grad_query,
        grad_key,
        grad_value,
        grad_out,
        small[SUMMED],
        small[:experts].T,
        assemble(0, True),
        assemble(1, True),
        assemble(2, False),
    )


def solution(mesh):
    in_specs = (
        P(("dp", "expert"), "col"),
        P("col"),
        P("col", "expert"),
        P("col", "expert"),
        P("col", "expert"),
        P("expert", "col"),
        P("col"),
        P("col", None),
        P("expert", "col", None),
        P("expert", "col", None),
        P("expert", None, "col"),
        P("dp", None),
        P(("dp", "expert"), None),
        P(("dp", "expert"), "col"),
    )
    out_specs = (
        P(("dp", "expert"), "col"),
        P(("dp", "expert"), "col"),
        P("col"),
        P("col", "expert"),
        P("col", "expert"),
        P("col", "expert"),
        P("expert", "col"),
        P("col"),
        P("col", None),
        P("expert", "col", "dp"),
        P("expert", "col", "dp"),
        P("expert", "dp", "col"),
    )
    return jax.shard_map(
        on_device, mesh=mesh, in_specs=in_specs, out_specs=out_specs, check_vma=False
    )
```
